32 devices in a mesh: cols: 8 (over z, x), edge: 4 (over y, core).
Axes of the slice: x: 2, y: 2, z: 4, core: 2. Of those that a mesh axis runs over, the one named last changes fastest.
Arguments:
- state: float32 [4, 1024, 512], P('edge', 'cols'), may hold values from -6 to 6
- owners: int32 [4, 1024, 1], P('edge', 'cols'), may hold values from 0 to 7; in each aligned block of 128 rows (0 to 127, 128 to 255, ..., all dimensions but the last counted through in order) at most 32 rows name the same one
- orient: int32 [4, 8, 2], P('edge', 'cols'), may hold values from 0 to 1
- crm_state: bfloat16 [4, 8, 58, 16384], P('edge', 'cols'), may hold values from -6 to 6
- active_levels: int32 [4, 8, 256], P('edge', 'cols'), may hold values from 14 to 58
- vertical_map: float32 [58, 64], replicated, may hold values from -0.75 to 0.75
- diffusion: float32 [57], replicated, may hold values from 0.1 to 4
Outputs:
- new_state: float32 [4, 1024, 512], P('edge', 'cols')
- crm_out: bfloat16 [4, 8, 58, 16384], P('edge', 'cols')
The draws below stay inside these ranges and needn't reach their ends.
Inputs may be any that keep to these rules, and one draw needn't show every extreme that they name: `owners`: within the columns of one tile no group is named more than 32 times.
All inputs are finite; a program needn't handle non-finite values.
Results may differ from the reference program's by a relative error of at most 0.001.
Values sent between devices are 32-bit elements; how exact they have to be, the bound alone decides.
No kernel may reach another device: no remote copies, remote signals or barrier semaphores. Data moves between devices by JAX's collectives and lax.ppermute only.
A program may use at most 64 MiB of HBM per device.

```python
import math
import jax
import jax.numpy as jnp
import numpy as np
from jax import lax

L = 64
CX = 64
CZ = 58
TW = 8
SUBSTEPS = 2
CPD = 128
EH = 16
FL = 512
CAP = 32
SLOTS = 256
STRIPS = 4
NCOLS = 1024
N_COLS = 8


def set_ends(entries, stream_key, low, high):
    longest = entries.shape.index(max(entries.shape))
    spots = []
    for shift in (0, 1):
        where = [jax.random.randint(jax.random.fold_in(stream_key, axis), (), 0, length) for axis, length in enumerate(entries.shape)]
        where[longest] = (where[longest] + shift) % entries.shape[longest]
        spots.append(tuple(where))
    return entries.at[spots[0]].set(low).at[spots[1]].set(high)


def level_of(key, shape, split, least, largest):
    gain, own = 1.0, jax.random.fold_in(key, 6)
    for dim, parts in split:
        draws = jnp.exp(jax.random.uniform(jax.random.fold_in(own, dim), (parts,), jnp.float32, least / len(split), largest / len(split)))
        gain = gain * jnp.repeat(draws, shape[dim] // parts).reshape([-1 if axis == dim else 1 for axis in range(len(shape))])
    return gain


def routed_block(own_key, own, number, rows, number_of, top, reach, lean):
    order = jax.random.permutation(own_key, number_of)
    crowded, usual = load_shares(number_of, rows * top, reach, lean, True), load_shares(number_of, rows * top, reach, lean, False)
    places = jnp.arange(number_of)

    def named(sizes, offset_by):
        used = int((sizes > 0).sum())
        fixed = max(1, used // 4)
        moved = fixed + (places - fixed + offset_by * (used - fixed)) % max(1, number_of - fixed)
        return jnp.zeros((number_of,), jnp.int32).at[order[jnp.where(places < fixed, places, moved)]].set(jnp.asarray(sizes, jnp.int32))

    sizes = jnp.where(number % 4 == 0, named(crowded, number // 4), named(usual, number - number // 4 - 1))
    mixed = jax.random.permutation(jax.random.fold_in(own, 3), number_of)
    source_of, taker = mixed[0:number_of // 2 * 2:2], mixed[1:number_of // 2 * 2:2]
    margin = jnp.minimum(sizes[source_of] - 1, reach - sizes[taker]) // 2
    margin = jnp.where((source_of == order[0]) | (taker == order[0]) | (sizes[taker] == 0), 0, jnp.maximum(margin, 0))
    moved = jax.random.randint(jax.random.fold_in(own, 4), (number_of // 2,), 0, 1 << 20) % (margin + 1)
    sizes = sizes.at[source_of].add(-moved).at[taker].add(moved)
    labels = jnp.searchsorted(jnp.cumsum(sizes), jnp.arange(rows * top), side="right").astype(jnp.int32)
    listing = labels.reshape(top, rows).T
    listing = listing[jax.random.permutation(jax.random.fold_in(own, 1), rows)]
    offset_by = jax.random.randint(jax.random.fold_in(own, 2), (rows, 1), 0, top)
    return jnp.take_along_axis(listing, (jnp.arange(top)[None, :] + offset_by) % top, axis=1)


def load_shares(count, total, limit, slope, full):
    portions = [(1 << 20) // math.isqrt(standing ** slope) + 1 for standing in range(1, count + 1)]
    largest = limit if full else min(limit, max(-(-total // count), total * portions[0] // sum(portions)))
    least = 1 if total - largest >= count - 1 else 0
    given, spare = [largest] + [least] * (count - 1), total - largest - least * (count - 1)
    while spare > 0:
        movable = [i for i in range(1, count) if given[i] < largest] or [i for i in range(1, count) if given[i] < limit]
        pool, remaining = sum([portions[i] for i in movable]), spare
        for i in movable:
            addition = min(limit - given[i], max(1, remaining * portions[i] // pool), spare)
            given[i] = given[i] + addition
            spare = spare - addition
    return np.array(given)


def normal_values(key, dims, width, reach, pieces=(), kind=jnp.bfloat16):
    array = jax.random.normal(key, dims, jnp.float32) * width
    if len(pieces) > 0:
        array = level_of(key, dims, pieces, -0.22, 0.18) * array
    return jnp.clip(array, min=-reach, max=reach).astype(kind)


def setup_inputs(seed: int = 0) -> dict:
    key_of = jax.random.split(jax.random.key(seed), 8)
    state = normal_values(key_of[0], (STRIPS, NCOLS, FL), 1.0, 6.0, ((0, 4), (1, 8)), jnp.float32)
    owners_keys = jax.random.split(jax.random.fold_in(key_of[1], 1), STRIPS * NCOLS // CPD)
    owners_turns = jax.random.permutation(jax.random.fold_in(key_of[1], 3), STRIPS * NCOLS // CPD)
    owners = jax.vmap(lambda own, number: routed_block(jax.random.fold_in(key_of[1], 2), own, number, CPD, N_COLS, 1, CAP, 2))(owners_keys, owners_turns).reshape((STRIPS, NCOLS, 1))
    orient = set_ends(jax.random.randint(key_of[2], (STRIPS, N_COLS, 2), 0, 2), jax.random.fold_in(key_of[2], 1), 0, 1).astype(jnp.int32)
    crm_state = normal_values(key_of[3], (STRIPS, N_COLS, CZ, CX * SLOTS), 1.0, 6.0, ((0, 4), (1, 8)))
    active_levels = set_ends(jax.random.randint(key_of[4], (STRIPS, N_COLS, SLOTS), CZ // 4, CZ + 1), jax.random.fold_in(key_of[4], 1), CZ // 4, CZ).astype(jnp.int32)
    vertical_map = normal_values(key_of[5], (CZ, L), L ** -0.5, 0.75, (), jnp.float32)
    diffusion = jnp.clip(jnp.exp(jax.random.uniform(key_of[6], (CZ - 1,), jnp.float32, math.log(0.1), math.log(4.0))), 0.1, 4.0)
    return dict(state=state, owners=owners, orient=orient, crm_state=crm_state, active_levels=active_levels, vertical_map=vertical_map, diffusion=diffusion)


kappa_edge = 0.25
max_courant = 0.9
relax_rate = 0.5


def factorize(lower, diagonal, upper):
    depth = diagonal.shape[0]
    prev_c = jnp.zeros(diagonal.shape[1:], jnp.float32)
    factors = []
    denoms = []
    for level in range(depth):
        denom = diagonal[level] + lower[level] * prev_c
        prev_c = -upper[level] / denom
        factors.append(prev_c)
        denoms.append(denom)
    return factors, denoms


def tridiag(lower, factors, denoms, values):
    depth = values.shape[0]
    prev_d = jnp.zeros(values.shape[1:], jnp.float32)
    offsets = []
    for level in range(depth):
        prev_d = (values[level] + lower[level][None, :] * prev_d) / denoms[level][None, :]
        offsets.append(prev_d)
    after = jnp.zeros(values.shape[1:], jnp.float32)
    solved = [None] * depth
    for level in range(depth - 1, -1, -1):
        after = offsets[level] - factors[level][None, :] * after
        solved[level] = after
    return jnp.stack(solved, axis=0)


def physics(columns, crm_slab, active_count, vertical_map, diffusion):
    slots = columns.shape[0]
    temper = columns[:, 0:L]
    moisture = columns[:, L:2 * L]
    forcing = jnp.einsum("zl,sl->zs", vertical_map, temper, precision=lax.Precision.HIGHEST, preferred_element_type=jnp.float32)
    courant = max_courant * jax.nn.sigmoid(jnp.einsum("zl,sl->zs", vertical_map, moisture, precision=lax.Precision.HIGHEST, preferred_element_type=jnp.float32))
    field = crm_slab.reshape(CZ, CX, slots).astype(jnp.float32)
    mean_before = jnp.mean(field, axis=1)
    spread_before = jnp.mean(field * field, axis=1) - mean_before * mean_before
    field = field + relax_rate * (forcing - mean_before)[:, None, :]
    heights = jnp.arange(CZ - 1, dtype=jnp.int32)
    coupled = (heights[:, None] + 1 < active_count[None, :]).astype(jnp.float32)
    interfaces = diffusion[:, None] * coupled
    zero_row = jnp.zeros((1, slots), jnp.float32)
    lower = jnp.concatenate([zero_row, interfaces], axis=0)
    upper = jnp.concatenate([interfaces, zero_row], axis=0)
    diagonal = 1.0 + lower + upper
    factors, denoms = factorize(lower, diagonal, upper)
    for substep in range(SUBSTEPS):
        field = field - courant[:, None, :] * (field - jnp.roll(field, 1, axis=1))
        field = tridiag(lower, factors, denoms, field)
    mean_after = jnp.mean(field, axis=1)
    spread_after = jnp.mean(field * field, axis=1) - mean_after * mean_after
    tend_mean = jnp.einsum("zs,zl->sl", mean_after - mean_before, vertical_map, precision=lax.Precision.HIGHEST, preferred_element_type=jnp.float32)
    tend_spread = jnp.einsum("zs,zl->sl", spread_after - spread_before, vertical_map, precision=lax.Precision.HIGHEST, preferred_element_type=jnp.float32)
    tend = jnp.concatenate([tend_mean, tend_spread], axis=1)
    return tend, field.reshape(CZ, CX * slots).astype(jnp.bfloat16)


def fill_slots(index, rows):
    return jnp.zeros((N_COLS * SLOTS, 2 * L), jnp.float32).at[index].set(rows)


def pick_rows(table, index):
    return table[index]


def reference(state, owners, orient, crm_state, active_levels, vertical_map, diffusion):
    tiles = state.reshape(STRIPS, N_COLS, EH, TW, FL)
    upper_row = tiles[:, :, EH - 1]
    lower_row = tiles[:, :, 0]
    ghost_low = jnp.roll(upper_row, 1, axis=0)
    ghost_high = jnp.roll(lower_row, -1, axis=0)
    flip_low = (orient[:, :, 0] == 1)[:, :, None, None]
    flip_high = (orient[:, :, 1] == 1)[:, :, None, None]
    ghost_low = jnp.where(flip_low, ghost_low[:, :, ::-1], ghost_low)
    ghost_high = jnp.where(flip_high, ghost_high[:, :, ::-1], ghost_high)
    padded = jnp.concatenate([ghost_low[:, :, None], tiles, ghost_high[:, :, None]], axis=2)
    moved = tiles + kappa_edge * ((padded[:, :, 2:] + padded[:, :, :-2]) - 2.0 * tiles)
    moved = moved.reshape(STRIPS, N_COLS, CPD, FL)
    group_of = owners.reshape(STRIPS, N_COLS, CPD)
    same = group_of[..., :, None] == group_of[..., None, :]
    order = jnp.arange(CPD, dtype=jnp.int32)
    earlier = order[None, :] < order[:, None]
    ranking = jnp.sum((same & earlier).astype(jnp.int32), axis=-1).astype(jnp.int32)
    source = jnp.arange(N_COLS, dtype=jnp.int32)[None, :, None]
    flat_index = (group_of * SLOTS + source * CAP + ranking).astype(jnp.int32)
    used = moved[..., 0:2 * L]
    buffers = jax.vmap(fill_slots)(flat_index.reshape(STRIPS, N_COLS * CPD), used.reshape(STRIPS, N_COLS * CPD, 2 * L))

    def run(items):
        columns, slab, counts = items
        return physics(columns, slab, counts, vertical_map, diffusion)

    tends, crm_new = lax.map(run, (buffers.reshape(STRIPS * N_COLS, SLOTS, 2 * L), crm_state.reshape(STRIPS * N_COLS, CZ, CX * SLOTS), active_levels.reshape(STRIPS * N_COLS, SLOTS)))
    picked = jax.vmap(pick_rows)(tends.reshape(STRIPS, N_COLS * SLOTS, 2 * L), flat_index.reshape(STRIPS, N_COLS * CPD))
    moved = moved.reshape(STRIPS, N_COLS * CPD, FL)
    new_state = jnp.concatenate([moved[..., 0:2 * L] + picked, moved[..., 2 * L:]], axis=2)
    return new_state, crm_new.reshape(STRIPS, N_COLS, CZ, CX * SLOTS)
```

```python
import functools

import jax
import jax.numpy as jnp
from jax import lax
from jax.experimental import pallas as pl
from jax.experimental.pallas import tpu as pltpu
from jax.sharding import PartitionSpec as P

L = 64
CX = 64
CZ = 58
TW = 8
SUBSTEPS = 2
ZP = 64
LANES = 128
SUB = 8
NI = CX // SUB
TZ = 16

kappa_edge = 0.25
max_courant = 0.9
relax_rate = 0.5

HI = lax.Precision.HIGHEST


def call(body, outs, args, scratch=(), in_specs=None, cost=None, limit=32 << 20, aliases=None):
    kw = {}
    if in_specs is not None:
        kw["in_specs"] = in_specs
    return pl.pallas_call(
        body,
        out_shape=outs,
        scratch_shapes=list(scratch),
        compiler_params=pltpu.CompilerParams(vmem_limit_bytes=limit),
        cost_estimate=cost,
        input_output_aliases=aliases or {},
        **kw,
    )(*args)


def dot(a, b, dims):
    return lax.dot_general(a, b, (dims, ((), ())), precision=HI, preferred_element_type=jnp.float32)


def from_behind(value, axis, steps):
    count = lax.axis_size(axis)
    pairs = [(source, (source + steps) % count) for source in range(count)]
    return lax.ppermute(value, axis, pairs)


def slots_kernel(cap, owners_ref, put_ref, take_ref):
    per_tile = owners_ref.shape[0]
    n_slots = put_ref.shape[0]
    down = jnp.broadcast_to(owners_ref[...], (per_tile, per_tile))
    across = down.T
    row = lax.broadcasted_iota(jnp.int32, (per_tile, per_tile), 0)
    col = lax.broadcasted_iota(jnp.int32, (per_tile, per_tile), 1)
    same = down == across
    before_col = jnp.where(same & (row < col), 1.0, 0.0)
    before_row = jnp.where(same & (col < row), 1.0, 0.0)
    rank_across = jnp.sum(before_col, axis=0, keepdims=True).astype(jnp.int32)
    rank_down = jnp.sum(before_row, axis=1, keepdims=True).astype(jnp.int32)
    slot_across = across[0:1, :] * cap + rank_across
    slot_down = owners_ref[...] * cap + rank_down
    q_down = lax.broadcasted_iota(jnp.int32, (n_slots, per_tile), 0)
    q_across = lax.broadcasted_iota(jnp.int32, (per_tile, n_slots), 1)
    put_ref[...] = jnp.where(q_down == slot_across, 1.0, 0.0)
    take_ref[...] = jnp.where(q_across == slot_down, 1.0, 0.0)


def edge_kernel(state_ref, low_ref, high_ref, flag_ref, put_ref, moved_ref, out_ref):
    per_tile = state_ref.shape[0]

    def turned(ref, flag):
        value = ref[...]
        back = jnp.concatenate([value[TW - 1 - w : TW - w] for w in range(TW)], axis=0)
        return jnp.where(flag == 1, back, value)

    low = turned(low_ref, flag_ref[0, 0])
    high = turned(high_ref, flag_ref[0, 1])
    tiles = state_ref[...]
    below = jnp.concatenate([low, tiles[: per_tile - TW]], axis=0)
    above = jnp.concatenate([tiles[TW:], high], axis=0)
    moved = tiles + kappa_edge * ((above + below) - 2.0 * tiles)
    moved_ref[...] = moved
    out_ref[...] = dot(put_ref[...], moved[:, : 2 * L], ((1,), (0,)))


def prepare_kernel(crm_ref, active_ref, diff_ref, vm_ref, f_ref, mean_ref, sq_ref, coef_ref, w_ref):
    slots = active_ref.shape[1]
    halves = slots // LANES
    zero = jnp.zeros((TZ, LANES), jnp.float32)
    n_t = ZP // TZ

    def column(x, sums):
        sums = list(sums)
        place = (x % NI) * SUB + x // NI
        for h in range(halves):
            lane = pl.multiple_of(x * slots + h * LANES, LANES)
            for t in range(n_t):
                rows = min(TZ, CZ - t * TZ)
                v = crm_ref[t * TZ : t * TZ + rows, pl.ds(lane, LANES)].astype(jnp.float32)
                first = (t * TZ * halves + h) * CX + place
                f_ref[pl.ds(first, rows, stride=halves * CX), :] = v
                k = (h * n_t + t) * 2
                if rows < TZ:
                    v = jnp.concatenate([v, jnp.zeros((TZ - rows, LANES), jnp.float32)], axis=0)
                sums[k] = sums[k] + v
                sums[k + 1] = sums[k + 1] + v * v
        return tuple(sums)

    sums = lax.fori_loop(0, CX, column, (zero,) * (halves * n_t * 2))
    for h in range(halves):
        for t in range(n_t):
            k = (h * n_t + t) * 2
            here = (slice(t * TZ, (t + 1) * TZ), slice(h * LANES, (h + 1) * LANES))
            mean_ref[here] = sums[k] * (1.0 / CX)
            sq_ref[here] = sums[k + 1] * (1.0 / CX)

    coef_ref[...] = jnp.zeros_like(coef_ref)
    active = active_ref[...]
    nothing = jnp.zeros((1, slots), jnp.float32)

    def link(i):
        if i < 0 or i >= CZ - 1:
            return nothing
        return jnp.where(i + 1 < active, diff_ref[i], 0.0)

    inv = nothing
    for z in range(CZ):
        lower, upper = link(z - 1), link(z)
        scaled = lower * inv
        inv = 1.0 / (1.0 + lower + upper - lower * scaled)
        coef_ref[0, z : z + 1, :] = inv
        coef_ref[1, z : z + 1, :] = lower * inv
        coef_ref[2, z : z + 1, :] = upper * inv
    inv = nothing
    for z in range(CZ - 1, -1, -1):
        lower, upper = link(z - 1), link(z)
        scaled = upper * inv
        inv = 1.0 / (1.0 + lower + upper - upper * scaled)
        coef_ref[3, z : z + 1, :] = inv
        coef_ref[4, z : z + 1, :] = upper * inv
        coef_ref[5, z : z + 1, :] = lower * inv

    w_ref[...] = jnp.zeros_like(w_ref)
    pad = jnp.zeros((CZ, L), jnp.float32)
    w_ref[0:CZ, :] = jnp.concatenate([vm_ref[...], pad], axis=1)
    w_ref[ZP : ZP + CZ, :] = jnp.concatenate([pad, vm_ref[...]], axis=1)


def physics_kernel(cols_ref, f_ref, mean_ref, sq_ref, coef_ref, w_ref, tend_ref, y_ref, adv_ref, acc_ref):
    slots = cols_ref.shape[0]
    halves = slots // LANES
    w = w_ref[...]
    mapped = dot(w, cols_ref[...], ((1,), (1,)))
    forcing = mapped[0:ZP]
    courant = max_courant * jax.nn.sigmoid(mapped[ZP:])
    inv1 = coef_ref[0]
    inv2 = coef_ref[3]
    adv_ref[0] = inv1 * (1.0 - courant)
    adv_ref[1] = inv1 * courant
    adv_ref[2] = inv2 * (1.0 - courant)
    adv_ref[3] = inv2 * courant
    adv_ref[4] = inv1 * (relax_rate * (forcing - mean_ref[...]))

    def spread(ref, k, z, lane):
        return jnp.broadcast_to(ref[k, z : z + 1, lane], (SUB, LANES))

    dev = []
    for h in range(halves):
        lane = slice(h * LANES, (h + 1) * LANES)

        def at(z, i):
            base = (z * halves + h) * CX + i * SUB
            return slice(base, base + SUB)

        zero = jnp.zeros((SUB, LANES), jnp.float32)
        prev = [zero] * NI
        for z in range(CZ):
            a, b = spread(adv_ref, 0, z, lane), spread(adv_ref, 1, z, lane)
            d, e = spread(adv_ref, 4, z, lane), spread(coef_ref, 1, z, lane)
            f = [f_ref[at(z, i), :] for i in range(NI)]
            behind = [pltpu.roll(f[NI - 1], 1, axis=0)] + f[: NI - 1]
            prev = [(a * f[i] + b * behind[i]) + (d + e * prev[i]) for i in range(NI)]
            for i in range(NI):
                y_ref[at(z, i), :] = prev[i]
        after = [zero] * NI
        prev = [zero] * NI
        for z in range(CZ - 1, -1, -1):
            g = spread(coef_ref, 2, z, lane)
            a, b = spread(adv_ref, 2, z, lane), spread(adv_ref, 3, z, lane)
            e = spread(coef_ref, 4, z, lane)
            after = [y_ref[at(z, i), :] + g * after[i] for i in range(NI)]
            behind = [pltpu.roll(after[NI - 1], 1, axis=0)] + after[: NI - 1]
            prev = [(a * after[i] + b * behind[i]) + e * prev[i] for i in range(NI)]
            for i in range(NI):
                y_ref[at(z, i), :] = prev[i]
        after = [zero] * NI
        for z in range(CZ):
            g = spread(coef_ref, 5, z, lane)
            after = [y_ref[at(z, i), :] + g * after[i] for i in range(NI)]
            total, square = after[0], after[0] * after[0]
            for i in range(NI):
                y_ref[at(z, i), :] = after[i]
                if i > 0:
                    total = total + after[i]
                    square = square + after[i] * after[i]
            acc_ref[0, z * SUB : (z + 1) * SUB, :] = total
            acc_ref[1, z * SUB : (z + 1) * SUB, :] = square
        acc_ref[:, CZ * SUB :, :] = jnp.zeros((2, (ZP - CZ) * SUB, LANES), jnp.float32)
        sums = []
        for k in range(2):
            part = acc_ref[k, pl.ds(0, ZP, stride=SUB), :]
            for s in range(1, SUB):
                part = part + acc_ref[k, pl.ds(s, ZP, stride=SUB), :]
            sums.append(part * (1.0 / CX))
        mean0, sq0 = mean_ref[:, lane], sq_ref[:, lane]
        mean1, sq1 = sums
        dev.append(jnp.concatenate([mean1 - mean0, (sq1 - mean1 * mean1) - (sq0 - mean0 * mean0)], axis=0))
    x = jnp.concatenate(dev, axis=1)
    tend_ref[...] = dot(x, w, ((0,), (0,)))


def store_kernel(y_ref, crm_ref):
    slots = crm_ref.shape[1] // CX
    halves = slots // LANES

    def column(x, carry):
        place = (x % NI) * SUB + x // NI
        for h in range(halves):
            lane = pl.multiple_of(x * slots + h * LANES, LANES)
            for t in range(ZP // TZ):
                rows = min(TZ, CZ - t * TZ)
                first = (t * TZ * halves + h) * CX + place
                v = y_ref[pl.ds(first, rows, stride=halves * CX), :]
                crm_ref[t * TZ : t * TZ + rows, pl.ds(lane, LANES)] = v.astype(jnp.bfloat16)
        return carry

    lax.fori_loop(0, CX, column, 0)


def finish_kernel(moved_ref, take_ref, back_ref, out_ref):
    out_ref[:, 2 * L :] = moved_ref[:, 2 * L :]
    out_ref[:, : 2 * L] = moved_ref[:, : 2 * L] + dot(take_ref[...], back_ref[...], ((1,), (0,)))


def cost(us):
    return pl.CostEstimate(flops=0, bytes_accessed=int(us * 3.0e6), transcendentals=0)


def shards(state, owners, orient, crm_state, active_levels, vertical_map, diffusion):
    f32 = jnp.float32
    n_tiles = lax.axis_size("cols")
    per_tile = state.shape[1]
    width = state.shape[2]
    cap_slots = max(2, 2 * per_tile // n_tiles)
    slots = n_tiles * cap_slots
    rows_f = CZ * CX * slots // LANES
    tile = state[0]
    low = from_behind(tile[per_tile - TW :], "edge", 1)
    high = from_behind(tile[:TW], "edge", -1)
    put, take = call(
        functools.partial(slots_kernel, cap_slots),
        (jax.ShapeDtypeStruct((slots, per_tile), f32), jax.ShapeDtypeStruct((per_tile, slots), f32)),
        (owners[0],),
        cost=cost(0.6),
    )
    vmem = pl.BlockSpec(memory_space=pltpu.VMEM)
    smem = pl.BlockSpec(memory_space=pltpu.SMEM)
    moved, outgoing = call(
        edge_kernel,
        (jax.ShapeDtypeStruct((per_tile, width), f32), jax.ShapeDtypeStruct((slots, 2 * L), f32)),
        (tile, low, high, orient[0], put),
        in_specs=[vmem, vmem, vmem, smem, vmem],
        cost=cost(1),
    )
    received = lax.all_to_all(
        outgoing.reshape(n_tiles, cap_slots, 2 * L), "cols", split_axis=0, concat_axis=0, tiled=True
    ).reshape(slots, 2 * L)
    prepared = call(
        prepare_kernel,
        (
            pltpu.VMEM((rows_f, LANES), f32),
            pltpu.VMEM((ZP, slots), f32),
            pltpu.VMEM((ZP, slots), f32),
            pltpu.VMEM((6, ZP, slots), f32),
            pltpu.VMEM((2 * ZP, 2 * L), f32),
        ),
        (crm_state[0, 0], active_levels[0], diffusion, vertical_map),
        in_specs=[vmem, vmem, smem, vmem],
        cost=cost(4),
    )
    tend, after = call(
        physics_kernel,
        (jax.ShapeDtypeStruct((slots, 2 * L), f32), pltpu.VMEM((rows_f, LANES), f32)),
        (received, *prepared),
        scratch=(pltpu.VMEM((5, ZP, slots), f32), pltpu.VMEM((2, ZP * SUB, LANES), f32)),
        cost=cost(5),
    )
    returned = lax.all_to_all(
        tend.reshape(n_tiles, cap_slots, 2 * L), "cols", split_axis=0, concat_axis=0, tiled=True
    ).reshape(slots, 2 * L)
    crm_new = call(
        store_kernel,
        jax.ShapeDtypeStruct((CZ, CX * slots), jnp.bfloat16),
        (after,),
        cost=cost(3),
    )
    new_state = call(
        finish_kernel,
        jax.ShapeDtypeStruct((per_tile, width), f32),
        (moved, take, returned),
        cost=cost(0.7),
    )
    return (new_state[None], crm_new[None, None])


def solution(mesh):
    in_specs = (
        P("edge", "cols", None),
        P("edge", "cols", None),
        P("edge", "cols", None),
        P("edge", "cols", None, None),
        P("edge", "cols", None),
        P(),
        P(),
    )
    out_specs = (P("edge", "cols", None), P("edge", "cols", None, None))
    return jax.shard_map(shards, mesh=mesh, in_specs=in_specs, out_specs=out_specs, check_vma=False)
```

```python
import functools

import jax
import jax.numpy as jnp
from jax import lax
from jax.experimental import pallas as pl
from jax.experimental.pallas import tpu as pltpu
from jax.sharding import PartitionSpec as P

L = 64
CX = 64
CZ = 58
TW = 8
SUBSTEPS = 2
ZP = 64
LANES = 128
SUB = 8
NI = CX // SUB
TZ = 16

kappa_edge = 0.25
max_courant = 0.9
relax_rate = 0.5

HI = lax.Precision.HIGHEST


def call(body, outs, args, scratch=(), in_specs=None, out_specs=None, cost=None, limit=32 << 20, aliases=None):
    kw = {}
    if out_specs is not None:
        kw["out_specs"] = out_specs
    if in_specs is not None:
        kw["in_specs"] = in_specs
    return pl.pallas_call(
        body,
        out_shape=outs,
        scratch_shapes=list(scratch),
        compiler_params=pltpu.CompilerParams(vmem_limit_bytes=limit),
        cost_estimate=cost,
        input_output_aliases=aliases or {},
        **kw,
    )(*args)


def dot(a, b, dims):
    return lax.dot_general(a, b, (dims, ((), ())), precision=HI, preferred_element_type=jnp.float32)


def from_behind(value, axis, steps):
    count = lax.axis_size(axis)
    pairs = [(source, (source + steps) % count) for source in range(count)]
    return lax.ppermute(value, axis, pairs)


def split_dot(chosen, value):
    high = value.astype(jnp.bfloat16)
    low = (value - high.astype(jnp.float32)).astype(jnp.bfloat16)
    pick = lambda part: lax.dot_general(chosen, part, (((1,), (0,)), ((), ())), preferred_element_type=jnp.float32)
    return pick(high) + pick(low)


def slots_kernel(cap, state_hbm, owners_hbm, orient_hbm, tile_ref, put_ref, take_ref, flip_ref, own_ref, turn_ref, sems):
    per_tile = owners_hbm.shape[1]
    n_slots = put_ref.shape[0]
    copies = [
        pltpu.make_async_copy(owners_hbm, own_ref, sems.at[0]),
        pltpu.make_async_copy(orient_hbm, turn_ref, sems.at[1]),
        pltpu.make_async_copy(state_hbm, tile_ref, sems.at[2]),
    ]
    for copy in copies:
        copy.start()
    row = lax.broadcasted_iota(jnp.int32, (per_tile, per_tile), 0)
    col = lax.broadcasted_iota(jnp.int32, (per_tile, per_tile), 1)
    q_down = lax.broadcasted_iota(jnp.int32, (n_slots, per_tile), 0)
    q_across = lax.broadcasted_iota(jnp.int32, (per_tile, n_slots), 1)
    copies[0].wait()
    across = jnp.broadcast_to(own_ref[...], (per_tile, per_tile))
    down = across.T
    same = down == across
    before_col = jnp.where(same & (row < col), 1.0, 0.0)
    before_row = jnp.where(same & (col < row), 1.0, 0.0)
    rank_across = jnp.sum(before_col, axis=0, keepdims=True).astype(jnp.int32)
    rank_down = jnp.sum(before_row, axis=1, keepdims=True).astype(jnp.int32)
    slot_across = across[0:1, :] * cap + rank_across
    slot_down = down[:, 0:1] * cap + rank_down
    put_ref[...] = jnp.where(q_down == slot_across, 1.0, 0.0).astype(jnp.bfloat16)
    take_ref[...] = jnp.where(q_across == slot_down, 1.0, 0.0).astype(jnp.bfloat16)
    copies[1].wait()
    for k in range(2):
        flip_ref[k] = jnp.broadcast_to(turn_ref[0:1, k : k + 1], (TW, LANES))
    copies[2].wait()


def edge_kernel(tile_ref, low_ref, high_ref, flip_ref, put_ref, moved_ref, out_ref):
    per_tile, width = tile_ref.shape

    def turned(ref, k):
        value = ref[...]
        back = jnp.concatenate([value[TW - 1 - w : TW - w] for w in range(TW)], axis=0)
        flip = jnp.concatenate([flip_ref[k]] * (width // LANES), axis=1)
        return jnp.where(flip == 1, back, value)

    low = turned(low_ref, 0)
    high = turned(high_ref, 1)
    tiles = tile_ref[...]
    below = jnp.concatenate([low, tiles[: per_tile - TW]], axis=0)
    above = jnp.concatenate([tiles[TW:], high], axis=0)
    moved = tiles + kappa_edge * ((above + below) - 2.0 * tiles)
    out_ref[...] = split_dot(put_ref[...], moved[:, : 2 * L])
    moved_ref[...] = moved


def rows_from_levels(flipped):
    n = 2 * SUB * TZ
    a = lax.broadcasted_iota(jnp.int32, (n, n), 1 if flipped else 0)
    b = lax.broadcasted_iota(jnp.int32, (n, n), 0 if flipped else 1)
    z, p, s = a >> 4, (a >> 3) & 1, a & 7
    return jnp.where(b == p * (SUB * TZ) + s * TZ + z, 1.0, 0.0).astype(jnp.bfloat16)


def prepare_kernel(
    crm_hbm, active_hbm, diff_hbm, vm_hbm, f_ref, mean_ref, sq_ref, coef_ref, w_ref, crm_ref, act_ref, diff_ref, vm_ref, sems
):
    slots = active_hbm.shape[1]
    copies = [
        pltpu.make_async_copy(active_hbm, act_ref, sems.at[0]),
        pltpu.make_async_copy(diff_hbm, diff_ref, sems.at[1]),
        pltpu.make_async_copy(vm_hbm, vm_ref, sems.at[2]),
        pltpu.make_async_copy(crm_hbm, crm_ref, sems.at[3]),
    ]
    for copy in copies:
        copy.start()
    order = rows_from_levels(False)
    coef_ref[...] = jnp.zeros_like(coef_ref)
    w_ref[...] = jnp.zeros_like(w_ref)
    copies[0].wait()
    copies[1].wait()
    active = act_ref[...]
    nothing = jnp.zeros((1, slots), jnp.float32)

    def link(i):
        if i < 0 or i >= CZ - 1:
            return nothing
        return jnp.where(i + 1 < active, diff_ref[i], 0.0)

    up, down = nothing, nothing
    for z in range(CZ):
        lower, upper = link(z - 1), link(z)
        up = 1.0 / (1.0 + lower + upper - lower * (lower * up))
        coef_ref[0, z : z + 1, :] = up
        coef_ref[1, z : z + 1, :] = lower * up
        coef_ref[2, z : z + 1, :] = upper * up
        y = CZ - 1 - z
        lower, upper = link(y - 1), link(y)
        down = 1.0 / (1.0 + lower + upper - upper * (upper * down))
        coef_ref[3, y : y + 1, :] = down
        coef_ref[4, y : y + 1, :] = upper * down
        coef_ref[5, y : y + 1, :] = lower * down
    copies[2].wait()
    pad = jnp.zeros((CZ, L), jnp.float32)
    w_ref[0:CZ, :] = jnp.concatenate([vm_ref[...], pad], axis=1)
    w_ref[ZP : ZP + CZ, :] = jnp.concatenate([pad, vm_ref[...]], axis=1)

    copies[3].wait()
    for t in range(ZP // TZ):
        rows = min(TZ, CZ - t * TZ)
        total = jnp.zeros((TZ, slots), jnp.float32)
        square = jnp.zeros((TZ, slots), jnp.float32)
        for p in range(NI // 2):
            parts = []
            for i in (2 * p, 2 * p + 1):
                for s in range(SUB):
                    x = s * NI + i
                    v = crm_ref[t * TZ : t * TZ + rows, x * slots : (x + 1) * slots]
                    wide = v.astype(jnp.float32)
                    if rows < TZ:
                        wide = jnp.concatenate([wide, jnp.zeros((TZ - rows, slots), jnp.float32)], axis=0)
                        v = wide.astype(jnp.bfloat16)
                    total = total + wide
                    square = square + wide * wide
                    parts.append(v)
            turned = lax.dot_general(
                order, jnp.concatenate(parts, axis=0), (((1,), (0,)), ((), ())), preferred_element_type=jnp.float32
            ).astype(jnp.bfloat16)
            for z in range(rows):
                base = (t * TZ + z) * CX + p * 2 * SUB
                f_ref[base : base + 2 * SUB, :] = turned[z * 2 * SUB : (z + 1) * 2 * SUB]
        mean_ref[t * TZ : (t + 1) * TZ, :] = total * (1.0 / CX)
        sq_ref[t * TZ : (t + 1) * TZ, :] = square * (1.0 / CX)


def physics_kernel(cols_ref, f_ref, mean_ref, sq_ref, coef_ref, w_ref, tend_ref, y_ref, g_ref, adv_ref, acc_ref):
    slots = cols_ref.shape[0]
    halves = slots // LANES
    w = w_ref[...]
    mapped = dot(w, cols_ref[...], ((1,), (1,)))
    forcing = mapped[0:ZP]
    courant = max_courant * jax.nn.sigmoid(mapped[ZP:])
    inv1 = coef_ref[0]
    inv2 = coef_ref[3]
    adv_ref[0] = inv1 * (1.0 - courant)
    adv_ref[1] = inv1 * courant
    adv_ref[2] = inv2 * (1.0 - courant)
    adv_ref[3] = inv2 * courant
    adv_ref[4] = inv1 * (relax_rate * (forcing - mean_ref[...]))

    def spread(ref, k, z, lane):
        return jnp.broadcast_to(ref[k, z : z + 1, lane], (SUB, LANES))

    dev = []
    for h in range(halves):
        lane = slice(h * LANES, (h + 1) * LANES)

        def at(z, i, n=1):
            base = z * CX + i * SUB
            return slice(base, base + n * SUB)

        zero = jnp.zeros((SUB, LANES), jnp.float32)
        prev = [zero] * NI
        for z in range(CZ):
            a, b = spread(adv_ref, 0, z, lane), spread(adv_ref, 1, z, lane)
            d, e = spread(adv_ref, 4, z, lane), spread(coef_ref, 1, z, lane)
            f = []
            for i in range(0, NI, 2):
                pair = f_ref[at(z, i, 2), lane].astype(jnp.float32)
                f += [pair[:SUB], pair[SUB:]]
            behind = [pltpu.roll(f[NI - 1], 1, axis=0)] + f[: NI - 1]
            prev = [(a * f[i] + b * behind[i]) + (d + e * prev[i]) for i in range(NI)]
            for i in range(NI):
                g_ref[at(z, i), lane] = prev[i]
        after = [zero] * NI
        prev = [zero] * NI
        for z in range(CZ - 1, -1, -1):
            g = spread(coef_ref, 2, z, lane)
            a, b = spread(adv_ref, 2, z, lane), spread(adv_ref, 3, z, lane)
            e = spread(coef_ref, 4, z, lane)
            after = [g_ref[at(z, i), lane] + g * after[i] for i in range(NI)]
            behind = [pltpu.roll(after[NI - 1], 1, axis=0)] + after[: NI - 1]
            prev = [(a * after[i] + b * behind[i]) + e * prev[i] for i in range(NI)]
            for i in range(NI):
                g_ref[at(z, i), lane] = prev[i]
        after = [zero] * NI
        for z in range(CZ):
            g = spread(coef_ref, 5, z, lane)
            after = [g_ref[at(z, i), lane] + g * after[i] for i in range(NI)]
            total, square = after[0], after[0] * after[0]
            for i in range(1, NI):
                total = total + after[i]
                square = square + after[i] * after[i]
            for i in range(0, NI, 2):
                y_ref[at(z, i, 2), lane] = jnp.concatenate(after[i : i + 2], axis=0).astype(jnp.bfloat16)
            acc_ref[0, z * SUB : (z + 1) * SUB, :] = total
            acc_ref[1, z * SUB : (z + 1) * SUB, :] = square
        acc_ref[:, CZ * SUB :, :] = jnp.zeros((2, (ZP - CZ) * SUB, LANES), jnp.float32)
        sums = []
        for k in range(2):
            part = acc_ref[k, pl.ds(0, ZP, stride=SUB), :]
            for s in range(1, SUB):
                part = part + acc_ref[k, pl.ds(s, ZP, stride=SUB), :]
            sums.append(part * (1.0 / CX))
        mean0, sq0 = mean_ref[:, lane], sq_ref[:, lane]
        mean1, sq1 = sums
        dev.append(jnp.concatenate([mean1 - mean0, (sq1 - mean1 * mean1) - (sq0 - mean0 * mean0)], axis=0))
    x = jnp.concatenate(dev, axis=1)
    tend_ref[...] = dot(x, w, ((0,), (0,)))


def store_kernel(y_ref, crm_hbm, crm_ref, sems):
    slots = crm_hbm.shape[1] // CX
    order = rows_from_levels(True)
    copies = []
    for p in range(NI // 2):
        for t in range(ZP // TZ):
            rows = min(TZ, CZ - t * TZ)
            parts = [y_ref[(t * TZ + z) * CX + p * 2 * SUB : (t * TZ + z) * CX + (p + 1) * 2 * SUB, :] for z in range(rows)]
            if rows < TZ:
                parts.append(jnp.zeros(((TZ - rows) * 2 * SUB, slots), jnp.bfloat16))
            turned = lax.dot_general(
                order, jnp.concatenate(parts, axis=0), (((1,), (0,)), ((), ())), preferred_element_type=jnp.float32
            ).astype(jnp.bfloat16)
            for i in range(2):
                for s in range(SUB):
                    x = s * NI + 2 * p + i
                    k = (i * SUB + s) * TZ
                    crm_ref[t * TZ : t * TZ + rows, x * slots : (x + 1) * slots] = turned[k : k + rows]
        for s in range(SUB):
            here = pl.ds((s * NI + 2 * p) * slots, 2 * slots)
            copy = pltpu.make_async_copy(crm_ref.at[:, here], crm_hbm.at[:, here], sems.at[p * SUB + s])
            copy.start()
            copies.append(copy)
    for copy in copies:
        copy.wait()


def finish_kernel(moved_ref, take_ref, back_ref, out_ref):
    out_ref[:, 2 * L :] = moved_ref[:, 2 * L :]
    out_ref[:, : 2 * L] = moved_ref[:, : 2 * L] + split_dot(take_ref[...], back_ref[...])


def cost(us):
    return pl.CostEstimate(flops=0, bytes_accessed=int(us * 3.0e6), transcendentals=0)


def far(x):
    return pltpu.with_memory_space_constraint(x, pltpu.HBM)


def shards(state, owners, orient, crm_state, active_levels, vertical_map, diffusion):
    f32, bf16 = jnp.float32, jnp.bfloat16
    n_tiles = lax.axis_size("cols")
    per_tile = state.shape[1]
    width = state.shape[2]
    cap_slots = max(2, 2 * per_tile // n_tiles)
    slots = n_tiles * cap_slots
    rows_f = CZ * CX
    hbm = pl.BlockSpec(memory_space=pltpu.HBM)
    dma = pltpu.SemaphoreType.DMA
    tile = state[0]
    low = from_behind(tile[per_tile - TW :], "edge", 1)
    high = from_behind(tile[:TW], "edge", -1)
    near, put, take, flip = call(
        functools.partial(slots_kernel, cap_slots),
        (
            pltpu.VMEM((per_tile, width), f32),
            pltpu.VMEM((slots, per_tile), bf16),
            pltpu.VMEM((per_tile, slots), bf16),
            pltpu.VMEM((2, TW, LANES), jnp.int32),
        ),
        (far(tile), far(owners.reshape(1, per_tile)), far(orient[0])),
        in_specs=[hbm] * 3,
        scratch=(pltpu.VMEM((1, per_tile), jnp.int32), pltpu.VMEM((1, 2), jnp.int32), dma((3,))),
        cost=cost(1),
    )
    moved, outgoing = call(
        edge_kernel,
        (pltpu.VMEM((per_tile, width), f32), jax.ShapeDtypeStruct((slots, 2 * L), f32)),
        (near, low, high, flip, put),
        cost=cost(1),
    )
    received = lax.all_to_all(
        outgoing.reshape(n_tiles, cap_slots, 2 * L), "cols", split_axis=0, concat_axis=0, tiled=True
    ).reshape(slots, 2 * L)
    prepared = call(
        prepare_kernel,
        (
            pltpu.VMEM((rows_f, slots), bf16),
            pltpu.VMEM((ZP, slots), f32),
            pltpu.VMEM((ZP, slots), f32),
            pltpu.VMEM((6, ZP, slots), f32),
            pltpu.VMEM((2 * ZP, 2 * L), f32),
        ),
        (far(crm_state[0, 0]), far(active_levels[0]), far(diffusion), far(vertical_map)),
        in_specs=[hbm] * 4,
        scratch=(
            pltpu.VMEM((CZ, CX * slots), bf16),
            pltpu.VMEM((1, slots), jnp.int32),
            pltpu.SMEM((CZ - 1,), f32),
            pltpu.VMEM((CZ, L), f32),
            dma((4,)),
        ),
        cost=cost(4),
    )
    tend, after = call(
        physics_kernel,
        (jax.ShapeDtypeStruct((slots, 2 * L), f32), pltpu.VMEM((rows_f, slots), bf16)),
        (received, *prepared),
        scratch=(
            pltpu.VMEM((rows_f, slots), f32),
            pltpu.VMEM((5, ZP, slots), f32),
            pltpu.VMEM((2, ZP * SUB, LANES), f32),
        ),
        cost=cost(5),
    )
    returned = lax.all_to_all(
        tend.reshape(n_tiles, cap_slots, 2 * L), "cols", split_axis=0, concat_axis=0, tiled=True
    ).reshape(slots, 2 * L)
    crm_new = call(
        store_kernel,
        jax.ShapeDtypeStruct((CZ, CX * slots), bf16),
        (after,),
        scratch=(pltpu.VMEM((CZ, CX * slots), bf16), dma((NI // 2 * SUB,))),
        out_specs=hbm,
        cost=cost(3),
    )
    new_state = call(
        finish_kernel,
        jax.ShapeDtypeStruct((per_tile, width), f32),
        (moved, take, returned),
        cost=cost(0.7),
    )
    return (new_state[None], crm_new[None, None])


def solution(mesh):
    in_specs = (
        P("edge", "cols", None),
        P("edge", "cols", None),
        P("edge", "cols", None),
        P("edge", "cols", None, None),
        P("edge", "cols", None),
        P(),
        P(),
    )
    out_specs = (P("edge", "cols", None), P("edge", "cols", None, None))
    return jax.shard_map(shards, mesh=mesh, in_specs=in_specs, out_specs=out_specs, check_vma=False)
```

```python
import functools

import jax
import jax.numpy as jnp
from jax import lax
from jax.experimental import pallas as pl
from jax.experimental.pallas import tpu as pltpu
from jax.sharding import PartitionSpec as P

L = 64
CX = 64
CZ = 58
TW = 8
SUBSTEPS = 2
ZP = 64
LANES = 128
SUB = 8
NI = CX // SUB
TZ = 16

kappa_edge = 0.25
max_courant = 0.9
relax_rate = 0.5

HI = lax.Precision.HIGHEST


def call(body, outs, args, scratch=(), in_specs=None, out_specs=None, cost=None, limit=32 << 20, aliases=None):
    kw = {}
    if out_specs is not None:
        kw["out_specs"] = out_specs
    if in_specs is not None:
        kw["in_specs"] = in_specs
    return pl.pallas_call(
        body,
        out_shape=outs,
        scratch_shapes=list(scratch),
        compiler_params=pltpu.CompilerParams(vmem_limit_bytes=limit),
        cost_estimate=cost,
        input_output_aliases=aliases or {},
        **kw,
    )(*args)


def dot(a, b, dims):
    return lax.dot_general(a, b, (dims, ((), ())), precision=HI, preferred_element_type=jnp.float32)


def from_behind(value, axis, steps):
    count = lax.axis_size(axis)
    pairs = [(source, (source + steps) % count) for source in range(count)]
    return lax.ppermute(value, axis, pairs)


def split_dot(chosen, value, dims=((1,), (0,))):
    high = value.astype(jnp.bfloat16)
    low = (value - high.astype(jnp.float32)).astype(jnp.bfloat16)
    pick = lambda part: lax.dot_general(chosen, part, (dims, ((), ())), preferred_element_type=jnp.float32)
    return pick(high) + pick(low)


def load_kernel(state_hbm, owners_hbm, orient_hbm, tile_ref, named_ref, flip_ref, own_ref, turn_ref, sems):
    copies = [
        pltpu.make_async_copy(owners_hbm, own_ref, sems.at[0]),
        pltpu.make_async_copy(orient_hbm, turn_ref, sems.at[1]),
        pltpu.make_async_copy(state_hbm, tile_ref, sems.at[2]),
    ]
    for copy in copies:
        copy.start()
    copies[0].wait()
    named_ref[...] = jnp.broadcast_to(own_ref[...].astype(jnp.float32), named_ref.shape)
    copies[1].wait()
    for k in range(2):
        flip_ref[k] = jnp.broadcast_to(turn_ref[0:1, k : k + 1], (TW, LANES))
    copies[2].wait()


def edge_kernel(tile_ref, low_ref, high_ref, flip_ref, named_ref, moved_ref, out_ref):
    per_tile, width = tile_ref.shape

    def turned(ref, k):
        value = ref[...]
        back = jnp.concatenate([value[TW - 1 - w : TW - w] for w in range(TW)], axis=0)
        flip = jnp.concatenate([flip_ref[k]] * (width // LANES), axis=1)
        return jnp.where(flip == 1, back, value)

    low = turned(low_ref, 0)
    high = turned(high_ref, 1)
    tiles = tile_ref[...]
    below = jnp.concatenate([low, tiles[: per_tile - TW]], axis=0)
    above = jnp.concatenate([tiles[TW:], high], axis=0)
    moved = tiles + kappa_edge * ((above + below) - 2.0 * tiles)
    out_ref[:per_tile, :] = moved[:, : 2 * L]
    out_ref[per_tile:, :] = named_ref[...]
    moved_ref[...] = moved


def rows_from_levels(flipped):
    n = 2 * SUB * TZ
    a = lax.broadcasted_iota(jnp.int32, (n, n), 1 if flipped else 0)
    b = lax.broadcasted_iota(jnp.int32, (n, n), 0 if flipped else 1)
    z, p, s = a >> 4, (a >> 3) & 1, a & 7
    return jnp.where(b == p * (SUB * TZ) + s * TZ + z, 1.0, 0.0).astype(jnp.bfloat16)


def prepare_kernel(
    crm_hbm, active_hbm, diff_hbm, vm_hbm, f_ref, mean_ref, sq_ref, coef_ref, w_ref, crm_ref, act_ref, diff_ref, vm_ref, sems
):
    slots = active_hbm.shape[1]
    copies = [
        pltpu.make_async_copy(active_hbm, act_ref, sems.at[0]),
        pltpu.make_async_copy(diff_hbm, diff_ref, sems.at[1]),
        pltpu.make_async_copy(vm_hbm, vm_ref, sems.at[2]),
        pltpu.make_async_copy(crm_hbm, crm_ref, sems.at[3]),
    ]
    for copy in copies:
        copy.start()
    order = rows_from_levels(False)
    coef_ref[...] = jnp.zeros_like(coef_ref)
    w_ref[...] = jnp.zeros_like(w_ref)
    copies[0].wait()
    copies[1].wait()
    active = act_ref[...]
    nothing = jnp.zeros((1, slots), jnp.float32)

    def link(i):
        if i < 0 or i >= CZ - 1:
            return nothing
        return jnp.where(i + 1 < active, diff_ref[i], 0.0)

    up, down = nothing, nothing
    for z in range(CZ):
        lower, upper = link(z - 1), link(z)
        up = 1.0 / (1.0 + lower + upper - lower * (lower * up))
        coef_ref[0, z : z + 1, :] = up
        coef_ref[1, z : z + 1, :] = lower * up
        coef_ref[2, z : z + 1, :] = upper * up
        y = CZ - 1 - z
        lower, upper = link(y - 1), link(y)
        down = 1.0 / (1.0 + lower + upper - upper * (upper * down))
        coef_ref[3, y : y + 1, :] = down
        coef_ref[4, y : y + 1, :] = upper * down
        coef_ref[5, y : y + 1, :] = lower * down
    copies[2].wait()
    pad = jnp.zeros((CZ, L), jnp.float32)
    w_ref[0:CZ, :] = jnp.concatenate([vm_ref[...], pad], axis=1)
    w_ref[ZP : ZP + CZ, :] = jnp.concatenate([pad, vm_ref[...]], axis=1)

    copies[3].wait()
    for t in range(ZP // TZ):
        rows = min(TZ, CZ - t * TZ)
        total = jnp.zeros((TZ, slots), jnp.float32)
        square = jnp.zeros((TZ, slots), jnp.float32)
        for p in range(NI // 2):
            parts = []
            for i in (2 * p, 2 * p + 1):
                for s in range(SUB):
                    x = s * NI + i
                    v = crm_ref[t * TZ : t * TZ + rows, x * slots : (x + 1) * slots]
                    wide = v.astype(jnp.float32)
                    if rows < TZ:
                        wide = jnp.concatenate([wide, jnp.zeros((TZ - rows, slots), jnp.float32)], axis=0)
                        v = wide.astype(jnp.bfloat16)
                    total = total + wide
                    square = square + wide * wide
                    parts.append(v)
            turned = lax.dot_general(
                order, jnp.concatenate(parts, axis=0), (((1,), (0,)), ((), ())), preferred_element_type=jnp.float32
            ).astype(jnp.bfloat16)
            for z in range(rows):
                base = (t * TZ + z) * CX + p * 2 * SUB
                f_ref[base : base + 2 * SUB, :] = turned[z * 2 * SUB : (z + 1) * 2 * SUB]
        mean_ref[t * TZ : (t + 1) * TZ, :] = total * (1.0 / CX)
        sq_ref[t * TZ : (t + 1) * TZ, :] = square * (1.0 / CX)


def physics_kernel(
    all_ref, f_ref, mean_ref, sq_ref, coef_ref, w_ref, tend_ref, y_ref, g_ref, adv_ref, acc_ref, sel_ref, cols_ref
):
    n_tiles = all_ref.shape[0]
    slots = f_ref.shape[1]
    per_tile = all_ref.shape[1] - SUB
    cap = slots // n_tiles
    halves = slots // LANES
    me = lax.axis_index("cols").astype(jnp.float32)
    named = jnp.concatenate([all_ref[t, per_tile : per_tile + 1, :] for t in range(n_tiles)], axis=0)
    mine = jnp.where(named == me, 1.0, 0.0)
    row = lax.broadcasted_iota(jnp.int32, (per_tile, per_tile), 0)
    col = lax.broadcasted_iota(jnp.int32, (per_tile, per_tile), 1)
    earlier = jnp.where(row < col, 1.0, 0.0).astype(jnp.bfloat16)
    rank = lax.dot_general(
        mine.astype(jnp.bfloat16), earlier, (((1,), (0,)), ((), ())), preferred_element_type=jnp.float32
    )
    rank = jnp.where(mine == 1.0, rank, -1.0)
    place = lax.broadcasted_iota(jnp.int32, (cap, per_tile), 0).astype(jnp.float32)
    for t in range(n_tiles):
        chosen = jnp.where(rank[t : t + 1] == place, 1.0, 0.0).astype(jnp.bfloat16)
        sel_ref[t] = chosen
        cols_ref[t * cap : (t + 1) * cap, :] = split_dot(chosen, all_ref[t, :per_tile, :])
    w = w_ref[...]
    mapped = dot(w, cols_ref[...], ((1,), (1,)))
    forcing = mapped[0:ZP]
    courant = max_courant * jax.nn.sigmoid(mapped[ZP:])
    inv1 = coef_ref[0]
    inv2 = coef_ref[3]
    adv_ref[0] = inv1 * (1.0 - courant)
    adv_ref[1] = inv1 * courant
    adv_ref[2] = inv2 * (1.0 - courant)
    adv_ref[3] = inv2 * courant
    adv_ref[4] = inv1 * (relax_rate * (forcing - mean_ref[...]))

    def spread(ref, k, z, lane):
        return jnp.broadcast_to(ref[k, z : z + 1, lane], (SUB, LANES))

    dev = []
    for h in range(halves):
        lane = slice(h * LANES, (h + 1) * LANES)

        def at(z, i, n=1):
            base = z * CX + i * SUB
            return slice(base, base + n * SUB)

        zero = jnp.zeros((SUB, LANES), jnp.float32)
        prev = [zero] * NI
        for z in range(CZ):
            a, b = spread(adv_ref, 0, z, lane), spread(adv_ref, 1, z, lane)
            d, e = spread(adv_ref, 4, z, lane), spread(coef_ref, 1, z, lane)
            f = []
            for i in range(0, NI, 2):
                pair = f_ref[at(z, i, 2), lane].astype(jnp.float32)
                f += [pair[:SUB], pair[SUB:]]
            behind = [pltpu.roll(f[NI - 1], 1, axis=0)] + f[: NI - 1]
            prev = [(a * f[i] + b * behind[i]) + (d + e * prev[i]) for i in range(NI)]
            for i in range(NI):
                g_ref[at(z, i), lane] = prev[i]
        after = [zero] * NI
        prev = [zero] * NI
        for z in range(CZ - 1, -1, -1):
            g = spread(coef_ref, 2, z, lane)
            a, b = spread(adv_ref, 2, z, lane), spread(adv_ref, 3, z, lane)
            e = spread(coef_ref, 4, z, lane)
            after = [g_ref[at(z, i), lane] + g * after[i] for i in range(NI)]
            behind = [pltpu.roll(after[NI - 1], 1, axis=0)] + after[: NI - 1]
            prev = [(a * after[i] + b * behind[i]) + e * prev[i] for i in range(NI)]
            for i in range(NI):
                g_ref[at(z, i), lane] = prev[i]
        after = [zero] * NI
        for z in range(CZ):
            g = spread(coef_ref, 5, z, lane)
            after = [g_ref[at(z, i), lane] + g * after[i] for i in range(NI)]
            total, square = after[0], after[0] * after[0]
            for i in range(1, NI):
                total = total + after[i]
                square = square + after[i] * after[i]
            for i in range(0, NI, 2):
                y_ref[at(z, i, 2), lane] = jnp.concatenate(after[i : i + 2], axis=0).astype(jnp.bfloat16)
            acc_ref[0, z * SUB : (z + 1) * SUB, :] = total
            acc_ref[1, z * SUB : (z + 1) * SUB, :] = square
        acc_ref[:, CZ * SUB :, :] = jnp.zeros((2, (ZP - CZ) * SUB, LANES), jnp.float32)
        sums = []
        for k in range(2):
            part = acc_ref[k, pl.ds(0, ZP, stride=SUB), :]
            for s in range(1, SUB):
                part = part + acc_ref[k, pl.ds(s, ZP, stride=SUB), :]
            sums.append(part * (1.0 / CX))
        mean0, sq0 = mean_ref[:, lane], sq_ref[:, lane]
        mean1, sq1 = sums
        dev.append(jnp.concatenate([mean1 - mean0, (sq1 - mean1 * mean1) - (sq0 - mean0 * mean0)], axis=0))
    x = jnp.concatenate(dev, axis=1)
    tend = dot(x, w, ((0,), (0,)))
    for t in range(n_tiles):
        tend_ref[t * per_tile : (t + 1) * per_tile, :] = split_dot(
            sel_ref[t], tend[t * cap : (t + 1) * cap], ((0,), (0,))
        )


def store_kernel(y_ref, crm_hbm, crm_ref, sems):
    slots = crm_hbm.shape[1] // CX
    order = rows_from_levels(True)
    copies = []
    for p in range(NI // 2):
        for t in range(ZP // TZ):
            rows = min(TZ, CZ - t * TZ)
            parts = [y_ref[(t * TZ + z) * CX + p * 2 * SUB : (t * TZ + z) * CX + (p + 1) * 2 * SUB, :] for z in range(rows)]
            if rows < TZ:
                parts.append(jnp.zeros(((TZ - rows) * 2 * SUB, slots), jnp.bfloat16))
            turned = lax.dot_general(
                order, jnp.concatenate(parts, axis=0), (((1,), (0,)), ((), ())), preferred_element_type=jnp.float32
            ).astype(jnp.bfloat16)
            for i in range(2):
                for s in range(SUB):
                    x = s * NI + 2 * p + i
                    k = (i * SUB + s) * TZ
                    crm_ref[t * TZ : t * TZ + rows, x * slots : (x + 1) * slots] = turned[k : k + rows]
        for s in range(SUB):
            here = pl.ds((s * NI + 2 * p) * slots, 2 * slots)
            copy = pltpu.make_async_copy(crm_ref.at[:, here], crm_hbm.at[:, here], sems.at[p * SUB + s])
            copy.start()
            copies.append(copy)
    for copy in copies:
        copy.wait()


def finish_kernel(moved_ref, back_ref, out_ref):
    out_ref[:, 2 * L :] = moved_ref[:, 2 * L :]
    out_ref[:, : 2 * L] = moved_ref[:, : 2 * L] + back_ref[...]


def cost(us):
    return pl.CostEstimate(flops=0, bytes_accessed=int(us * 3.0e6), transcendentals=0)


def far(x):
    return pltpu.with_memory_space_constraint(x, pltpu.HBM)


def shards(state, owners, orient, crm_state, active_levels, vertical_map, diffusion):
    f32, bf16 = jnp.float32, jnp.bfloat16
    n_tiles = lax.axis_size("cols")
    per_tile = state.shape[1]
    width = state.shape[2]
    cap_slots = max(2, 2 * per_tile // n_tiles)
    slots = n_tiles * cap_slots
    rows_f = CZ * CX
    hbm = pl.BlockSpec(memory_space=pltpu.HBM)
    dma = pltpu.SemaphoreType.DMA
    tile = state[0]
    low = from_behind(tile[per_tile - TW :], "edge", 1)
    high = from_behind(tile[:TW], "edge", -1)
    near, named, flip = call(
        load_kernel,
        (
            pltpu.VMEM((per_tile, width), f32),
            pltpu.VMEM((SUB, per_tile), f32),
            pltpu.VMEM((2, TW, LANES), jnp.int32),
        ),
        (far(tile), far(owners.reshape(1, per_tile)), far(orient[0])),
        in_specs=[hbm] * 3,
        scratch=(pltpu.VMEM((1, per_tile), jnp.int32), pltpu.VMEM((1, 2), jnp.int32), dma((3,))),
        cost=cost(1),
    )
    moved, outgoing = call(
        edge_kernel,
        (pltpu.VMEM((per_tile, width), f32), jax.ShapeDtypeStruct((per_tile + SUB, 2 * L), f32)),
        (near, low, high, flip, named),
        cost=cost(1),
    )
    received = lax.all_gather(outgoing, "cols")
    prepared = call(
        prepare_kernel,
        (
            pltpu.VMEM((rows_f, slots), bf16),
            pltpu.VMEM((ZP, slots), f32),
            pltpu.VMEM((ZP, slots), f32),
            pltpu.VMEM((6, ZP, slots), f32),
            pltpu.VMEM((2 * ZP, 2 * L), f32),
        ),
        (far(crm_state[0, 0]), far(active_levels[0]), far(diffusion), far(vertical_map)),
        in_specs=[hbm] * 4,
        scratch=(
            pltpu.VMEM((CZ, CX * slots), bf16),
            pltpu.VMEM((1, slots), jnp.int32),
            pltpu.SMEM((CZ - 1,), f32),
            pltpu.VMEM((CZ, L), f32),
            dma((4,)),
        ),
        cost=cost(4),
    )
    tend, after = call(
        physics_kernel,
        (jax.ShapeDtypeStruct((n_tiles * per_tile, 2 * L), f32), pltpu.VMEM((rows_f, slots), bf16)),
        (received, *prepared),
        scratch=(
            pltpu.VMEM((rows_f, slots), f32),
            pltpu.VMEM((5, ZP, slots), f32),
            pltpu.VMEM((2, ZP * SUB, LANES), f32),
            pltpu.VMEM((n_tiles, cap_slots, per_tile), bf16),
            pltpu.VMEM((slots, 2 * L), f32),
        ),
        cost=cost(5),
    )
    returned = lax.psum_scatter(tend, "cols", scatter_dimension=0, tiled=True)
    crm_new = call(
        store_kernel,
        jax.ShapeDtypeStruct((CZ, CX * slots), bf16),
        (after,),
        scratch=(pltpu.VMEM((CZ, CX * slots), bf16), dma((NI // 2 * SUB,))),
        out_specs=hbm,
        cost=cost(3),
    )
    new_state = call(
        finish_kernel,
        jax.ShapeDtypeStruct((per_tile, width), f32),
        (moved, returned),
        cost=cost(0.7),
    )
    return (new_state[None], crm_new[None, None])


def solution(mesh):
    in_specs = (
        P("edge", "cols", None),
        P("edge", "cols", None),
        P("edge", "cols", None),
        P("edge", "cols", None, None),
        P("edge", "cols", None),
        P(),
        P(),
    )
    out_specs = (P("edge", "cols", None), P("edge", "cols", None, None))
    return jax.shard_map(shards, mesh=mesh, in_specs=in_specs, out_specs=out_specs, check_vma=False)
```

```python
import functools

import jax
import jax.numpy as jnp
from jax import lax
from jax.experimental import pallas as pl
from jax.experimental.pallas import tpu as pltpu
from jax.sharding import PartitionSpec as P

L = 64
CX = 64
CZ = 58
TW = 8
SUBSTEPS = 2
ZP = 64
LANES = 128
SUB = 8
NI = CX // SUB
TZ = 16

kappa_edge = 0.25
max_courant = 0.9
relax_rate = 0.5


def call(body, outs, args, scratch=(), in_specs=None, out_specs=None, cost=None, limit=32 << 20, aliases=None):
    kw = {}
    if out_specs is not None:
        kw["out_specs"] = out_specs
    if in_specs is not None:
        kw["in_specs"] = in_specs
    return pl.pallas_call(
        body,
        out_shape=outs,
        scratch_shapes=list(scratch),
        compiler_params=pltpu.CompilerParams(vmem_limit_bytes=limit),
        cost_estimate=cost,
        input_output_aliases=aliases or {},
        **kw,
    )(*args)


def from_behind(value, axis, steps):
    count = lax.axis_size(axis)
    pairs = [(source, (source + steps) % count) for source in range(count)]
    return lax.ppermute(value, axis, pairs)


def split_dot(chosen, value):
    high, low = parts_of(value)
    pick = lambda part: lax.dot_general(chosen, part, (((1,), (0,)), ((), ())), preferred_element_type=jnp.float32)
    return pick(high) + pick(low)


def parts_of(value):
    high = value.astype(jnp.bfloat16)
    return high, (value - high.astype(jnp.float32)).astype(jnp.bfloat16)


def rows_kernel(state_hbm, upper_ref, lower_ref, sems):
    per_tile = state_hbm.shape[0]
    copies = [
        pltpu.make_async_copy(state_hbm.at[per_tile - TW :], upper_ref, sems.at[0]),
        pltpu.make_async_copy(state_hbm.at[:TW], lower_ref, sems.at[1]),
    ]
    for copy in copies:
        copy.start()
    for copy in copies:
        copy.wait()


def slots_kernel(cap, state_hbm, owners_hbm, orient_hbm, tile_ref, put_ref, take_ref, flip_ref, own_ref, turn_ref, sems):
    per_tile = owners_hbm.shape[1]
    n_slots = put_ref.shape[0]
    copies = [
        pltpu.make_async_copy(owners_hbm, own_ref, sems.at[0]),
        pltpu.make_async_copy(orient_hbm, turn_ref, sems.at[1]),
        pltpu.make_async_copy(state_hbm, tile_ref, sems.at[2]),
    ]
    for copy in copies:
        copy.start()
    row = lax.broadcasted_iota(jnp.int32, (per_tile, per_tile), 0)
    col = lax.broadcasted_iota(jnp.int32, (per_tile, per_tile), 1)
    q_down = lax.broadcasted_iota(jnp.int32, (n_slots, per_tile), 0)
    q_across = lax.broadcasted_iota(jnp.int32, (per_tile, n_slots), 1)
    copies[0].wait()
    across = jnp.broadcast_to(own_ref[...], (per_tile, per_tile))
    down = across.T
    same = down == across
    before_col = jnp.where(same & (row < col), 1.0, 0.0)
    before_row = jnp.where(same & (col < row), 1.0, 0.0)
    rank_across = jnp.sum(before_col, axis=0, keepdims=True).astype(jnp.int32)
    rank_down = jnp.sum(before_row, axis=1, keepdims=True).astype(jnp.int32)
    slot_across = across[0:1, :] * cap + rank_across
    slot_down = down[:, 0:1] * cap + rank_down
    put_ref[...] = jnp.where(q_down == slot_across, 1.0, 0.0).astype(jnp.bfloat16)
    take_ref[...] = jnp.where(q_across == slot_down, 1.0, 0.0).astype(jnp.bfloat16)
    copies[1].wait()
    for k in range(2):
        flip_ref[k] = jnp.broadcast_to(turn_ref[0:1, k : k + 1], (TW, LANES))
    copies[2].wait()


def edge_kernel(tile_ref, low_ref, high_ref, flip_ref, put_ref, moved_ref, out_ref):
    per_tile, width = tile_ref.shape

    def turned(ref, k):
        value = ref[...]
        back = jnp.concatenate([value[TW - 1 - w : TW - w] for w in range(TW)], axis=0)
        flip = jnp.concatenate([flip_ref[k]] * (width // LANES), axis=1)
        return jnp.where(flip == 1, back, value)

    low = turned(low_ref, 0)
    high = turned(high_ref, 1)
    tiles = tile_ref[...]
    below = jnp.concatenate([low, tiles[: per_tile - TW]], axis=0)
    above = jnp.concatenate([tiles[TW:], high], axis=0)
    moved = tiles + kappa_edge * ((above + below) - 2.0 * tiles)
    out_ref[...] = split_dot(put_ref[...], moved[:, : 2 * L])
    moved_ref[...] = moved


def rows_from_levels(flipped):
    n = 2 * SUB * TZ
    a = lax.broadcasted_iota(jnp.int32, (n, n), 1 if flipped else 0)
    b = lax.broadcasted_iota(jnp.int32, (n, n), 0 if flipped else 1)
    z, p, s = a >> 4, (a >> 3) & 1, a & 7
    return jnp.where(b == p * (SUB * TZ) + s * TZ + z, 1.0, 0.0).astype(jnp.bfloat16)


def prepare_kernel(
    crm_hbm, active_hbm, diff_hbm, vm_hbm, f_ref, mean_ref, sq_ref, coef_ref, wa_ref, wb_ref, crm_ref, act_ref, diff_ref, vm_ref, sems
):
    slots = active_hbm.shape[1]
    copies = [
        pltpu.make_async_copy(active_hbm, act_ref, sems.at[0]),
        pltpu.make_async_copy(diff_hbm, diff_ref, sems.at[1]),
        pltpu.make_async_copy(vm_hbm, vm_ref, sems.at[2]),
        pltpu.make_async_copy(crm_hbm, crm_ref, sems.at[3]),
    ]
    for copy in copies:
        copy.start()
    order = rows_from_levels(False)
    coef_ref[...] = jnp.zeros_like(coef_ref)
    copies[0].wait()
    copies[1].wait()
    active = act_ref[...]
    nothing = jnp.zeros((1, slots), jnp.float32)

    def link(i):
        if i < 0 or i >= CZ - 1:
            return nothing
        return jnp.where(i + 1 < active, diff_ref[i], 0.0)

    up, down = nothing, nothing
    for z in range(CZ):
        lower, upper = link(z - 1), link(z)
        up = 1.0 / (1.0 + lower + upper - lower * (lower * up))
        coef_ref[0, z : z + 1, :] = up
        coef_ref[1, z : z + 1, :] = lower * up
        coef_ref[2, z : z + 1, :] = upper * up
        y = CZ - 1 - z
        lower, upper = link(y - 1), link(y)
        down = 1.0 / (1.0 + lower + upper - upper * (upper * down))
        coef_ref[3, y : y + 1, :] = down
        coef_ref[4, y : y + 1, :] = upper * down
        coef_ref[5, y : y + 1, :] = lower * down
    copies[2].wait()
    pad = jnp.zeros((CZ, L), jnp.float32)
    rest = jnp.zeros((ZP - CZ, 2 * L), jnp.float32)
    both = [jnp.concatenate([vm_ref[...], pad], axis=1), rest, jnp.concatenate([pad, vm_ref[...]], axis=1), rest]
    high, low = parts_of(jnp.concatenate(both, axis=0))
    wa_ref[...] = jnp.concatenate([high, low, high], axis=1)
    wb_ref[...] = jnp.concatenate([high, high, low], axis=0)

    copies[3].wait()
    for t in range(ZP // TZ):
        rows = min(TZ, CZ - t * TZ)
        total = jnp.zeros((TZ, slots), jnp.float32)
        square = jnp.zeros((TZ, slots), jnp.float32)
        for p in range(NI // 2):
            parts = []
            for i in (2 * p, 2 * p + 1):
                for s in range(SUB):
                    x = s * NI + i
                    v = crm_ref[t * TZ : t * TZ + rows, x * slots : (x + 1) * slots]
                    wide = v.astype(jnp.float32)
                    if rows < TZ:
                        wide = jnp.concatenate([wide, jnp.zeros((TZ - rows, slots), jnp.float32)], axis=0)
                        v = wide.astype(jnp.bfloat16)
                    total = total + wide
                    square = square + wide * wide
                    parts.append(v)
            turned = lax.dot_general(
                order, jnp.concatenate(parts, axis=0), (((1,), (0,)), ((), ())), preferred_element_type=jnp.float32
            ).astype(jnp.bfloat16)
            for z in range(rows):
                base = (t * TZ + z) * CX + p * 2 * SUB
                f_ref[base : base + 2 * SUB, :] = turned[z * 2 * SUB : (z + 1) * 2 * SUB]
        mean_ref[t * TZ : (t + 1) * TZ, :] = total * (1.0 / CX)
        sq_ref[t * TZ : (t + 1) * TZ, :] = square * (1.0 / CX)


def physics_kernel(
    cols_ref, f_ref, mean_ref, sq_ref, coef_ref, wa_ref, wb_ref, tend_ref, y_ref, g_ref, adv_ref, sum_ref
):
    slots = cols_ref.shape[0]
    halves = slots // LANES
    for h in range(halves):
        lane = slice(h * LANES, (h + 1) * LANES)
        high, low = parts_of(cols_ref[lane, :])
        mapped = lax.dot_general(
            wa_ref[...],
            jnp.concatenate([high, high, low], axis=1),
            (((1,), (1,)), ((), ())),
            preferred_element_type=jnp.float32,
        )
        forcing = mapped[0:ZP]
        courant = max_courant * jax.nn.sigmoid(mapped[ZP:])
        inv1 = coef_ref[0, :, lane]
        inv2 = coef_ref[3, :, lane]
        adv_ref[0, :, lane] = inv1 * (1.0 - courant)
        adv_ref[1, :, lane] = inv1 * courant
        adv_ref[2, :, lane] = inv2 * (1.0 - courant)
        adv_ref[3, :, lane] = inv2 * courant
        adv_ref[4, :, lane] = inv1 * (relax_rate * (forcing - mean_ref[:, lane]))
    sum_ref[:, CZ:, :] = jnp.zeros((2, ZP - CZ, slots), jnp.float32)

    def spread(ref, k, z, lane):
        return jnp.broadcast_to(ref[k, z : z + 1, lane], (SUB, LANES))

    for h in range(halves):
        lane = slice(h * LANES, (h + 1) * LANES)

        def at(z, i, n=1):
            base = z * CX + i * SUB
            return slice(base, base + n * SUB)

        zero = jnp.zeros((SUB, LANES), jnp.float32)
        prev = [zero] * NI
        for z in range(CZ):
            a, b = spread(adv_ref, 0, z, lane), spread(adv_ref, 1, z, lane)
            d, e = spread(adv_ref, 4, z, lane), spread(coef_ref, 1, z, lane)
            f = []
            for i in range(0, NI, 2):
                pair = f_ref[at(z, i, 2), lane].astype(jnp.float32)
                f += [pair[:SUB], pair[SUB:]]
            behind = [pltpu.roll(f[NI - 1], 1, axis=0)] + f[: NI - 1]
            prev = [((a * f[i] + d) + b * behind[i]) + e * prev[i] for i in range(NI)]
            for i in range(NI):
                g_ref[at(z, i), lane] = prev[i]
        after = [zero] * NI
        prev = [zero] * NI
        for z in range(CZ - 1, -1, -1):
            g = spread(coef_ref, 2, z, lane)
            a, b = spread(adv_ref, 2, z, lane), spread(adv_ref, 3, z, lane)
            e = spread(coef_ref, 4, z, lane)
            after = [g_ref[at(z, i), lane] + g * after[i] for i in range(NI)]
            behind = [pltpu.roll(after[NI - 1], 1, axis=0)] + after[: NI - 1]
            prev = [(a * after[i] + b * behind[i]) + e * prev[i] for i in range(NI)]
            for i in range(NI):
                g_ref[at(z, i), lane] = prev[i]
        after = [zero] * NI
        for z in range(CZ):
            g = spread(coef_ref, 5, z, lane)
            after = [g_ref[at(z, i), lane] + g * after[i] for i in range(NI)]
            total = [after[i] + after[i + 1] for i in range(0, NI, 2)]
            square = [after[i] * after[i] + after[i + 1] * after[i + 1] for i in range(0, NI, 2)]
            for i in range(0, NI, 2):
                y_ref[at(z, i, 2), lane] = jnp.concatenate(after[i : i + 2], axis=0).astype(jnp.bfloat16)
            sum_ref[0, z : z + 1, lane] = jnp.sum((total[0] + total[1]) + (total[2] + total[3]), axis=0, keepdims=True)
            sum_ref[1, z : z + 1, lane] = jnp.sum((square[0] + square[1]) + (square[2] + square[3]), axis=0, keepdims=True)
        mean0, sq0 = mean_ref[:, lane], sq_ref[:, lane]
        mean1, sq1 = sum_ref[0, :, lane] * (1.0 / CX), sum_ref[1, :, lane] * (1.0 / CX)
        change = jnp.concatenate([mean1 - mean0, (sq1 - mean1 * mean1) - (sq0 - mean0 * mean0)], axis=0)
        high, low = parts_of(change)
        tend_ref[lane, :] = lax.dot_general(
            jnp.concatenate([high, low, high], axis=0),
            wb_ref[...],
            (((0,), (0,)), ((), ())),
            preferred_element_type=jnp.float32,
        )


def store_kernel(y_ref, crm_hbm, crm_ref, sems):
    slots = crm_hbm.shape[1] // CX
    order = rows_from_levels(True)
    copies = []
    for p in range(NI // 2):
        for t in range(ZP // TZ):
            rows = min(TZ, CZ - t * TZ)
            parts = [y_ref[(t * TZ + z) * CX + p * 2 * SUB : (t * TZ + z) * CX + (p + 1) * 2 * SUB, :] for z in range(rows)]
            if rows < TZ:
                parts.append(jnp.zeros(((TZ - rows) * 2 * SUB, slots), jnp.bfloat16))
            turned = lax.dot_general(
                order, jnp.concatenate(parts, axis=0), (((1,), (0,)), ((), ())), preferred_element_type=jnp.float32
            ).astype(jnp.bfloat16)
            for i in range(2):
                for s in range(SUB):
                    x = s * NI + 2 * p + i
                    k = (i * SUB + s) * TZ
                    crm_ref[t * TZ : t * TZ + rows, x * slots : (x + 1) * slots] = turned[k : k + rows]
        for s in range(SUB):
            here = pl.ds((s * NI + 2 * p) * slots, 2 * slots)
            copy = pltpu.make_async_copy(crm_ref.at[:, here], crm_hbm.at[:, here], sems.at[p * SUB + s])
            copy.start()
            copies.append(copy)
    for copy in copies:
        copy.wait()


def finish_kernel(moved_ref, take_ref, back_ref, out_hbm, part_ref, sems):
    rest = pltpu.make_async_copy(moved_ref.at[:, 2 * L :], out_hbm.at[:, 2 * L :], sems.at[0])
    rest.start()
    part_ref[...] = moved_ref[:, : 2 * L] + split_dot(take_ref[...], back_ref[...])
    first = pltpu.make_async_copy(part_ref, out_hbm.at[:, : 2 * L], sems.at[1])
    first.start()
    rest.wait()
    first.wait()


def cost(us):
    return pl.CostEstimate(flops=0, bytes_accessed=int(us * 3.0e6), transcendentals=0)


def far(x):
    return pltpu.with_memory_space_constraint(x, pltpu.HBM)


def shards(state, owners, orient, crm_state, active_levels, vertical_map, diffusion):
    f32, bf16 = jnp.float32, jnp.bfloat16
    n_tiles = lax.axis_size("cols")
    per_tile = state.shape[1]
    width = state.shape[2]
    cap_slots = max(2, 2 * per_tile // n_tiles)
    slots = n_tiles * cap_slots
    rows_f = CZ * CX
    hbm = pl.BlockSpec(memory_space=pltpu.HBM)
    dma = pltpu.SemaphoreType.DMA
    tile = state[0]
    upper, lower = call(
        rows_kernel,
        (pltpu.VMEM((TW, width), f32), pltpu.VMEM((TW, width), f32)),
        (far(tile),),
        in_specs=[hbm],
        scratch=(dma((2,)),),
        cost=cost(0.5),
    )
    low = from_behind(upper, "edge", 1)
    high = from_behind(lower, "edge", -1)
    near, put, take, flip = call(
        functools.partial(slots_kernel, cap_slots),
        (
            pltpu.VMEM((per_tile, width), f32),
            pltpu.VMEM((slots, per_tile), bf16),
            pltpu.VMEM((per_tile, slots), bf16),
            pltpu.VMEM((2, TW, LANES), jnp.int32),
        ),
        (far(tile), far(owners.reshape(1, per_tile)), far(orient[0])),
        in_specs=[hbm] * 3,
        scratch=(pltpu.VMEM((1, per_tile), jnp.int32), pltpu.VMEM((1, 2), jnp.int32), dma((3,))),
        cost=cost(1),
    )
    moved, outgoing = call(
        edge_kernel,
        (pltpu.VMEM((per_tile, width), f32), jax.ShapeDtypeStruct((slots, 2 * L), f32)),
        (near, low, high, flip, put),
        cost=cost(1),
    )
    received = lax.all_to_all(
        outgoing.reshape(n_tiles, cap_slots, 2 * L), "cols", split_axis=0, concat_axis=0, tiled=True
    ).reshape(slots, 2 * L)
    prepared = call(
        prepare_kernel,
        (
            pltpu.VMEM((rows_f, slots), bf16),
            pltpu.VMEM((ZP, slots), f32),
            pltpu.VMEM((ZP, slots), f32),
            pltpu.VMEM((6, ZP, slots), f32),
            pltpu.VMEM((2 * ZP, 6 * L), bf16),
            pltpu.VMEM((6 * ZP, 2 * L), bf16),
        ),
        (far(crm_state[0, 0]), far(active_levels[0]), far(diffusion), far(vertical_map)),
        in_specs=[hbm] * 4,
        scratch=(
            pltpu.VMEM((CZ, CX * slots), bf16),
            pltpu.VMEM((1, slots), jnp.int32),
            pltpu.SMEM((CZ - 1,), f32),
            pltpu.VMEM((CZ, L), f32),
            dma((4,)),
        ),
        cost=cost(4),
    )
    tend, after = call(
        physics_kernel,
        (jax.ShapeDtypeStruct((slots, 2 * L), f32), pltpu.VMEM((rows_f, slots), bf16)),
        (received, *prepared),
        scratch=(
            pltpu.VMEM((rows_f, slots), f32),
            pltpu.VMEM((5, ZP, slots), f32),
            pltpu.VMEM((2, ZP, slots), f32),
        ),
        aliases={1: 1},
        cost=cost(5),
    )
    returned = lax.all_to_all(
        tend.reshape(n_tiles, cap_slots, 2 * L), "cols", split_axis=0, concat_axis=0, tiled=True
    ).reshape(slots, 2 * L)
    crm_new = call(
        store_kernel,
        jax.ShapeDtypeStruct((CZ, CX * slots), bf16),
        (after,),
        scratch=(pltpu.VMEM((CZ, CX * slots), bf16), dma((NI // 2 * SUB,))),
        out_specs=hbm,
        cost=cost(3),
    )
    new_state = call(
        finish_kernel,
        jax.ShapeDtypeStruct((per_tile, width), f32),
        (moved, take, returned),
        scratch=(pltpu.VMEM((per_tile, 2 * L), f32), dma((2,))),
        out_specs=hbm,
        cost=cost(0.7),
    )
    return (new_state[None], crm_new[None, None])


def solution(mesh):
    in_specs = (
        P("edge", "cols", None),
        P("edge", "cols", None),
        P("edge", "cols", None),
        P("edge", "cols", None, None),
        P("edge", "cols", None),
        P(),
        P(),
    )
    out_specs = (P("edge", "cols", None), P("edge", "cols", None, None))
    return jax.shard_map(shards, mesh=mesh, in_specs=in_specs, out_specs=out_specs, check_vma=False)
```

```python
import functools

import jax
import jax.numpy as jnp
from jax import lax
from jax.experimental import pallas as pl
from jax.experimental.pallas import tpu as pltpu
from jax.sharding import PartitionSpec as P

L = 64
CX = 64
CZ = 58
TW = 8
SUBSTEPS = 2
ZP = 64
LANES = 128
SUB = 8
NI = CX // SUB
TZ = 16

kappa_edge = 0.25
max_courant = 0.9
relax_rate = 0.5


def call(body, outs, args, scratch=(), in_specs=None, out_specs=None, cost=None, limit=32 << 20, aliases=None):
    kw = {}
    if out_specs is not None:
        kw["out_specs"] = out_specs
    if in_specs is not None:
        kw["in_specs"] = in_specs
    return pl.pallas_call(
        body,
        out_shape=outs,
        scratch_shapes=list(scratch),
        compiler_params=pltpu.CompilerParams(vmem_limit_bytes=limit),
        cost_estimate=cost,
        input_output_aliases=aliases or {},
        **kw,
    )(*args)


def from_behind(value, axis, steps):
    count = lax.axis_size(axis)
    pairs = [(source, (source + steps) % count) for source in range(count)]
    return lax.ppermute(value, axis, pairs)


def split_dot(chosen, value):
    high, low = parts_of(value)
    pick = lambda part: lax.dot_general(chosen, part, (((1,), (0,)), ((), ())), preferred_element_type=jnp.float32)
    return pick(high) + pick(low)


def parts_of(value):
    high = value.astype(jnp.bfloat16)
    return high, (value - high.astype(jnp.float32)).astype(jnp.bfloat16)


def rows_kernel(state_hbm, upper_ref, lower_ref, sems):
    per_tile = state_hbm.shape[0]
    copies = [
        pltpu.make_async_copy(state_hbm.at[per_tile - TW :], upper_ref, sems.at[0]),
        pltpu.make_async_copy(state_hbm.at[:TW], lower_ref, sems.at[1]),
    ]
    for copy in copies:
        copy.start()
    for copy in copies:
        copy.wait()


def slots_kernel(cap, state_hbm, owners_hbm, orient_hbm, tile_ref, put_ref, take_ref, flip_ref, own_ref, turn_ref, sems):
    per_tile = owners_hbm.shape[1]
    n_slots = put_ref.shape[0]
    copies = [
        pltpu.make_async_copy(owners_hbm, own_ref, sems.at[0]),
        pltpu.make_async_copy(orient_hbm, turn_ref, sems.at[1]),
        pltpu.make_async_copy(state_hbm, tile_ref, sems.at[2]),
    ]
    for copy in copies:
        copy.start()
    row = lax.broadcasted_iota(jnp.int32, (per_tile, per_tile), 0)
    col = lax.broadcasted_iota(jnp.int32, (per_tile, per_tile), 1)
    q_down = lax.broadcasted_iota(jnp.int32, (n_slots, per_tile), 0)
    q_across = lax.broadcasted_iota(jnp.int32, (per_tile, n_slots), 1)
    copies[0].wait()
    across = jnp.broadcast_to(own_ref[...], (per_tile, per_tile))
    down = across.T
    same = down == across
    before_col = jnp.where(same & (row < col), 1.0, 0.0)
    before_row = jnp.where(same & (col < row), 1.0, 0.0)
    rank_across = jnp.sum(before_col, axis=0, keepdims=True).astype(jnp.int32)
    rank_down = jnp.sum(before_row, axis=1, keepdims=True).astype(jnp.int32)
    slot_across = across[0:1, :] * cap + rank_across
    slot_down = down[:, 0:1] * cap + rank_down
    put_ref[...] = jnp.where(q_down == slot_across, 1.0, 0.0).astype(jnp.bfloat16)
    take_ref[...] = jnp.where(q_across == slot_down, 1.0, 0.0).astype(jnp.bfloat16)
    copies[1].wait()
    for k in range(2):
        flip_ref[k] = jnp.broadcast_to(turn_ref[0:1, k : k + 1], (TW, LANES))
    copies[2].wait()


def edge_kernel(tile_ref, low_ref, high_ref, flip_ref, put_ref, moved_ref, out_ref):
    per_tile, width = tile_ref.shape

    def turned(ref, k):
        value = ref[...]
        back = jnp.concatenate([value[TW - 1 - w : TW - w] for w in range(TW)], axis=0)
        flip = jnp.concatenate([flip_ref[k]] * (width // LANES), axis=1)
        return jnp.where(flip == 1, back, value)

    low = turned(low_ref, 0)
    high = turned(high_ref, 1)
    tiles = tile_ref[...]
    below = jnp.concatenate([low, tiles[: per_tile - TW]], axis=0)
    above = jnp.concatenate([tiles[TW:], high], axis=0)
    moved = tiles + kappa_edge * ((above + below) - 2.0 * tiles)
    out_ref[...] = split_dot(put_ref[...], moved[:, : 2 * L])
    moved_ref[...] = moved


def rows_from_levels(flipped):
    n = 2 * SUB * TZ
    a = lax.broadcasted_iota(jnp.int32, (n, n), 1 if flipped else 0)
    b = lax.broadcasted_iota(jnp.int32, (n, n), 0 if flipped else 1)
    z, p, s = a >> 4, (a >> 3) & 1, a & 7
    return jnp.where(b == p * (SUB * TZ) + s * TZ + z, 1.0, 0.0).astype(jnp.bfloat16)


def prepare_kernel(
    crm_hbm, active_hbm, diff_hbm, vm_hbm, f_ref, mean_ref, sq_ref, coef_ref, wa_ref, wb_ref, crm_ref, act_ref, diff_ref, vm_ref, sems
):
    slots = active_hbm.shape[1]
    copies = [
        pltpu.make_async_copy(active_hbm, act_ref, sems.at[0]),
        pltpu.make_async_copy(diff_hbm, diff_ref, sems.at[1]),
        pltpu.make_async_copy(vm_hbm, vm_ref, sems.at[2]),
        pltpu.make_async_copy(crm_hbm, crm_ref, sems.at[3]),
    ]
    for copy in copies:
        copy.start()
    order = rows_from_levels(False)
    coef_ref[...] = jnp.zeros_like(coef_ref)
    copies[0].wait()
    copies[1].wait()
    active = act_ref[...]
    nothing = jnp.zeros((1, slots), jnp.float32)

    def link(i):
        if i < 0 or i >= CZ - 1:
            return nothing
        return jnp.where(i + 1 < active, diff_ref[i], 0.0)

    up, down = nothing, nothing
    for z in range(CZ):
        lower, upper = link(z - 1), link(z)
        up = 1.0 / (1.0 + lower + upper - lower * (lower * up))
        coef_ref[0, z : z + 1, :] = up
        coef_ref[1, z : z + 1, :] = lower * up
        coef_ref[2, z : z + 1, :] = upper * up
        y = CZ - 1 - z
        lower, upper = link(y - 1), link(y)
        down = 1.0 / (1.0 + lower + upper - upper * (upper * down))
        coef_ref[3, y : y + 1, :] = down
        coef_ref[4, y : y + 1, :] = upper * down
        coef_ref[5, y : y + 1, :] = lower * down
    copies[2].wait()
    pad = jnp.zeros((CZ, L), jnp.float32)
    rest = jnp.zeros((ZP - CZ, 2 * L), jnp.float32)
    both = [jnp.concatenate([vm_ref[...], pad], axis=1), rest, jnp.concatenate([pad, vm_ref[...]], axis=1), rest]
    high, low = parts_of(jnp.concatenate(both, axis=0))
    wa_ref[...] = jnp.concatenate([high, low, high], axis=1)
    wb_ref[...] = jnp.concatenate([high, high, low], axis=0)

    copies[3].wait()
    for t in range(ZP // TZ):
        rows = min(TZ, CZ - t * TZ)
        total = jnp.zeros((TZ, slots), jnp.float32)
        square = jnp.zeros((TZ, slots), jnp.float32)
        for p in range(NI // 2):
            parts = []
            for i in (2 * p, 2 * p + 1):
                for s in range(SUB):
                    x = s * NI + i
                    v = crm_ref[t * TZ : t * TZ + rows, x * slots : (x + 1) * slots]
                    wide = v.astype(jnp.float32)
                    if rows < TZ:
                        wide = jnp.concatenate([wide, jnp.zeros((TZ - rows, slots), jnp.float32)], axis=0)
                        v = wide.astype(jnp.bfloat16)
                    total = total + wide
                    square = square + wide * wide
                    parts.append(v)
            turned = lax.dot_general(
                order, jnp.concatenate(parts, axis=0), (((1,), (0,)), ((), ())), preferred_element_type=jnp.float32
            ).astype(jnp.bfloat16)
            for z in range(rows):
                base = (t * TZ + z) * CX + p * 2 * SUB
                f_ref[base : base + 2 * SUB, :] = turned[z * 2 * SUB : (z + 1) * 2 * SUB]
        mean_ref[t * TZ : (t + 1) * TZ, :] = total * (1.0 / CX)
        sq_ref[t * TZ : (t + 1) * TZ, :] = square * (1.0 / CX)


def physics_kernel(
    cols_ref, f_ref, mean_ref, sq_ref, coef_ref, wa_ref, wb_ref, tend_ref, y_ref, g_ref, adv_ref, sum_ref
):
    slots = cols_ref.shape[0]
    halves = slots // LANES
    for h in range(halves):
        lane = slice(h * LANES, (h + 1) * LANES)
        high, low = parts_of(cols_ref[lane, :])
        mapped = lax.dot_general(
            wa_ref[...],
            jnp.concatenate([high, high, low], axis=1),
            (((1,), (1,)), ((), ())),
            preferred_element_type=jnp.float32,
        )
        forcing = mapped[0:ZP]
        courant = max_courant * jax.nn.sigmoid(mapped[ZP:])
        inv1 = coef_ref[0, :, lane]
        inv2 = coef_ref[3, :, lane]
        adv_ref[0, :, lane] = inv1 * (1.0 - courant)
        adv_ref[1, :, lane] = inv1 * courant
        adv_ref[2, :, lane] = inv2 * (1.0 - courant)
        adv_ref[3, :, lane] = inv2 * courant
        adv_ref[4, :, lane] = inv1 * (relax_rate * (forcing - mean_ref[:, lane]))
    sum_ref[:, CZ:, :] = jnp.zeros((2, ZP - CZ, slots), jnp.float32)

    lanes = [slice(h * LANES, (h + 1) * LANES) for h in range(halves)]
    whole = CZ // SUB
    zero = jnp.zeros((SUB, LANES), jnp.float32)
    still = tuple(tuple(zero for _ in range(NI)) for _ in range(halves))

    def group(ref, k, base):
        return ref.at[k, pl.ds(base, SUB), :]

    def spread(rows, u, lane):
        return jnp.broadcast_to(rows[u : u + 1, lane], (SUB, LANES))

    def at(base, u, i, n=1):
        return pl.ds(pl.multiple_of(base * CX + (u * CX + i * SUB), n * SUB), n * SUB)

    def rise(base, levels, carry):
        prev = list(carry)
        rows = [group(adv_ref, 0, base), group(adv_ref, 1, base), group(adv_ref, 4, base), group(coef_ref, 1, base)]
        for u in levels:
            for h, lane in enumerate(lanes):
                a, b, d, e = [spread(r, u, lane) for r in rows]
                f = []
                for i in range(0, NI, 2):
                    pair = f_ref[at(base, u, i, 2), lane].astype(jnp.float32)
                    f += [pair[:SUB], pair[SUB:]]
                behind = [pltpu.roll(f[NI - 1], 1, axis=0)] + f[: NI - 1]
                prev[h] = tuple(((a * f[i] + d) + b * behind[i]) + e * prev[h][i] for i in range(NI))
                for i in range(NI):
                    g_ref[at(base, u, i), lane] = prev[h][i]
        return tuple(prev)

    def fall(base, levels, carry):
        after, prev = list(carry[0]), list(carry[1])
        rows = [group(coef_ref, 2, base), group(adv_ref, 2, base), group(adv_ref, 3, base), group(coef_ref, 4, base)]
        for u in levels:
            for h, lane in enumerate(lanes):
                g, a, b, e = [spread(r, u, lane) for r in rows]
                y = tuple(g_ref[at(base, u, i), lane] + g * after[h][i] for i in range(NI))
                behind = (pltpu.roll(y[NI - 1], 1, axis=0),) + y[: NI - 1]
                after[h] = y
                prev[h] = tuple((a * y[i] + b * behind[i]) + e * prev[h][i] for i in range(NI))
                for i in range(NI):
                    g_ref[at(base, u, i), lane] = prev[h][i]
        return tuple(after), tuple(prev)

    def settle(base, levels, carry):
        after = list(carry)
        rows = group(coef_ref, 5, base)
        sums = [group(sum_ref, q, base) for q in range(2)]
        for u in levels:
            for h, lane in enumerate(lanes):
                g = spread(rows, u, lane)
                y = tuple(g_ref[at(base, u, i), lane] + g * after[h][i] for i in range(NI))
                after[h] = y
                for i in range(0, NI, 2):
                    y_ref[at(base, u, i, 2), lane] = jnp.concatenate(y[i : i + 2], axis=0).astype(jnp.bfloat16)
                for q in range(2):
                    part = [v * v for v in y] if q else list(y)
                    while len(part) > 1:
                        part = [part[i] + part[i + 1] for i in range(0, len(part), 2)]
                    sums[q][u : u + 1, lane] = jnp.sum(part[0], axis=0, keepdims=True)
        return tuple(after)

    every, some = range(SUB), range(CZ - whole * SUB)
    base_of = lambda k: pl.multiple_of(k * SUB, SUB)
    last = whole * SUB
    carry = lax.fori_loop(0, whole, lambda k, c: rise(base_of(k), every, c), still)
    rise(last, some, carry)
    carry = fall(last, some[::-1], (still, still))
    lax.fori_loop(0, whole, lambda k, c: fall(base_of(whole - 1 - k), every[::-1], c), carry)
    carry = lax.fori_loop(0, whole, lambda k, c: settle(base_of(k), every, c), still)
    settle(last, some, carry)
    for lane in lanes:
        mean0, sq0 = mean_ref[:, lane], sq_ref[:, lane]
        mean1, sq1 = sum_ref[0, :, lane] * (1.0 / CX), sum_ref[1, :, lane] * (1.0 / CX)
        change = jnp.concatenate([mean1 - mean0, (sq1 - mean1 * mean1) - (sq0 - mean0 * mean0)], axis=0)
        high, low = parts_of(change)
        tend_ref[lane, :] = lax.dot_general(
            jnp.concatenate([high, low, high], axis=0),
            wb_ref[...],
            (((0,), (0,)), ((), ())),
            preferred_element_type=jnp.float32,
        )


def store_kernel(y_ref, crm_hbm, crm_ref, sems):
    slots = crm_hbm.shape[1] // CX
    order = rows_from_levels(True)
    copies = []
    for p in range(NI // 2):
        for t in range(ZP // TZ):
            rows = min(TZ, CZ - t * TZ)
            parts = [y_ref[(t * TZ + z) * CX + p * 2 * SUB : (t * TZ + z) * CX + (p + 1) * 2 * SUB, :] for z in range(rows)]
            if rows < TZ:
                parts.append(jnp.zeros(((TZ - rows) * 2 * SUB, slots), jnp.bfloat16))
            turned = lax.dot_general(
                order, jnp.concatenate(parts, axis=0), (((1,), (0,)), ((), ())), preferred_element_type=jnp.float32
            ).astype(jnp.bfloat16)
            for i in range(2):
                for s in range(SUB):
                    x = s * NI + 2 * p + i
                    k = (i * SUB + s) * TZ
                    crm_ref[t * TZ : t * TZ + rows, x * slots : (x + 1) * slots] = turned[k : k + rows]
        for s in range(SUB):
            here = pl.ds((s * NI + 2 * p) * slots, 2 * slots)
            copy = pltpu.make_async_copy(crm_ref.at[:, here], crm_hbm.at[:, here], sems.at[p * SUB + s])
            copy.start()
            copies.append(copy)
    for copy in copies:
        copy.wait()


def finish_kernel(moved_ref, take_ref, back_ref, out_hbm, part_ref, sems):
    rest = pltpu.make_async_copy(moved_ref.at[:, 2 * L :], out_hbm.at[:, 2 * L :], sems.at[0])
    rest.start()
    part_ref[...] = moved_ref[:, : 2 * L] + split_dot(take_ref[...], back_ref[...])
    first = pltpu.make_async_copy(part_ref, out_hbm.at[:, : 2 * L], sems.at[1])
    first.start()
    rest.wait()
    first.wait()


def cost(us):
    return pl.CostEstimate(flops=0, bytes_accessed=int(us * 3.0e6), transcendentals=0)


def far(x):
    return pltpu.with_memory_space_constraint(x, pltpu.HBM)


def shards(state, owners, orient, crm_state, active_levels, vertical_map, diffusion):
    f32, bf16 = jnp.float32, jnp.bfloat16
    n_tiles = lax.axis_size("cols")
    per_tile = state.shape[1]
    width = state.shape[2]
    cap_slots = max(2, 2 * per_tile // n_tiles)
    slots = n_tiles * cap_slots
    rows_f = CZ * CX
    hbm = pl.BlockSpec(memory_space=pltpu.HBM)
    dma = pltpu.SemaphoreType.DMA
    tile = state[0]
    upper, lower = call(
        rows_kernel,
        (pltpu.VMEM((TW, width), f32), pltpu.VMEM((TW, width), f32)),
        (far(tile),),
        in_specs=[hbm],
        scratch=(dma((2,)),),
        cost=cost(0.5),
    )
    low = from_behind(upper, "edge", 1)
    high = from_behind(lower, "edge", -1)
    near, put, take, flip = call(
        functools.partial(slots_kernel, cap_slots),
        (
            pltpu.VMEM((per_tile, width), f32),
            pltpu.VMEM((slots, per_tile), bf16),
            pltpu.VMEM((per_tile, slots), bf16),
            pltpu.VMEM((2, TW, LANES), jnp.int32),
        ),
        (far(tile), far(owners.reshape(1, per_tile)), far(orient[0])),
        in_specs=[hbm] * 3,
        scratch=(pltpu.VMEM((1, per_tile), jnp.int32), pltpu.VMEM((1, 2), jnp.int32), dma((3,))),
        cost=cost(1),
    )
    moved, outgoing = call(
        edge_kernel,
        (pltpu.VMEM((per_tile, width), f32), pltpu.VMEM((slots, 2 * L), f32)),
        (near, low, high, flip, put),
        cost=cost(1),
    )
    received = lax.all_to_all(
        outgoing.reshape(n_tiles, cap_slots, 2 * L), "cols", split_axis=0, concat_axis=0, tiled=True
    ).reshape(slots, 2 * L)
    prepared = call(
        prepare_kernel,
        (
            pltpu.VMEM((rows_f, slots), bf16),
            pltpu.VMEM((ZP, slots), f32),
            pltpu.VMEM((ZP, slots), f32),
            pltpu.VMEM((6, ZP, slots), f32),
            pltpu.VMEM((2 * ZP, 6 * L), bf16),
            pltpu.VMEM((6 * ZP, 2 * L), bf16),
        ),
        (far(crm_state[0, 0]), far(active_levels[0]), far(diffusion), far(vertical_map)),
        in_specs=[hbm] * 4,
        scratch=(
            pltpu.VMEM((CZ, CX * slots), bf16),
            pltpu.VMEM((1, slots), jnp.int32),
            pltpu.SMEM((CZ - 1,), f32),
            pltpu.VMEM((CZ, L), f32),
            dma((4,)),
        ),
        cost=cost(4),
    )
    tend, after = call(
        physics_kernel,
        (pltpu.VMEM((slots, 2 * L), f32), pltpu.VMEM((rows_f, slots), bf16)),
        (received, *prepared),
        scratch=(
            pltpu.VMEM((rows_f, slots), f32),
            pltpu.VMEM((5, ZP, slots), f32),
            pltpu.VMEM((2, ZP, slots), f32),
        ),
        aliases={1: 1},
        cost=cost(5),
    )
    returned = lax.all_to_all(
        tend.reshape(n_tiles, cap_slots, 2 * L), "cols", split_axis=0, concat_axis=0, tiled=True
    ).reshape(slots, 2 * L)
    crm_new = call(
        store_kernel,
        jax.ShapeDtypeStruct((CZ, CX * slots), bf16),
        (after,),
        scratch=(pltpu.VMEM((CZ, CX * slots), bf16), dma((NI // 2 * SUB,))),
        out_specs=hbm,
        cost=cost(3),
    )
    new_state = call(
        finish_kernel,
        jax.ShapeDtypeStruct((per_tile, width), f32),
        (moved, take, returned),
        scratch=(pltpu.VMEM((per_tile, 2 * L), f32), dma((2,))),
        out_specs=hbm,
        cost=cost(0.7),
    )
    return (new_state[None], crm_new[None, None])


def solution(mesh):
    in_specs = (
        P("edge", "cols", None),
        P("edge", "cols", None),
        P("edge", "cols", None),
        P("edge", "cols", None, None),
        P("edge", "cols", None),
        P(),
        P(),
    )
    out_specs = (P("edge", "cols", None), P("edge", "cols", None, None))
    return jax.shard_map(shards, mesh=mesh, in_specs=in_specs, out_specs=out_specs, check_vma=False)
```

```python
import functools

import jax
import jax.numpy as jnp
from jax import lax
from jax.experimental import pallas as pl
from jax.experimental.pallas import tpu as pltpu
from jax.sharding import PartitionSpec as P

L = 64
CX = 64
CZ = 58
TW = 8
SUBSTEPS = 2
ZP = 64
LANES = 128
SUB = 8
NI = CX // SUB
TZ = 16

kappa_edge = 0.25
max_courant = 0.9
relax_rate = 0.5


def call(body, outs, args, scratch=(), in_specs=None, out_specs=None, cost=None, limit=32 << 20, aliases=None):
    kw = {}
    if out_specs is not None:
        kw["out_specs"] = out_specs
    if in_specs is not None:
        kw["in_specs"] = in_specs
    return pl.pallas_call(
        body,
        out_shape=outs,
        scratch_shapes=list(scratch),
        compiler_params=pltpu.CompilerParams(vmem_limit_bytes=limit),
        cost_estimate=cost,
        input_output_aliases=aliases or {},
        **kw,
    )(*args)


def from_behind(value, axis, steps):
    count = lax.axis_size(axis)
    pairs = [(source, (source + steps) % count) for source in range(count)]
    return lax.ppermute(value, axis, pairs)


def exchange(pieces):
    count = lax.axis_size("cols")
    if len(pieces) == 1:
        whole = pieces[0].reshape(count, -1, pieces[0].shape[1])
        return [lax.all_to_all(whole, "cols", split_axis=0, concat_axis=0, tiled=True).reshape(pieces[0].shape)]
    out = list(pieces)
    for k in sorted(range(1, count), reverse=True):
        out[k] = lax.ppermute(pieces[k], "cols", [(c, c ^ k) for c in range(count)])
    return out


def place_of(k, pieces, rows):
    if pieces == 1:
        return 0
    return pl.multiple_of((lax.axis_index("cols") ^ k) * rows, SUB)


def split_dot(chosen, value):
    high, low = parts_of(value)
    pick = lambda part: lax.dot_general(chosen, part, (((1,), (0,)), ((), ())), preferred_element_type=jnp.float32)
    return pick(high) + pick(low)


def parts_of(value):
    high = value.astype(jnp.bfloat16)
    return high, (value - high.astype(jnp.float32)).astype(jnp.bfloat16)


def rows_kernel(state_hbm, upper_ref, lower_ref, sems):
    per_tile = state_hbm.shape[0]
    copies = [
        pltpu.make_async_copy(state_hbm.at[per_tile - TW :], upper_ref, sems.at[0]),
        pltpu.make_async_copy(state_hbm.at[:TW], lower_ref, sems.at[1]),
    ]
    for copy in copies:
        copy.start()
    for copy in copies:
        copy.wait()


def slots_kernel(cap, pieces, state_hbm, owners_hbm, orient_hbm, tile_ref, put_ref, take_ref, flip_ref, own_ref, turn_ref, sems):
    per_tile = owners_hbm.shape[1]
    n_slots = put_ref.shape[0]
    copies = [
        pltpu.make_async_copy(owners_hbm, own_ref, sems.at[0]),
        pltpu.make_async_copy(orient_hbm, turn_ref, sems.at[1]),
        pltpu.make_async_copy(state_hbm, tile_ref, sems.at[2]),
    ]
    for copy in copies:
        copy.start()
    row = lax.broadcasted_iota(jnp.int32, (per_tile, per_tile), 0)
    col = lax.broadcasted_iota(jnp.int32, (per_tile, per_tile), 1)
    q_down = lax.broadcasted_iota(jnp.int32, (n_slots, per_tile), 0)
    q_across = lax.broadcasted_iota(jnp.int32, (per_tile, n_slots), 1)
    copies[0].wait()
    named = own_ref[...]
    if pieces > 1:
        named = named ^ lax.axis_index("cols")
    across = jnp.broadcast_to(named, (per_tile, per_tile))
    down = across.T
    same = down == across
    before_col = jnp.where(same & (row < col), 1.0, 0.0)
    before_row = jnp.where(same & (col < row), 1.0, 0.0)
    rank_across = jnp.sum(before_col, axis=0, keepdims=True).astype(jnp.int32)
    rank_down = jnp.sum(before_row, axis=1, keepdims=True).astype(jnp.int32)
    slot_across = across[0:1, :] * cap + rank_across
    slot_down = down[:, 0:1] * cap + rank_down
    put_ref[...] = jnp.where(q_down == slot_across, 1.0, 0.0).astype(jnp.bfloat16)
    take_ref[...] = jnp.where(q_across == slot_down, 1.0, 0.0).astype(jnp.bfloat16)
    copies[1].wait()
    for k in range(2):
        flip_ref[k] = jnp.broadcast_to(turn_ref[0:1, k : k + 1], (TW, LANES))
    copies[2].wait()


def edge_kernel(tile_ref, low_ref, high_ref, flip_ref, put_ref, moved_ref, *out_refs):
    per_tile, width = tile_ref.shape

    def turned(ref, k):
        value = ref[...]
        back = jnp.concatenate([value[TW - 1 - w : TW - w] for w in range(TW)], axis=0)
        flip = jnp.concatenate([flip_ref[k]] * (width // LANES), axis=1)
        return jnp.where(flip == 1, back, value)

    low = turned(low_ref, 0)
    high = turned(high_ref, 1)
    tiles = tile_ref[...]
    below = jnp.concatenate([low, tiles[: per_tile - TW]], axis=0)
    above = jnp.concatenate([tiles[TW:], high], axis=0)
    moved = tiles + kappa_edge * ((above + below) - 2.0 * tiles)
    picked = split_dot(put_ref[...], moved[:, : 2 * L])
    for k, ref in enumerate(out_refs):
        rows = ref.shape[0]
        ref[...] = picked[k * rows : (k + 1) * rows]
    moved_ref[...] = moved


def rows_from_levels(flipped):
    n = 2 * SUB * TZ
    a = lax.broadcasted_iota(jnp.int32, (n, n), 1 if flipped else 0)
    b = lax.broadcasted_iota(jnp.int32, (n, n), 0 if flipped else 1)
    z, p, s = a >> 4, (a >> 3) & 1, a & 7
    return jnp.where(b == p * (SUB * TZ) + s * TZ + z, 1.0, 0.0).astype(jnp.bfloat16)


def prepare_kernel(
    crm_hbm, active_hbm, diff_hbm, vm_hbm, f_ref, mean_ref, sq_ref, coef_ref, wa_ref, wb_ref, crm_ref, act_ref, diff_ref, vm_ref, sems
):
    slots = active_hbm.shape[1]
    copies = [
        pltpu.make_async_copy(active_hbm, act_ref, sems.at[0]),
        pltpu.make_async_copy(diff_hbm, diff_ref, sems.at[1]),
        pltpu.make_async_copy(vm_hbm, vm_ref, sems.at[2]),
        pltpu.make_async_copy(crm_hbm, crm_ref, sems.at[3]),
    ]
    for copy in copies:
        copy.start()
    order = rows_from_levels(False)
    coef_ref[...] = jnp.zeros_like(coef_ref)
    copies[0].wait()
    copies[1].wait()
    active = act_ref[...]
    nothing = jnp.zeros((1, slots), jnp.float32)

    def link(i):
        if i < 0 or i >= CZ - 1:
            return nothing
        return jnp.where(i + 1 < active, diff_ref[i], 0.0)

    up, down = nothing, nothing
    for z in range(CZ):
        lower, upper = link(z - 1), link(z)
        up = 1.0 / (1.0 + lower + upper - lower * (lower * up))
        coef_ref[0, z : z + 1, :] = up
        coef_ref[1, z : z + 1, :] = lower * up
        coef_ref[2, z : z + 1, :] = upper * up
        y = CZ - 1 - z
        lower, upper = link(y - 1), link(y)
        down = 1.0 / (1.0 + lower + upper - upper * (upper * down))
        coef_ref[3, y : y + 1, :] = down
        coef_ref[4, y : y + 1, :] = upper * down
        coef_ref[5, y : y + 1, :] = lower * down
    copies[2].wait()
    pad = jnp.zeros((CZ, L), jnp.float32)
    rest = jnp.zeros((ZP - CZ, 2 * L), jnp.float32)
    both = [jnp.concatenate([vm_ref[...], pad], axis=1), rest, jnp.concatenate([pad, vm_ref[...]], axis=1), rest]
    high, low = parts_of(jnp.concatenate(both, axis=0))
    wa_ref[...] = jnp.concatenate([high, low, high], axis=1)
    wb_ref[...] = jnp.concatenate([high, high, low], axis=0)

    copies[3].wait()
    for t in range(ZP // TZ):
        rows = min(TZ, CZ - t * TZ)
        total = jnp.zeros((TZ, slots), jnp.float32)
        square = jnp.zeros((TZ, slots), jnp.float32)
        for p in range(NI // 2):
            parts = []
            for i in (2 * p, 2 * p + 1):
                for s in range(SUB):
                    x = s * NI + i
                    v = crm_ref[t * TZ : t * TZ + rows, x * slots : (x + 1) * slots]
                    wide = v.astype(jnp.float32)
                    if rows < TZ:
                        wide = jnp.concatenate([wide, jnp.zeros((TZ - rows, slots), jnp.float32)], axis=0)
                        v = wide.astype(jnp.bfloat16)
                    total = total + wide
                    square = square + wide * wide
                    parts.append(v)
            turned = lax.dot_general(
                order, jnp.concatenate(parts, axis=0), (((1,), (0,)), ((), ())), preferred_element_type=jnp.float32
            ).astype(jnp.bfloat16)
            for z in range(rows):
                base = (t * TZ + z) * CX + p * 2 * SUB
                f_ref[base : base + 2 * SUB, :] = turned[z * 2 * SUB : (z + 1) * 2 * SUB]
        mean_ref[t * TZ : (t + 1) * TZ, :] = total * (1.0 / CX)
        sq_ref[t * TZ : (t + 1) * TZ, :] = square * (1.0 / CX)


def physics_kernel(pieces, *refs):
    sent_refs, refs = refs[:pieces], refs[pieces:]
    f_ref, mean_ref, sq_ref, coef_ref, wa_ref, wb_ref, y_ref = refs[:7]
    back_refs = refs[7 : 7 + pieces]
    g_ref, adv_ref, sum_ref, cols_ref, tend_ref = refs[7 + pieces :]
    rows = sent_refs[0].shape[0]
    for k, ref in enumerate(sent_refs):
        cols_ref[pl.ds(place_of(k, pieces, rows), rows), :] = ref[...]
    slots = cols_ref.shape[0]
    halves = slots // LANES
    for h in range(halves):
        lane = slice(h * LANES, (h + 1) * LANES)
        high, low = parts_of(cols_ref[lane, :])
        mapped = lax.dot_general(
            wa_ref[...],
            jnp.concatenate([high, high, low], axis=1),
            (((1,), (1,)), ((), ())),
            preferred_element_type=jnp.float32,
        )
        forcing = mapped[0:ZP]
        courant = max_courant * jax.nn.sigmoid(mapped[ZP:])
        inv1 = coef_ref[0, :, lane]
        inv2 = coef_ref[3, :, lane]
        adv_ref[0, :, lane] = inv1 * (1.0 - courant)
        adv_ref[1, :, lane] = inv1 * courant
        adv_ref[2, :, lane] = inv2 * (1.0 - courant)
        adv_ref[3, :, lane] = inv2 * courant
        adv_ref[4, :, lane] = inv1 * (relax_rate * (forcing - mean_ref[:, lane]))
    sum_ref[:, CZ:, :] = jnp.zeros((2, ZP - CZ, slots), jnp.float32)

    def spread(ref, k, z, lane):
        return jnp.broadcast_to(ref[k, z : z + 1, lane], (SUB, LANES))

    for h in range(halves):
        lane = slice(h * LANES, (h + 1) * LANES)

        def at(z, i, n=1):
            base = z * CX + i * SUB
            return slice(base, base + n * SUB)

        zero = jnp.zeros((SUB, LANES), jnp.float32)
        prev = [zero] * NI
        for z in range(CZ):
            a, b = spread(adv_ref, 0, z, lane), spread(adv_ref, 1, z, lane)
            d, e = spread(adv_ref, 4, z, lane), spread(coef_ref, 1, z, lane)
            f = []
            for i in range(0, NI, 2):
                pair = f_ref[at(z, i, 2), lane].astype(jnp.float32)
                f += [pair[:SUB], pair[SUB:]]
            behind = [pltpu.roll(f[NI - 1], 1, axis=0)] + f[: NI - 1]
            prev = [((a * f[i] + d) + b * behind[i]) + e * prev[i] for i in range(NI)]
            for i in range(NI):
                g_ref[at(z, i), lane] = prev[i]
        after = [zero] * NI
        prev = [zero] * NI
        for z in range(CZ - 1, -1, -1):
            g = spread(coef_ref, 2, z, lane)
            a, b = spread(adv_ref, 2, z, lane), spread(adv_ref, 3, z, lane)
            e = spread(coef_ref, 4, z, lane)
            after = [g_ref[at(z, i), lane] + g * after[i] for i in range(NI)]
            behind = [pltpu.roll(after[NI - 1], 1, axis=0)] + after[: NI - 1]
            prev = [(a * after[i] + b * behind[i]) + e * prev[i] for i in range(NI)]
            for i in range(NI):
                g_ref[at(z, i), lane] = prev[i]
        after = [zero] * NI
        for z in range(CZ):
            g = spread(coef_ref, 5, z, lane)
            after = [g_ref[at(z, i), lane] + g * after[i] for i in range(NI)]
            total = [after[i] + after[i + 1] for i in range(0, NI, 2)]
            square = [after[i] * after[i] + after[i + 1] * after[i + 1] for i in range(0, NI, 2)]
            for i in range(0, NI, 2):
                y_ref[at(z, i, 2), lane] = jnp.concatenate(after[i : i + 2], axis=0).astype(jnp.bfloat16)
            sum_ref[0, z : z + 1, lane] = jnp.sum((total[0] + total[1]) + (total[2] + total[3]), axis=0, keepdims=True)
            sum_ref[1, z : z + 1, lane] = jnp.sum((square[0] + square[1]) + (square[2] + square[3]), axis=0, keepdims=True)
        mean0, sq0 = mean_ref[:, lane], sq_ref[:, lane]
        mean1, sq1 = sum_ref[0, :, lane] * (1.0 / CX), sum_ref[1, :, lane] * (1.0 / CX)
        change = jnp.concatenate([mean1 - mean0, (sq1 - mean1 * mean1) - (sq0 - mean0 * mean0)], axis=0)
        high, low = parts_of(change)
        tend_ref[lane, :] = lax.dot_general(
            jnp.concatenate([high, low, high], axis=0),
            wb_ref[...],
            (((0,), (0,)), ((), ())),
            preferred_element_type=jnp.float32,
        )
    for k, ref in enumerate(back_refs):
        ref[...] = tend_ref[pl.ds(place_of(k, pieces, rows), rows), :]


def store_kernel(y_ref, crm_hbm, crm_ref, sems):
    slots = crm_hbm.shape[1] // CX
    order = rows_from_levels(True)
    copies = []
    for p in range(NI // 2):
        for t in range(ZP // TZ):
            rows = min(TZ, CZ - t * TZ)
            parts = [y_ref[(t * TZ + z) * CX + p * 2 * SUB : (t * TZ + z) * CX + (p + 1) * 2 * SUB, :] for z in range(rows)]
            if rows < TZ:
                parts.append(jnp.zeros(((TZ - rows) * 2 * SUB, slots), jnp.bfloat16))
            turned = lax.dot_general(
                order, jnp.concatenate(parts, axis=0), (((1,), (0,)), ((), ())), preferred_element_type=jnp.float32
            ).astype(jnp.bfloat16)
            for i in range(2):
                for s in range(SUB):
                    x = s * NI + 2 * p + i
                    k = (i * SUB + s) * TZ
                    crm_ref[t * TZ : t * TZ + rows, x * slots : (x + 1) * slots] = turned[k : k + rows]
        for s in range(SUB):
            here = pl.ds((s * NI + 2 * p) * slots, 2 * slots)
            copy = pltpu.make_async_copy(crm_ref.at[:, here], crm_hbm.at[:, here], sems.at[p * SUB + s])
            copy.start()
            copies.append(copy)
    for copy in copies:
        copy.wait()


def finish_kernel(pieces, moved_ref, take_ref, *refs):
    back_refs = refs[:pieces]
    out_hbm, part_ref, sems = refs[pieces:]
    back = jnp.concatenate([ref[...] for ref in back_refs], axis=0)
    rest = pltpu.make_async_copy(moved_ref.at[:, 2 * L :], out_hbm.at[:, 2 * L :], sems.at[0])
    rest.start()
    part_ref[...] = moved_ref[:, : 2 * L] + split_dot(take_ref[...], back)
    first = pltpu.make_async_copy(part_ref, out_hbm.at[:, : 2 * L], sems.at[1])
    first.start()
    rest.wait()
    first.wait()


def cost(us):
    return pl.CostEstimate(flops=0, bytes_accessed=int(us * 3.0e6), transcendentals=0)


def far(x):
    return pltpu.with_memory_space_constraint(x, pltpu.HBM)


def shards(state, owners, orient, crm_state, active_levels, vertical_map, diffusion):
    f32, bf16 = jnp.float32, jnp.bfloat16
    n_tiles = lax.axis_size("cols")
    per_tile = state.shape[1]
    width = state.shape[2]
    cap_slots = max(2, 2 * per_tile // n_tiles)
    slots = n_tiles * cap_slots
    rows_f = CZ * CX
    pieces = n_tiles if n_tiles <= 8 else 1
    piece = (slots // pieces, 2 * L)
    near_by = pltpu.VMEM(piece, f32) if pieces > 1 else jax.ShapeDtypeStruct(piece, f32)
    hbm = pl.BlockSpec(memory_space=pltpu.HBM)
    dma = pltpu.SemaphoreType.DMA
    tile = state[0]
    upper, lower = call(
        rows_kernel,
        (pltpu.VMEM((TW, width), f32), pltpu.VMEM((TW, width), f32)),
        (far(tile),),
        in_specs=[hbm],
        scratch=(dma((2,)),),
        cost=cost(0.5),
    )
    low = from_behind(upper, "edge", 1)
    high = from_behind(lower, "edge", -1)
    near, put, take, flip = call(
        functools.partial(slots_kernel, cap_slots, pieces),
        (
            pltpu.VMEM((per_tile, width), f32),
            pltpu.VMEM((slots, per_tile), bf16),
            pltpu.VMEM((per_tile, slots), bf16),
            pltpu.VMEM((2, TW, LANES), jnp.int32),
        ),
        (far(tile), far(owners.reshape(1, per_tile)), far(orient[0])),
        in_specs=[hbm] * 3,
        scratch=(pltpu.VMEM((1, per_tile), jnp.int32), pltpu.VMEM((1, 2), jnp.int32), dma((3,))),
        cost=cost(1),
    )
    moved, *outgoing = call(
        edge_kernel,
        (pltpu.VMEM((per_tile, width), f32), *[near_by] * pieces),
        (near, low, high, flip, put),
        cost=cost(1),
    )
    received = exchange(outgoing)
    prepared = call(
        prepare_kernel,
        (
            pltpu.VMEM((rows_f, slots), bf16),
            pltpu.VMEM((ZP, slots), f32),
            pltpu.VMEM((ZP, slots), f32),
            pltpu.VMEM((6, ZP, slots), f32),
            pltpu.VMEM((2 * ZP, 6 * L), bf16),
            pltpu.VMEM((6 * ZP, 2 * L), bf16),
        ),
        (far(crm_state[0, 0]), far(active_levels[0]), far(diffusion), far(vertical_map)),
        in_specs=[hbm] * 4,
        scratch=(
            pltpu.VMEM((CZ, CX * slots), bf16),
            pltpu.VMEM((1, slots), jnp.int32),
            pltpu.SMEM((CZ - 1,), f32),
            pltpu.VMEM((CZ, L), f32),
            dma((4,)),
        ),
        cost=cost(4),
    )
    after, *tend = call(
        functools.partial(physics_kernel, pieces),
        (pltpu.VMEM((rows_f, slots), bf16), *[near_by] * pieces),
        (*received, *prepared),
        scratch=(
            pltpu.VMEM((rows_f, slots), f32),
            pltpu.VMEM((5, ZP, slots), f32),
            pltpu.VMEM((2, ZP, slots), f32),
            pltpu.VMEM((slots, 2 * L), f32),
            pltpu.VMEM((slots, 2 * L), f32),
        ),
        aliases={pieces: 0},
        cost=cost(5),
    )
    returned = exchange(tend)
    crm_new = call(
        store_kernel,
        jax.ShapeDtypeStruct((CZ, CX * slots), bf16),
        (after,),
        scratch=(pltpu.VMEM((CZ, CX * slots), bf16), dma((NI // 2 * SUB,))),
        out_specs=hbm,
        cost=cost(3),
    )
    new_state = call(
        functools.partial(finish_kernel, pieces),
        jax.ShapeDtypeStruct((per_tile, width), f32),
        (moved, take, *returned),
        scratch=(pltpu.VMEM((per_tile, 2 * L), f32), dma((2,))),
        out_specs=hbm,
        cost=cost(0.7),
    )
    return (new_state[None], crm_new[None, None])


def solution(mesh):
    in_specs = (
        P("edge", "cols", None),
        P("edge", "cols", None),
        P("edge", "cols", None),
        P("edge", "cols", None, None),
        P("edge", "cols", None),
        P(),
        P(),
    )
    out_specs = (P("edge", "cols", None), P("edge", "cols", None, None))
    return jax.shard_map(shards, mesh=mesh, in_specs=in_specs, out_specs=out_specs, check_vma=False)
```

```python
import functools

import jax
import jax.numpy as jnp
from jax import lax
from jax.experimental import pallas as pl
from jax.experimental.pallas import tpu as pltpu
from jax.sharding import PartitionSpec as P

L = 64
CX = 64
CZ = 58
TW = 8
SUBSTEPS = 2
ZP = 64
LANES = 128
SUB = 8
NI = CX // SUB
TZ = 16

kappa_edge = 0.25
max_courant = 0.9
relax_rate = 0.5


def call(body, outs, args, scratch=(), in_specs=None, out_specs=None, cost=None, limit=32 << 20, aliases=None):
    kw = {}
    if out_specs is not None:
        kw["out_specs"] = out_specs
    if in_specs is not None:
        kw["in_specs"] = in_specs
    return pl.pallas_call(
        body,
        out_shape=outs,
        scratch_shapes=list(scratch),
        compiler_params=pltpu.CompilerParams(vmem_limit_bytes=limit),
        cost_estimate=cost,
        input_output_aliases=aliases or {},
        **kw,
    )(*args)


def swap(value, axis, first):
    count = lax.axis_size(axis)
    pairs = []
    for one in range(first, count, 2):
        other = (one + 1) % count
        pairs += [(one, other), (other, one)]
    return lax.ppermute(value, axis, pairs)


def odd_strip():
    return lax.rem(lax.axis_index("edge"), 2)


def split_dot(chosen, value):
    high, low = parts_of(value)
    pick = lambda part: lax.dot_general(chosen, part, (((1,), (0,)), ((), ())), preferred_element_type=jnp.float32)
    return pick(high) + pick(low)


def parts_of(value):
    high = value.astype(jnp.bfloat16)
    return high, (value - high.astype(jnp.float32)).astype(jnp.bfloat16)


def rows_kernel(state_hbm, outer_ref, inner_ref, sems):
    last = state_hbm.shape[0] - TW
    outer = pl.multiple_of(odd_strip() * last, TW)
    inner = pl.multiple_of((1 - odd_strip()) * last, TW)
    copies = [
        pltpu.make_async_copy(state_hbm.at[pl.ds(outer, TW)], outer_ref, sems.at[0]),
        pltpu.make_async_copy(state_hbm.at[pl.ds(inner, TW)], inner_ref, sems.at[1]),
    ]
    for copy in copies:
        copy.start()
    for copy in copies:
        copy.wait()


def slots_kernel(cap, state_hbm, owners_hbm, orient_hbm, tile_ref, put_ref, take_ref, flip_ref, own_ref, turn_ref, sems):
    per_tile = owners_hbm.shape[1]
    n_slots = put_ref.shape[0]
    copies = [
        pltpu.make_async_copy(owners_hbm, own_ref, sems.at[0]),
        pltpu.make_async_copy(orient_hbm, turn_ref, sems.at[1]),
        pltpu.make_async_copy(state_hbm, tile_ref, sems.at[2]),
    ]
    for copy in copies:
        copy.start()
    row = lax.broadcasted_iota(jnp.int32, (per_tile, per_tile), 0)
    col = lax.broadcasted_iota(jnp.int32, (per_tile, per_tile), 1)
    q_down = lax.broadcasted_iota(jnp.int32, (n_slots, per_tile), 0)
    q_across = lax.broadcasted_iota(jnp.int32, (per_tile, n_slots), 1)
    copies[0].wait()
    across = jnp.broadcast_to(own_ref[...], (per_tile, per_tile))
    down = across.T
    same = down == across
    before_col = jnp.where(same & (row < col), 1.0, 0.0)
    before_row = jnp.where(same & (col < row), 1.0, 0.0)
    rank_across = jnp.sum(before_col, axis=0, keepdims=True).astype(jnp.int32)
    rank_down = jnp.sum(before_row, axis=1, keepdims=True).astype(jnp.int32)
    slot_across = across[0:1, :] * cap + rank_across
    slot_down = down[:, 0:1] * cap + rank_down
    put_ref[...] = jnp.where(q_down == slot_across, 1.0, 0.0).astype(jnp.bfloat16)
    take_ref[...] = jnp.where(q_across == slot_down, 1.0, 0.0).astype(jnp.bfloat16)
    copies[1].wait()
    for k in range(2):
        flip_ref[k] = jnp.broadcast_to(turn_ref[0:1, k : k + 1], (TW, LANES))
    copies[2].wait()


def edge_kernel(tile_ref, outer_ref, inner_ref, flip_ref, put_ref, moved_ref, out_ref):
    per_tile, width = tile_ref.shape

    odd = odd_strip() == 1

    def turned(value, k):
        back = jnp.concatenate([value[TW - 1 - w : TW - w] for w in range(TW)], axis=0)
        flip = jnp.concatenate([flip_ref[k]] * (width // LANES), axis=1)
        return jnp.where(flip == 1, back, value)

    outer, inner = outer_ref[...], inner_ref[...]
    low = turned(jnp.where(odd, inner, outer), 0)
    high = turned(jnp.where(odd, outer, inner), 1)
    tiles = tile_ref[...]
    below = jnp.concatenate([low, tiles[: per_tile - TW]], axis=0)
    above = jnp.concatenate([tiles[TW:], high], axis=0)
    moved = tiles + kappa_edge * ((above + below) - 2.0 * tiles)
    out_ref[...] = split_dot(put_ref[...], moved[:, : 2 * L])
    moved_ref[...] = moved


def rows_from_levels(flipped):
    n = 2 * SUB * TZ
    a = lax.broadcasted_iota(jnp.int32, (n, n), 1 if flipped else 0)
    b = lax.broadcasted_iota(jnp.int32, (n, n), 0 if flipped else 1)
    z, p, s = a >> 4, (a >> 3) & 1, a & 7
    return jnp.where(b == p * (SUB * TZ) + s * TZ + z, 1.0, 0.0).astype(jnp.bfloat16)


def prepare_kernel(
    crm_hbm, active_hbm, diff_hbm, vm_hbm, f_ref, mean_ref, sq_ref, coef_ref, wa_ref, wb_ref, crm_ref, act_ref, diff_ref, vm_ref, sems
):
    slots = active_hbm.shape[1]
    copies = [
        pltpu.make_async_copy(active_hbm, act_ref, sems.at[0]),
        pltpu.make_async_copy(diff_hbm, diff_ref, sems.at[1]),
        pltpu.make_async_copy(vm_hbm, vm_ref, sems.at[2]),
        pltpu.make_async_copy(crm_hbm, crm_ref, sems.at[3]),
    ]
    for copy in copies:
        copy.start()
    order = rows_from_levels(False)
    coef_ref[...] = jnp.zeros_like(coef_ref)
    copies[0].wait()
    copies[1].wait()
    active = act_ref[...]
    nothing = jnp.zeros((1, slots), jnp.float32)

    def link(i):
        if i < 0 or i >= CZ - 1:
            return nothing
        return jnp.where(i + 1 < active, diff_ref[i], 0.0)

    up, down = nothing, nothing
    for z in range(CZ):
        lower, upper = link(z - 1), link(z)
        up = 1.0 / (1.0 + lower + upper - lower * (lower * up))
        coef_ref[0, z : z + 1, :] = up
        coef_ref[1, z : z + 1, :] = lower * up
        coef_ref[2, z : z + 1, :] = upper * up
        y = CZ - 1 - z
        lower, upper = link(y - 1), link(y)
        down = 1.0 / (1.0 + lower + upper - upper * (upper * down))
        coef_ref[3, y : y + 1, :] = down
        coef_ref[4, y : y + 1, :] = upper * down
        coef_ref[5, y : y + 1, :] = lower * down
    copies[2].wait()
    pad = jnp.zeros((CZ, L), jnp.float32)
    rest = jnp.zeros((ZP - CZ, 2 * L), jnp.float32)
    both = [jnp.concatenate([vm_ref[...], pad], axis=1), rest, jnp.concatenate([pad, vm_ref[...]], axis=1), rest]
    high, low = parts_of(jnp.concatenate(both, axis=0))
    wa_ref[...] = jnp.concatenate([high, low, high], axis=1)
    wb_ref[...] = jnp.concatenate([high, high, low], axis=0)

    copies[3].wait()
    for t in range(ZP // TZ):
        rows = min(TZ, CZ - t * TZ)
        total = jnp.zeros((TZ, slots), jnp.float32)
        square = jnp.zeros((TZ, slots), jnp.float32)
        for p in range(NI // 2):
            parts = []
            for i in (2 * p, 2 * p + 1):
                for s in range(SUB):
                    x = s * NI + i
                    v = crm_ref[t * TZ : t * TZ + rows, x * slots : (x + 1) * slots]
                    wide = v.astype(jnp.float32)
                    if rows < TZ:
                        wide = jnp.concatenate([wide, jnp.zeros((TZ - rows, slots), jnp.float32)], axis=0)
                        v = wide.astype(jnp.bfloat16)
                    total = total + wide
                    square = square + wide * wide
                    parts.append(v)
            turned = lax.dot_general(
                order, jnp.concatenate(parts, axis=0), (((1,), (0,)), ((), ())), preferred_element_type=jnp.float32
            ).astype(jnp.bfloat16)
            for z in range(rows):
                base = (t * TZ + z) * CX + p * 2 * SUB
                f_ref[base : base + 2 * SUB, :] = turned[z * 2 * SUB : (z + 1) * 2 * SUB]
        mean_ref[t * TZ : (t + 1) * TZ, :] = total * (1.0 / CX)
        sq_ref[t * TZ : (t + 1) * TZ, :] = square * (1.0 / CX)


def physics_kernel(
    cols_ref, f_ref, mean_ref, sq_ref, coef_ref, wa_ref, wb_ref, tend_ref, y_ref, g_ref, adv_ref, sum_ref
):
    slots = cols_ref.shape[0]
    halves = slots // LANES
    for h in range(halves):
        lane = slice(h * LANES, (h + 1) * LANES)
        high, low = parts_of(cols_ref[lane, :])
        mapped = lax.dot_general(
            wa_ref[...],
            jnp.concatenate([high, high, low], axis=1),
            (((1,), (1,)), ((), ())),
            preferred_element_type=jnp.float32,
        )
        forcing = mapped[0:ZP]
        courant = max_courant * jax.nn.sigmoid(mapped[ZP:])
        inv1 = coef_ref[0, :, lane]
        inv2 = coef_ref[3, :, lane]
        adv_ref[0, :, lane] = inv1 * (1.0 - courant)
        adv_ref[1, :, lane] = inv1 * courant
        adv_ref[2, :, lane] = inv2 * (1.0 - courant)
        adv_ref[3, :, lane] = inv2 * courant
        adv_ref[4, :, lane] = inv1 * (relax_rate * (forcing - mean_ref[:, lane]))
    sum_ref[:, CZ:, :] = jnp.zeros((2, ZP - CZ, slots), jnp.float32)

    def spread(ref, k, z, lane):
        return jnp.broadcast_to(ref[k, z : z + 1, lane], (SUB, LANES))

    for h in range(halves):
        lane = slice(h * LANES, (h + 1) * LANES)

        def at(z, i, n=1):
            base = z * CX + i * SUB
            return slice(base, base + n * SUB)

        zero = jnp.zeros((SUB, LANES), jnp.float32)
        prev = [zero] * NI
        for z in range(CZ):
            a, b = spread(adv_ref, 0, z, lane), spread(adv_ref, 1, z, lane)
            d, e = spread(adv_ref, 4, z, lane), spread(coef_ref, 1, z, lane)
            f = []
            for i in range(0, NI, 2):
                pair = f_ref[at(z, i, 2), lane].astype(jnp.float32)
                f += [pair[:SUB], pair[SUB:]]
            behind = [pltpu.roll(f[NI - 1], 1, axis=0)] + f[: NI - 1]
            prev = [((a * f[i] + d) + b * behind[i]) + e * prev[i] for i in range(NI)]
            for i in range(NI):
                g_ref[at(z, i), lane] = prev[i]
        after = [zero] * NI
        prev = [zero] * NI
        for z in range(CZ - 1, -1, -1):
            g = spread(coef_ref, 2, z, lane)
            a, b = spread(adv_ref, 2, z, lane), spread(adv_ref, 3, z, lane)
            e = spread(coef_ref, 4, z, lane)
            after = [g_ref[at(z, i), lane] + g * after[i] for i in range(NI)]
            behind = [pltpu.roll(after[NI - 1], 1, axis=0)] + after[: NI - 1]
            prev = [(a * after[i] + b * behind[i]) + e * prev[i] for i in range(NI)]
            for i in range(NI):
                g_ref[at(z, i), lane] = prev[i]
        after = [zero] * NI
        for z in range(CZ):
            g = spread(coef_ref, 5, z, lane)
            after = [g_ref[at(z, i), lane] + g * after[i] for i in range(NI)]
            total = [after[i] + after[i + 1] for i in range(0, NI, 2)]
            square = [after[i] * after[i] + after[i + 1] * after[i + 1] for i in range(0, NI, 2)]
            for i in range(0, NI, 2):
                y_ref[at(z, i, 2), lane] = jnp.concatenate(after[i : i + 2], axis=0).astype(jnp.bfloat16)
            sum_ref[0, z : z + 1, lane] = jnp.sum((total[0] + total[1]) + (total[2] + total[3]), axis=0, keepdims=True)
            sum_ref[1, z : z + 1, lane] = jnp.sum((square[0] + square[1]) + (square[2] + square[3]), axis=0, keepdims=True)
        mean0, sq0 = mean_ref[:, lane], sq_ref[:, lane]
        mean1, sq1 = sum_ref[0, :, lane] * (1.0 / CX), sum_ref[1, :, lane] * (1.0 / CX)
        change = jnp.concatenate([mean1 - mean0, (sq1 - mean1 * mean1) - (sq0 - mean0 * mean0)], axis=0)
        high, low = parts_of(change)
        tend_ref[lane, :] = lax.dot_general(
            jnp.concatenate([high, low, high], axis=0),
            wb_ref[...],
            (((0,), (0,)), ((), ())),
            preferred_element_type=jnp.float32,
        )


def store_kernel(y_ref, crm_hbm, crm_ref, sems):
    slots = crm_hbm.shape[1] // CX
    order = rows_from_levels(True)
    copies = []
    for p in range(NI // 2):
        for t in range(ZP // TZ):
            rows = min(TZ, CZ - t * TZ)
            parts = [y_ref[(t * TZ + z) * CX + p * 2 * SUB : (t * TZ + z) * CX + (p + 1) * 2 * SUB, :] for z in range(rows)]
            if rows < TZ:
                parts.append(jnp.zeros(((TZ - rows) * 2 * SUB, slots), jnp.bfloat16))
            turned = lax.dot_general(
                order, jnp.concatenate(parts, axis=0), (((1,), (0,)), ((), ())), preferred_element_type=jnp.float32
            ).astype(jnp.bfloat16)
            for i in range(2):
                for s in range(SUB):
                    x = s * NI + 2 * p + i
                    k = (i * SUB + s) * TZ
                    crm_ref[t * TZ : t * TZ + rows, x * slots : (x + 1) * slots] = turned[k : k + rows]
        for s in range(SUB):
            here = pl.ds((s * NI + 2 * p) * slots, 2 * slots)
            copy = pltpu.make_async_copy(crm_ref.at[:, here], crm_hbm.at[:, here], sems.at[p * SUB + s])
            copy.start()
            copies.append(copy)
    for copy in copies:
        copy.wait()


def finish_kernel(moved_ref, take_ref, back_ref, out_hbm, part_ref, sems):
    rest = pltpu.make_async_copy(moved_ref.at[:, 2 * L :], out_hbm.at[:, 2 * L :], sems.at[0])
    rest.start()
    part_ref[...] = moved_ref[:, : 2 * L] + split_dot(take_ref[...], back_ref[...])
    first = pltpu.make_async_copy(part_ref, out_hbm.at[:, : 2 * L], sems.at[1])
    first.start()
    rest.wait()
    first.wait()


def cost(us):
    return pl.CostEstimate(flops=0, bytes_accessed=int(us * 3.0e6), transcendentals=0)


def far(x):
    return pltpu.with_memory_space_constraint(x, pltpu.HBM)


def shards(state, owners, orient, crm_state, active_levels, vertical_map, diffusion):
    f32, bf16 = jnp.float32, jnp.bfloat16
    n_tiles = lax.axis_size("cols")
    per_tile = state.shape[1]
    width = state.shape[2]
    cap_slots = max(2, 2 * per_tile // n_tiles)
    slots = n_tiles * cap_slots
    rows_f = CZ * CX
    hbm = pl.BlockSpec(memory_space=pltpu.HBM)
    dma = pltpu.SemaphoreType.DMA
    tile = state[0]
    outer, inner = call(
        rows_kernel,
        (pltpu.VMEM((TW, width), f32), pltpu.VMEM((TW, width), f32)),
        (far(tile),),
        in_specs=[hbm],
        scratch=(dma((2,)),),
        cost=cost(0.5),
    )
    outer = swap(outer, "edge", 1)
    inner = swap(inner, "edge", 0)
    near, put, take, flip = call(
        functools.partial(slots_kernel, cap_slots),
        (
            pltpu.VMEM((per_tile, width), f32),
            pltpu.VMEM((slots, per_tile), bf16),
            pltpu.VMEM((per_tile, slots), bf16),
            pltpu.VMEM((2, TW, LANES), jnp.int32),
        ),
        (far(tile), far(owners.reshape(1, per_tile)), far(orient[0])),
        in_specs=[hbm] * 3,
        scratch=(pltpu.VMEM((1, per_tile), jnp.int32), pltpu.VMEM((1, 2), jnp.int32), dma((3,))),
        cost=cost(1),
    )
    moved, outgoing = call(
        edge_kernel,
        (pltpu.VMEM((per_tile, width), f32), jax.ShapeDtypeStruct((slots, 2 * L), f32)),
        (near, outer, inner, flip, put),
        cost=cost(1),
    )
    received = lax.all_to_all(
        outgoing.reshape(n_tiles, cap_slots, 2 * L), "cols", split_axis=0, concat_axis=0, tiled=True
    ).reshape(slots, 2 * L)
    prepared = call(
        prepare_kernel,
        (
            pltpu.VMEM((rows_f, slots), bf16),
            pltpu.VMEM((ZP, slots), f32),
            pltpu.VMEM((ZP, slots), f32),
            pltpu.VMEM((6, ZP, slots), f32),
            pltpu.VMEM((2 * ZP, 6 * L), bf16),
            pltpu.VMEM((6 * ZP, 2 * L), bf16),
        ),
        (far(crm_state[0, 0]), far(active_levels[0]), far(diffusion), far(vertical_map)),
        in_specs=[hbm] * 4,
        scratch=(
            pltpu.VMEM((CZ, CX * slots), bf16),
            pltpu.VMEM((1, slots), jnp.int32),
            pltpu.SMEM((CZ - 1,), f32),
            pltpu.VMEM((CZ, L), f32),
            dma((4,)),
        ),
        cost=cost(4),
    )
    tend, after = call(
        physics_kernel,
        (jax.ShapeDtypeStruct((slots, 2 * L), f32), pltpu.VMEM((rows_f, slots), bf16)),
        (received, *prepared),
        scratch=(
            pltpu.VMEM((rows_f, slots), f32),
            pltpu.VMEM((5, ZP, slots), f32),
            pltpu.VMEM((2, ZP, slots), f32),
        ),
        aliases={1: 1},
        cost=cost(5),
    )
    returned = lax.all_to_all(
        tend.reshape(n_tiles, cap_slots, 2 * L), "cols", split_axis=0, concat_axis=0, tiled=True
    ).reshape(slots, 2 * L)
    crm_new = call(
        store_kernel,
        jax.ShapeDtypeStruct((CZ, CX * slots), bf16),
        (after,),
        scratch=(pltpu.VMEM((CZ, CX * slots), bf16), dma((NI // 2 * SUB,))),
        out_specs=hbm,
        cost=cost(3),
    )
    new_state = call(
        finish_kernel,
        jax.ShapeDtypeStruct((per_tile, width), f32),
        (moved, take, returned),
        scratch=(pltpu.VMEM((per_tile, 2 * L), f32), dma((2,))),
        out_specs=hbm,
        cost=cost(0.7),
    )
    return (new_state[None], crm_new[None, None])


def solution(mesh):
    in_specs = (
        P("edge", "cols", None),
        P("edge", "cols", None),
        P("edge", "cols", None),
        P("edge", "cols", None, None),
        P("edge", "cols", None),
        P(),
        P(),
    )
    out_specs = (P("edge", "cols", None), P("edge", "cols", None, None))
    return jax.shard_map(shards, mesh=mesh, in_specs=in_specs, out_specs=out_specs, check_vma=False)
```

```python
import functools

import jax
import jax.numpy as jnp
from jax import lax
from jax.experimental import pallas as pl
from jax.experimental.pallas import tpu as pltpu
from jax.sharding import PartitionSpec as P

L = 64
CX = 64
CZ = 58
TW = 8
SUBSTEPS = 2
ZP = 64
LANES = 128
SUB = 8
NI = CX // SUB
STAGED = 8
TZ = 16

kappa_edge = 0.25
max_courant = 0.9
relax_rate = 0.5


def call(body, outs, args, scratch=(), in_specs=None, out_specs=None, cost=None, limit=32 << 20, aliases=None):
    kw = {}
    if out_specs is not None:
        kw["out_specs"] = out_specs
    if in_specs is not None:
        kw["in_specs"] = in_specs
    return pl.pallas_call(
        body,
        out_shape=outs,
        scratch_shapes=list(scratch),
        compiler_params=pltpu.CompilerParams(vmem_limit_bytes=limit),
        cost_estimate=cost,
        input_output_aliases=aliases or {},
        **kw,
    )(*args)


def swap(value, axis, first):
    count = lax.axis_size(axis)
    pairs = []
    for one in range(first, count, 2):
        other = (one + 1) % count
        pairs += [(one, other), (other, one)]
    return lax.ppermute(value, axis, pairs)


def pair_kernel(own_ref, got_ref, *pair_refs):
    rows = pair_refs[0].shape[0] // 2
    for k, ref in enumerate(pair_refs):
        here = slice((k + 1) * rows, (k + 2) * rows)
        ref[:rows, :] = own_ref[here, :]
        ref[rows:, :] = got_ref[here, :]


def exchange(sent):
    count = lax.axis_size("cols")
    if len(sent) == 1:
        whole = sent[0].reshape(count, -1, sent[0].shape[1])
        return [lax.all_to_all(whole, "cols", split_axis=0, concat_axis=0, tiled=True).reshape(sent[0].shape)]

    def trade(value, k):
        return lax.ppermute(value, "cols", [(c, c ^ k) for c in range(count)])

    own, other = sent
    got = trade(other, 1)
    far_ones = count // 2 - 1
    pairs = call(
        pair_kernel,
        tuple(pltpu.VMEM((2 * own.shape[0] // (count // 2), own.shape[1]), jnp.float32) for _ in range(far_ones)),
        (own, got),
        cost=cost(0.2),
    )
    return [own, got, *[trade(pair, 2 * (k + 1)) for k, pair in enumerate(pairs)]]


def arrived(refs, rows):
    out = [(0, refs[0][:rows, :]), (1, refs[1][:rows, :])]
    for k, ref in enumerate(refs[2:]):
        out += [(2 * (k + 1), ref[:rows, :]), (2 * (k + 1) + 1, ref[rows:, :])]
    return out


def tile_rows(distance, rows):
    return pl.ds(pl.multiple_of((lax.axis_index("cols") ^ distance) * rows, SUB), rows)


def odd_strip():
    return lax.rem(lax.axis_index("edge"), 2)


def split_dot(chosen, value):
    high, low = parts_of(value)
    pick = lambda part: lax.dot_general(chosen, part, (((1,), (0,)), ((), ())), preferred_element_type=jnp.float32)
    return pick(high) + pick(low)


def parts_of(value):
    high = value.astype(jnp.bfloat16)
    return high, (value - high.astype(jnp.float32)).astype(jnp.bfloat16)


def rows_kernel(state_hbm, outer_ref, inner_ref, sems):
    last = state_hbm.shape[0] - TW
    outer = pl.multiple_of(odd_strip() * last, TW)
    inner = pl.multiple_of((1 - odd_strip()) * last, TW)
    copies = [
        pltpu.make_async_copy(state_hbm.at[pl.ds(outer, TW)], outer_ref, sems.at[0]),
        pltpu.make_async_copy(state_hbm.at[pl.ds(inner, TW)], inner_ref, sems.at[1]),
    ]
    for copy in copies:
        copy.start()
    for copy in copies:
        copy.wait()


def slots_kernel(cap, staged, state_hbm, owners_hbm, orient_hbm, tile_ref, put_ref, take_ref, flip_ref, own_ref, turn_ref, sems):
    per_tile = owners_hbm.shape[1]
    n_slots = put_ref.shape[0]
    copies = [
        pltpu.make_async_copy(owners_hbm, own_ref, sems.at[0]),
        pltpu.make_async_copy(orient_hbm, turn_ref, sems.at[1]),
        pltpu.make_async_copy(state_hbm, tile_ref, sems.at[2]),
    ]
    for copy in copies:
        copy.start()
    row = lax.broadcasted_iota(jnp.int32, (per_tile, per_tile), 0)
    col = lax.broadcasted_iota(jnp.int32, (per_tile, per_tile), 1)
    q_down = lax.broadcasted_iota(jnp.int32, (n_slots, per_tile), 0)
    q_across = lax.broadcasted_iota(jnp.int32, (per_tile, n_slots), 1)
    copies[0].wait()
    named = own_ref[...]
    if staged:
        named = named ^ lax.axis_index("cols")
        named = (named & 1) * (staged // 2) + (named >> 1)
    across = jnp.broadcast_to(named, (per_tile, per_tile))
    down = across.T
    same = down == across
    before_col = jnp.where(same & (row < col), 1.0, 0.0)
    before_row = jnp.where(same & (col < row), 1.0, 0.0)
    rank_across = jnp.sum(before_col, axis=0, keepdims=True).astype(jnp.int32)
    rank_down = jnp.sum(before_row, axis=1, keepdims=True).astype(jnp.int32)
    slot_across = across[0:1, :] * cap + rank_across
    slot_down = down[:, 0:1] * cap + rank_down
    put_ref[...] = jnp.where(q_down == slot_across, 1.0, 0.0).astype(jnp.bfloat16)
    take_ref[...] = jnp.where(q_across == slot_down, 1.0, 0.0).astype(jnp.bfloat16)
    copies[1].wait()
    for k in range(2):
        flip_ref[k] = jnp.broadcast_to(turn_ref[0:1, k : k + 1], (TW, LANES))
    copies[2].wait()


def edge_kernel(tile_ref, outer_ref, inner_ref, flip_ref, put_ref, moved_ref, *out_refs):
    per_tile, width = tile_ref.shape

    odd = odd_strip() == 1

    def turned(value, k):
        back = jnp.concatenate([value[TW - 1 - w : TW - w] for w in range(TW)], axis=0)
        flip = jnp.concatenate([flip_ref[k]] * (width // LANES), axis=1)
        return jnp.where(flip == 1, back, value)

    outer, inner = outer_ref[...], inner_ref[...]
    low = turned(jnp.where(odd, inner, outer), 0)
    high = turned(jnp.where(odd, outer, inner), 1)
    tiles = tile_ref[...]
    below = jnp.concatenate([low, tiles[: per_tile - TW]], axis=0)
    above = jnp.concatenate([tiles[TW:], high], axis=0)
    moved = tiles + kappa_edge * ((above + below) - 2.0 * tiles)
    picked = split_dot(put_ref[...], moved[:, : 2 * L])
    for k, ref in enumerate(out_refs):
        rows = ref.shape[0]
        ref[...] = picked[k * rows : (k + 1) * rows]
    moved_ref[...] = moved


def rows_from_levels(flipped):
    n = 2 * SUB * TZ
    a = lax.broadcasted_iota(jnp.int32, (n, n), 1 if flipped else 0)
    b = lax.broadcasted_iota(jnp.int32, (n, n), 0 if flipped else 1)
    z, p, s = a >> 4, (a >> 3) & 1, a & 7
    return jnp.where(b == p * (SUB * TZ) + s * TZ + z, 1.0, 0.0).astype(jnp.bfloat16)


def prepare_kernel(
    crm_hbm, active_hbm, diff_hbm, vm_hbm, f_ref, mean_ref, sq_ref, coef_ref, wa_ref, wb_ref, crm_ref, act_ref, diff_ref, vm_ref, sems
):
    slots = active_hbm.shape[1]
    copies = [
        pltpu.make_async_copy(active_hbm, act_ref, sems.at[0]),
        pltpu.make_async_copy(diff_hbm, diff_ref, sems.at[1]),
        pltpu.make_async_copy(vm_hbm, vm_ref, sems.at[2]),
        pltpu.make_async_copy(crm_hbm, crm_ref, sems.at[3]),
    ]
    for copy in copies:
        copy.start()
    order = rows_from_levels(False)
    coef_ref[...] = jnp.zeros_like(coef_ref)
    copies[0].wait()
    copies[1].wait()
    active = act_ref[...]
    nothing = jnp.zeros((1, slots), jnp.float32)

    def link(i):
        if i < 0 or i >= CZ - 1:
            return nothing
        return jnp.where(i + 1 < active, diff_ref[i], 0.0)

    up, down = nothing, nothing
    for z in range(CZ):
        lower, upper = link(z - 1), link(z)
        up = 1.0 / (1.0 + lower + upper - lower * (lower * up))
        coef_ref[0, z : z + 1, :] = up
        coef_ref[1, z : z + 1, :] = lower * up
        coef_ref[2, z : z + 1, :] = upper * up
        y = CZ - 1 - z
        lower, upper = link(y - 1), link(y)
        down = 1.0 / (1.0 + lower + upper - upper * (upper * down))
        coef_ref[3, y : y + 1, :] = down
        coef_ref[4, y : y + 1, :] = upper * down
        coef_ref[5, y : y + 1, :] = lower * down
    copies[2].wait()
    pad = jnp.zeros((CZ, L), jnp.float32)
    rest = jnp.zeros((ZP - CZ, 2 * L), jnp.float32)
    both = [jnp.concatenate([vm_ref[...], pad], axis=1), rest, jnp.concatenate([pad, vm_ref[...]], axis=1), rest]
    high, low = parts_of(jnp.concatenate(both, axis=0))
    wa_ref[...] = jnp.concatenate([high, low, high], axis=1)
    wb_ref[...] = jnp.concatenate([high, high, low], axis=0)

    copies[3].wait()
    for t in range(ZP // TZ):
        rows = min(TZ, CZ - t * TZ)
        total = jnp.zeros((TZ, slots), jnp.float32)
        square = jnp.zeros((TZ, slots), jnp.float32)
        for p in range(NI // 2):
            parts = []
            for i in (2 * p, 2 * p + 1):
                for s in range(SUB):
                    x = s * NI + i
                    v = crm_ref[t * TZ : t * TZ + rows, x * slots : (x + 1) * slots]
                    wide = v.astype(jnp.float32)
                    if rows < TZ:
                        wide = jnp.concatenate([wide, jnp.zeros((TZ - rows, slots), jnp.float32)], axis=0)
                        v = wide.astype(jnp.bfloat16)
                    total = total + wide
                    square = square + wide * wide
                    parts.append(v)
            turned = lax.dot_general(
                order, jnp.concatenate(parts, axis=0), (((1,), (0,)), ((), ())), preferred_element_type=jnp.float32
            ).astype(jnp.bfloat16)
            for z in range(rows):
                base = (t * TZ + z) * CX + p * 2 * SUB
                f_ref[base : base + 2 * SUB, :] = turned[z * 2 * SUB : (z + 1) * 2 * SUB]
        mean_ref[t * TZ : (t + 1) * TZ, :] = total * (1.0 / CX)
        sq_ref[t * TZ : (t + 1) * TZ, :] = square * (1.0 / CX)


def physics_kernel(staged, *refs):
    n_in = staged // 2 + 1 if staged else 1
    sent_refs, refs = refs[:n_in], refs[n_in:]
    f_ref, mean_ref, sq_ref, coef_ref, wa_ref, wb_ref, y_ref = refs[:7]
    back_refs = refs[7:-5]
    g_ref, adv_ref, sum_ref, cols_ref, tend_ref = refs[-5:]
    slots = cols_ref.shape[0]
    if staged:
        rows = slots // staged
        for distance, value in arrived(sent_refs, rows):
            cols_ref[tile_rows(distance, rows), :] = value
    else:
        cols_ref[...] = sent_refs[0][...]
    halves = slots // LANES
    for h in range(halves):
        lane = slice(h * LANES, (h + 1) * LANES)
        high, low = parts_of(cols_ref[lane, :])
        mapped = lax.dot_general(
            wa_ref[...],
            jnp.concatenate([high, high, low], axis=1),
            (((1,), (1,)), ((), ())),
            preferred_element_type=jnp.float32,
        )
        forcing = mapped[0:ZP]
        courant = max_courant * jax.nn.sigmoid(mapped[ZP:])
        inv1 = coef_ref[0, :, lane]
        inv2 = coef_ref[3, :, lane]
        adv_ref[0, :, lane] = inv1 * (1.0 - courant)
        adv_ref[1, :, lane] = inv1 * courant
        adv_ref[2, :, lane] = inv2 * (1.0 - courant)
        adv_ref[3, :, lane] = inv2 * courant
        adv_ref[4, :, lane] = inv1 * (relax_rate * (forcing - mean_ref[:, lane]))
    sum_ref[:, CZ:, :] = jnp.zeros((2, ZP - CZ, slots), jnp.float32)

    def spread(ref, k, z, lane):
        return jnp.broadcast_to(ref[k, z : z + 1, lane], (SUB, LANES))

    for h in range(halves):
        lane = slice(h * LANES, (h + 1) * LANES)

        def at(z, i, n=1):
            base = z * CX + i * SUB
            return slice(base, base + n * SUB)

        zero = jnp.zeros((SUB, LANES), jnp.float32)
        prev = [zero] * NI
        for z in range(CZ):
            a, b = spread(adv_ref, 0, z, lane), spread(adv_ref, 1, z, lane)
            d, e = spread(adv_ref, 4, z, lane), spread(coef_ref, 1, z, lane)
            f = []
            for i in range(0, NI, 2):
                pair = f_ref[at(z, i, 2), lane].astype(jnp.float32)
                f += [pair[:SUB], pair[SUB:]]
            behind = [pltpu.roll(f[NI - 1], 1, axis=0)] + f[: NI - 1]
            prev = [((a * f[i] + d) + b * behind[i]) + e * prev[i] for i in range(NI)]
            for i in range(NI):
                g_ref[at(z, i), lane] = prev[i]
        after = [zero] * NI
        prev = [zero] * NI
        for z in range(CZ - 1, -1, -1):
            g = spread(coef_ref, 2, z, lane)
            a, b = spread(adv_ref, 2, z, lane), spread(adv_ref, 3, z, lane)
            e = spread(coef_ref, 4, z, lane)
            after = [g_ref[at(z, i), lane] + g * after[i] for i in range(NI)]
            behind = [pltpu.roll(after[NI - 1], 1, axis=0)] + after[: NI - 1]
            prev = [(a * after[i] + b * behind[i]) + e * prev[i] for i in range(NI)]
            for i in range(NI):
                g_ref[at(z, i), lane] = prev[i]
        after = [zero] * NI
        for z in range(CZ):
            g = spread(coef_ref, 5, z, lane)
            after = [g_ref[at(z, i), lane] + g * after[i] for i in range(NI)]
            total = [after[i] + after[i + 1] for i in range(0, NI, 2)]
            square = [after[i] * after[i] + after[i + 1] * after[i + 1] for i in range(0, NI, 2)]
            for i in range(0, NI, 2):
                y_ref[at(z, i, 2), lane] = jnp.concatenate(after[i : i + 2], axis=0).astype(jnp.bfloat16)
            sum_ref[0, z : z + 1, lane] = jnp.sum((total[0] + total[1]) + (total[2] + total[3]), axis=0, keepdims=True)
            sum_ref[1, z : z + 1, lane] = jnp.sum((square[0] + square[1]) + (square[2] + square[3]), axis=0, keepdims=True)
        mean0, sq0 = mean_ref[:, lane], sq_ref[:, lane]
        mean1, sq1 = sum_ref[0, :, lane] * (1.0 / CX), sum_ref[1, :, lane] * (1.0 / CX)
        change = jnp.concatenate([mean1 - mean0, (sq1 - mean1 * mean1) - (sq0 - mean0 * mean0)], axis=0)
        high, low = parts_of(change)
        tend_ref[lane, :] = lax.dot_general(
            jnp.concatenate([high, low, high], axis=0),
            wb_ref[...],
            (((0,), (0,)), ((), ())),
            preferred_element_type=jnp.float32,
        )
    if staged:
        for distance in range(staged):
            place = distance // 2 * rows
            back_refs[distance % 2][place : place + rows, :] = tend_ref[tile_rows(distance, rows), :]
    else:
        back_refs[0][...] = tend_ref[...]


def store_kernel(y_ref, crm_hbm, crm_ref, sems):
    slots = crm_hbm.shape[1] // CX
    order = rows_from_levels(True)
    copies = []
    for p in range(NI // 2):
        for t in range(ZP // TZ):
            rows = min(TZ, CZ - t * TZ)
            parts = [y_ref[(t * TZ + z) * CX + p * 2 * SUB : (t * TZ + z) * CX + (p + 1) * 2 * SUB, :] for z in range(rows)]
            if rows < TZ:
                parts.append(jnp.zeros(((TZ - rows) * 2 * SUB, slots), jnp.bfloat16))
            turned = lax.dot_general(
                order, jnp.concatenate(parts, axis=0), (((1,), (0,)), ((), ())), preferred_element_type=jnp.float32
            ).astype(jnp.bfloat16)
            for i in range(2):
                for s in range(SUB):
                    x = s * NI + 2 * p + i
                    k = (i * SUB + s) * TZ
                    crm_ref[t * TZ : t * TZ + rows, x * slots : (x + 1) * slots] = turned[k : k + rows]
        for s in range(SUB):
            here = pl.ds((s * NI + 2 * p) * slots, 2 * slots)
            copy = pltpu.make_async_copy(crm_ref.at[:, here], crm_hbm.at[:, here], sems.at[p * SUB + s])
            copy.start()
            copies.append(copy)
    for copy in copies:
        copy.wait()


def finish_kernel(staged, moved_ref, take_ref, *refs):
    back_refs = refs[:-3]
    out_hbm, part_ref, sems = refs[-3:]
    rest = pltpu.make_async_copy(moved_ref.at[:, 2 * L :], out_hbm.at[:, 2 * L :], sems.at[0])
    rest.start()
    if staged:
        parts = arrived(back_refs, take_ref.shape[1] // staged)
        back = jnp.concatenate([part for _, part in parts[0::2] + parts[1::2]], axis=0)
    else:
        back = back_refs[0][...]
    part_ref[...] = moved_ref[:, : 2 * L] + split_dot(take_ref[...], back)
    first = pltpu.make_async_copy(part_ref, out_hbm.at[:, : 2 * L], sems.at[1])
    first.start()
    rest.wait()
    first.wait()


def cost(us):
    return pl.CostEstimate(flops=0, bytes_accessed=int(us * 3.0e6), transcendentals=0)


def far(x):
    return pltpu.with_memory_space_constraint(x, pltpu.HBM)


def shards(state, owners, orient, crm_state, active_levels, vertical_map, diffusion):
    f32, bf16 = jnp.float32, jnp.bfloat16
    n_tiles = lax.axis_size("cols")
    per_tile = state.shape[1]
    width = state.shape[2]
    cap_slots = max(2, 2 * per_tile // n_tiles)
    slots = n_tiles * cap_slots
    rows_f = CZ * CX
    staged = n_tiles if n_tiles == STAGED else 0
    if staged:
        sent = (pltpu.VMEM((slots // 2, 2 * L), f32),) * 2
    else:
        sent = (jax.ShapeDtypeStruct((slots, 2 * L), f32),)
    hbm = pl.BlockSpec(memory_space=pltpu.HBM)
    dma = pltpu.SemaphoreType.DMA
    tile = state[0]
    outer, inner = call(
        rows_kernel,
        (pltpu.VMEM((TW, width), f32), pltpu.VMEM((TW, width), f32)),
        (far(tile),),
        in_specs=[hbm],
        scratch=(dma((2,)),),
        cost=cost(0.5),
    )
    outer = swap(outer, "edge", 1)
    inner = swap(inner, "edge", 0)
    near, put, take, flip = call(
        functools.partial(slots_kernel, cap_slots, staged),
        (
            pltpu.VMEM((per_tile, width), f32),
            pltpu.VMEM((slots, per_tile), bf16),
            pltpu.VMEM((per_tile, slots), bf16),
            pltpu.VMEM((2, TW, LANES), jnp.int32),
        ),
        (far(tile), far(owners.reshape(1, per_tile)), far(orient[0])),
        in_specs=[hbm] * 3,
        scratch=(pltpu.VMEM((1, per_tile), jnp.int32), pltpu.VMEM((1, 2), jnp.int32), dma((3,))),
        cost=cost(1),
    )
    moved, *outgoing = call(
        edge_kernel,
        (pltpu.VMEM((per_tile, width), f32), *sent),
        (near, outer, inner, flip, put),
        cost=cost(1),
    )
    received = exchange(outgoing)
    prepared = call(
        prepare_kernel,
        (
            pltpu.VMEM((rows_f, slots), bf16),
            pltpu.VMEM((ZP, slots), f32),
            pltpu.VMEM((ZP, slots), f32),
            pltpu.VMEM((6, ZP, slots), f32),
            pltpu.VMEM((2 * ZP, 6 * L), bf16),
            pltpu.VMEM((6 * ZP, 2 * L), bf16),
        ),
        (far(crm_state[0, 0]), far(active_levels[0]), far(diffusion), far(vertical_map)),
        in_specs=[hbm] * 4,
        scratch=(
            pltpu.VMEM((CZ, CX * slots), bf16),
            pltpu.VMEM((1, slots), jnp.int32),
            pltpu.SMEM((CZ - 1,), f32),
            pltpu.VMEM((CZ, L), f32),
            dma((4,)),
        ),
        cost=cost(4),
    )
    after, *tend = call(
        functools.partial(physics_kernel, staged),
        (pltpu.VMEM((rows_f, slots), bf16), *sent),
        (*received, *prepared),
        scratch=(
            pltpu.VMEM((rows_f, slots), f32),
            pltpu.VMEM((5, ZP, slots), f32),
            pltpu.VMEM((2, ZP, slots), f32),
            pltpu.VMEM((slots, 2 * L), f32),
            pltpu.VMEM((slots, 2 * L), f32),
        ),
        aliases={len(received): 0},
        cost=cost(5),
    )
    returned = exchange(tend)
    crm_new = call(
        store_kernel,
        jax.ShapeDtypeStruct((CZ, CX * slots), bf16),
        (after,),
        scratch=(pltpu.VMEM((CZ, CX * slots), bf16), dma((NI // 2 * SUB,))),
        out_specs=hbm,
        cost=cost(3),
    )
    new_state = call(
        functools.partial(finish_kernel, staged),
        jax.ShapeDtypeStruct((per_tile, width), f32),
        (moved, take, *returned),
        scratch=(pltpu.VMEM((per_tile, 2 * L), f32), dma((2,))),
        out_specs=hbm,
        cost=cost(0.7),
    )
    return (new_state[None], crm_new[None, None])


def solution(mesh):
    in_specs = (
        P("edge", "cols", None),
        P("edge", "cols", None),
        P("edge", "cols", None),
        P("edge", "cols", None, None),
        P("edge", "cols", None),
        P(),
        P(),
    )
    out_specs = (P("edge", "cols", None), P("edge", "cols", None, None))
    return jax.shard_map(shards, mesh=mesh, in_specs=in_specs, out_specs=out_specs, check_vma=False)
```

```python
import functools

import jax
import jax.numpy as jnp
from jax import lax
from jax.experimental import pallas as pl
from jax.experimental.pallas import tpu as pltpu
from jax.sharding import PartitionSpec as P

L = 64
CX = 64
CZ = 58
TW = 8
SUBSTEPS = 2
ZP = 64
LANES = 128
SUB = 8
NI = CX // SUB
STAGED = 8
TZ = 16

kappa_edge = 0.25
max_courant = 0.9
relax_rate = 0.5


def call(body, outs, args, scratch=(), in_specs=None, out_specs=None, cost=None, limit=32 << 20, aliases=None):
    kw = {}
    if out_specs is not None:
        kw["out_specs"] = out_specs
    if in_specs is not None:
        kw["in_specs"] = in_specs
    return pl.pallas_call(
        body,
        out_shape=outs,
        scratch_shapes=list(scratch),
        compiler_params=pltpu.CompilerParams(vmem_limit_bytes=limit),
        cost_estimate=cost,
        input_output_aliases=aliases or {},
        **kw,
    )(*args)


def swap(value, axis, first):
    count = lax.axis_size(axis)
    pairs = []
    for one in range(first, count, 2):
        other = (one + 1) % count
        pairs += [(one, other), (other, one)]
    return lax.ppermute(value, axis, pairs)


def pair_kernel(own_ref, got_ref, *pair_refs):
    rows = pair_refs[0].shape[0] // 2
    for k, ref in enumerate(pair_refs):
        far = len(pair_refs) - k
        here = slice(far * rows, (far + 1) * rows)
        ref[:rows, :] = own_ref[here, :]
        ref[rows:, :] = got_ref[here, :]


def exchange(sent):
    count = lax.axis_size("cols")
    if len(sent) == 1:
        whole = sent[0].reshape(count, -1, sent[0].shape[1])
        return [lax.all_to_all(whole, "cols", split_axis=0, concat_axis=0, tiled=True).reshape(sent[0].shape)]

    def trade(value, k):
        return lax.ppermute(value, "cols", [(c, c ^ k) for c in range(count)])

    own, other = sent
    got = trade(other, 1)
    far_ones = count // 2 - 1
    pairs = call(
        pair_kernel,
        tuple(pltpu.VMEM((2 * own.shape[0] // (count // 2), own.shape[1]), jnp.float32) for _ in range(far_ones)),
        (own, got),
        cost=cost(0.2),
    )
    return [own, got, *[trade(pair, 2 * (far_ones - k)) for k, pair in enumerate(pairs)]]


def arrived(refs, rows):
    out = [(0, refs[0][:rows, :]), (1, refs[1][:rows, :])]
    for k, ref in enumerate(refs[:1:-1]):
        out += [(2 * (k + 1), ref[:rows, :]), (2 * (k + 1) + 1, ref[rows:, :])]
    return out


def tile_rows(distance, rows):
    return pl.ds(pl.multiple_of((lax.axis_index("cols") ^ distance) * rows, SUB), rows)


def odd_strip():
    return lax.rem(lax.axis_index("edge"), 2)


def split_dot(chosen, value):
    high, low = parts_of(value)
    pick = lambda part: lax.dot_general(chosen, part, (((1,), (0,)), ((), ())), preferred_element_type=jnp.float32)
    return pick(high) + pick(low)


def parts_of(value):
    high = value.astype(jnp.bfloat16)
    return high, (value - high.astype(jnp.float32)).astype(jnp.bfloat16)


def rows_kernel(state_hbm, outer_ref, inner_ref, sems):
    last = state_hbm.shape[0] - TW
    outer = pl.multiple_of(odd_strip() * last, TW)
    inner = pl.multiple_of((1 - odd_strip()) * last, TW)
    copies = [
        pltpu.make_async_copy(state_hbm.at[pl.ds(outer, TW)], outer_ref, sems.at[0]),
        pltpu.make_async_copy(state_hbm.at[pl.ds(inner, TW)], inner_ref, sems.at[1]),
    ]
    for copy in copies:
        copy.start()
    for copy in copies:
        copy.wait()


def slots_kernel(cap, staged, state_hbm, owners_hbm, orient_hbm, tile_ref, put_ref, take_ref, flip_ref, own_ref, turn_ref, sems):
    per_tile = owners_hbm.shape[1]
    n_slots = put_ref.shape[0]
    copies = [
        pltpu.make_async_copy(owners_hbm, own_ref, sems.at[0]),
        pltpu.make_async_copy(orient_hbm, turn_ref, sems.at[1]),
        pltpu.make_async_copy(state_hbm, tile_ref, sems.at[2]),
    ]
    for copy in copies:
        copy.start()
    row = lax.broadcasted_iota(jnp.int32, (per_tile, per_tile), 0)
    col = lax.broadcasted_iota(jnp.int32, (per_tile, per_tile), 1)
    q_down = lax.broadcasted_iota(jnp.int32, (n_slots, per_tile), 0)
    q_across = lax.broadcasted_iota(jnp.int32, (per_tile, n_slots), 1)
    copies[0].wait()
    named = own_ref[...]
    if staged:
        named = named ^ lax.axis_index("cols")
        named = (named & 1) * (staged // 2) + (named >> 1)
    across = jnp.broadcast_to(named, (per_tile, per_tile))
    down = across.T
    same = down == across
    before_col = jnp.where(same & (row < col), 1.0, 0.0)
    before_row = jnp.where(same & (col < row), 1.0, 0.0)
    rank_across = jnp.sum(before_col, axis=0, keepdims=True).astype(jnp.int32)
    rank_down = jnp.sum(before_row, axis=1, keepdims=True).astype(jnp.int32)
    slot_across = across[0:1, :] * cap + rank_across
    slot_down = down[:, 0:1] * cap + rank_down
    put_ref[...] = jnp.where(q_down == slot_across, 1.0, 0.0).astype(jnp.bfloat16)
    take_ref[...] = jnp.where(q_across == slot_down, 1.0, 0.0).astype(jnp.bfloat16)
    copies[1].wait()
    for k in range(2):
        flip_ref[k] = jnp.broadcast_to(turn_ref[0:1, k : k + 1], (TW, LANES))
    copies[2].wait()


def edge_kernel(tile_ref, outer_ref, inner_ref, flip_ref, put_ref, moved_ref, *out_refs):
    per_tile, width = tile_ref.shape

    odd = odd_strip() == 1

    def turned(value, k):
        back = jnp.concatenate([value[TW - 1 - w : TW - w] for w in range(TW)], axis=0)
        flip = jnp.concatenate([flip_ref[k]] * (width // LANES), axis=1)
        return jnp.where(flip == 1, back, value)

    outer, inner = outer_ref[...], inner_ref[...]
    low = turned(jnp.where(odd, inner, outer), 0)
    high = turned(jnp.where(odd, outer, inner), 1)
    tiles = tile_ref[...]
    below = jnp.concatenate([low, tiles[: per_tile - TW]], axis=0)
    above = jnp.concatenate([tiles[TW:], high], axis=0)
    moved = tiles + kappa_edge * ((above + below) - 2.0 * tiles)
    picked = split_dot(put_ref[...], moved[:, : 2 * L])
    for k, ref in enumerate(out_refs):
        rows = ref.shape[0]
        ref[...] = picked[k * rows : (k + 1) * rows]
    moved_ref[...] = moved


def rows_from_levels(flipped):
    n = 2 * SUB * TZ
    a = lax.broadcasted_iota(jnp.int32, (n, n), 1 if flipped else 0)
    b = lax.broadcasted_iota(jnp.int32, (n, n), 0 if flipped else 1)
    z, p, s = a >> 4, (a >> 3) & 1, a & 7
    return jnp.where(b == p * (SUB * TZ) + s * TZ + z, 1.0, 0.0).astype(jnp.bfloat16)


def prepare_kernel(
    crm_hbm, active_hbm, diff_hbm, vm_hbm, f_ref, mean_ref, sq_ref, coef_ref, wa_ref, wb_ref, crm_ref, act_ref, diff_ref, vm_ref, sems
):
    slots = active_hbm.shape[1]
    copies = [
        pltpu.make_async_copy(active_hbm, act_ref, sems.at[0]),
        pltpu.make_async_copy(diff_hbm, diff_ref, sems.at[1]),
        pltpu.make_async_copy(vm_hbm, vm_ref, sems.at[2]),
        pltpu.make_async_copy(crm_hbm, crm_ref, sems.at[3]),
    ]
    for copy in copies:
        copy.start()
    order = rows_from_levels(False)
    coef_ref[...] = jnp.zeros_like(coef_ref)
    copies[0].wait()
    copies[1].wait()
    active = act_ref[...]
    nothing = jnp.zeros((1, slots), jnp.float32)

    def link(i):
        if i < 0 or i >= CZ - 1:
            return nothing
        return jnp.where(i + 1 < active, diff_ref[i], 0.0)

    up, down = nothing, nothing
    for z in range(CZ):
        lower, upper = link(z - 1), link(z)
        up = 1.0 / (1.0 + lower + upper - lower * (lower * up))
        coef_ref[0, z : z + 1, :] = up
        coef_ref[1, z : z + 1, :] = lower * up
        coef_ref[2, z : z + 1, :] = upper * up
        y = CZ - 1 - z
        lower, upper = link(y - 1), link(y)
        down = 1.0 / (1.0 + lower + upper - upper * (upper * down))
        coef_ref[3, y : y + 1, :] = down
        coef_ref[4, y : y + 1, :] = upper * down
        coef_ref[5, y : y + 1, :] = lower * down
    copies[2].wait()
    pad = jnp.zeros((CZ, L), jnp.float32)
    rest = jnp.zeros((ZP - CZ, 2 * L), jnp.float32)
    both = [jnp.concatenate([vm_ref[...], pad], axis=1), rest, jnp.concatenate([pad, vm_ref[...]], axis=1), rest]
    high, low = parts_of(jnp.concatenate(both, axis=0))
    wa_ref[...] = jnp.concatenate([high, low, high], axis=1)
    wb_ref[...] = jnp.concatenate([high, high, low], axis=0)

    copies[3].wait()
    for t in range(ZP // TZ):
        rows = min(TZ, CZ - t * TZ)
        total = jnp.zeros((TZ, slots), jnp.float32)
        square = jnp.zeros((TZ, slots), jnp.float32)
        for p in range(NI // 2):
            parts = []
            for i in (2 * p, 2 * p + 1):
                for s in range(SUB):
                    x = s * NI + i
                    v = crm_ref[t * TZ : t * TZ + rows, x * slots : (x + 1) * slots]
                    wide = v.astype(jnp.float32)
                    if rows < TZ:
                        wide = jnp.concatenate([wide, jnp.zeros((TZ - rows, slots), jnp.float32)], axis=0)
                        v = wide.astype(jnp.bfloat16)
                    total = total + wide
                    square = square + wide * wide
                    parts.append(v)
            turned = lax.dot_general(
                order, jnp.concatenate(parts, axis=0), (((1,), (0,)), ((), ())), preferred_element_type=jnp.float32
            ).astype(jnp.bfloat16)
            for z in range(rows):
                base = (t * TZ + z) * CX + p * 2 * SUB
                f_ref[base : base + 2 * SUB, :] = turned[z * 2 * SUB : (z + 1) * 2 * SUB]
        mean_ref[t * TZ : (t + 1) * TZ, :] = total * (1.0 / CX)
        sq_ref[t * TZ : (t + 1) * TZ, :] = square * (1.0 / CX)


def physics_kernel(staged, *refs):
    n_in = staged // 2 + 1 if staged else 1
    sent_refs, refs = refs[:n_in], refs[n_in:]
    f_ref, mean_ref, sq_ref, coef_ref, wa_ref, wb_ref, y_ref = refs[:7]
    back_refs = refs[7:-5]
    g_ref, adv_ref, sum_ref, cols_ref, tend_ref = refs[-5:]
    slots = cols_ref.shape[0]
    if staged:
        rows = slots // staged
        for distance, value in arrived(sent_refs, rows):
            cols_ref[tile_rows(distance, rows), :] = value
    else:
        cols_ref[...] = sent_refs[0][...]
    halves = slots // LANES
    for h in range(halves):
        lane = slice(h * LANES, (h + 1) * LANES)
        high, low = parts_of(cols_ref[lane, :])
        mapped = lax.dot_general(
            wa_ref[...],
            jnp.concatenate([high, high, low], axis=1),
            (((1,), (1,)), ((), ())),
            preferred_element_type=jnp.float32,
        )
        forcing = mapped[0:ZP]
        courant = max_courant * jax.nn.sigmoid(mapped[ZP:])
        inv1 = coef_ref[0, :, lane]
        inv2 = coef_ref[3, :, lane]
        adv_ref[0, :, lane] = inv1 * (1.0 - courant)
        adv_ref[1, :, lane] = inv1 * courant
        adv_ref[2, :, lane] = inv2 * (1.0 - courant)
        adv_ref[3, :, lane] = inv2 * courant
        adv_ref[4, :, lane] = inv1 * (relax_rate * (forcing - mean_ref[:, lane]))
    sum_ref[:, CZ:, :] = jnp.zeros((2, ZP - CZ, slots), jnp.float32)

    def spread(ref, k, z, lane):
        return jnp.broadcast_to(ref[k, z : z + 1, lane], (SUB, LANES))

    for h in range(halves):
        lane = slice(h * LANES, (h + 1) * LANES)

        def at(z, i, n=1):
            base = z * CX + i * SUB
            return slice(base, base + n * SUB)

        zero = jnp.zeros((SUB, LANES), jnp.float32)
        prev = [zero] * NI
        for z in range(CZ):
            a, b = spread(adv_ref, 0, z, lane), spread(adv_ref, 1, z, lane)
            d, e = spread(adv_ref, 4, z, lane), spread(coef_ref, 1, z, lane)
            f = []
            for i in range(0, NI, 2):
                pair = f_ref[at(z, i, 2), lane].astype(jnp.float32)
                f += [pair[:SUB], pair[SUB:]]
            behind = [pltpu.roll(f[NI - 1], 1, axis=0)] + f[: NI - 1]
            prev = [((a * f[i] + d) + b * behind[i]) + e * prev[i] for i in range(NI)]
            for i in range(NI):
                g_ref[at(z, i), lane] = prev[i]
        after = [zero] * NI
        prev = [zero] * NI
        for z in range(CZ - 1, -1, -1):
            g = spread(coef_ref, 2, z, lane)
            a, b = spread(adv_ref, 2, z, lane), spread(adv_ref, 3, z, lane)
            e = spread(coef_ref, 4, z, lane)
            after = [g_ref[at(z, i), lane] + g * after[i] for i in range(NI)]
            behind = [pltpu.roll(after[NI - 1], 1, axis=0)] + after[: NI - 1]
            prev = [(a * after[i] + b * behind[i]) + e * prev[i] for i in range(NI)]
            for i in range(NI):
                g_ref[at(z, i), lane] = prev[i]
        after = [zero] * NI
        for z in range(CZ):
            g = spread(coef_ref, 5, z, lane)
            after = [g_ref[at(z, i), lane] + g * after[i] for i in range(NI)]
            total = [after[i] + after[i + 1] for i in range(0, NI, 2)]
            square = [after[i] * after[i] + after[i + 1] * after[i + 1] for i in range(0, NI, 2)]
            for i in range(0, NI, 2):
                y_ref[at(z, i, 2), lane] = jnp.concatenate(after[i : i + 2], axis=0).astype(jnp.bfloat16)
            sum_ref[0, z : z + 1, lane] = jnp.sum((total[0] + total[1]) + (total[2] + total[3]), axis=0, keepdims=True)
            sum_ref[1, z : z + 1, lane] = jnp.sum((square[0] + square[1]) + (square[2] + square[3]), axis=0, keepdims=True)
        mean0, sq0 = mean_ref[:, lane], sq_ref[:, lane]
        mean1, sq1 = sum_ref[0, :, lane] * (1.0 / CX), sum_ref[1, :, lane] * (1.0 / CX)
        change = jnp.concatenate([mean1 - mean0, (sq1 - mean1 * mean1) - (sq0 - mean0 * mean0)], axis=0)
        high, low = parts_of(change)
        tend_ref[lane, :] = lax.dot_general(
            jnp.concatenate([high, low, high], axis=0),
            wb_ref[...],
            (((0,), (0,)), ((), ())),
            preferred_element_type=jnp.float32,
        )
    if staged:
        for distance in range(staged):
            place = distance // 2 * rows
            back_refs[distance % 2][place : place + rows, :] = tend_ref[tile_rows(distance, rows), :]
    else:
        back_refs[0][...] = tend_ref[...]


def store_kernel(y_ref, crm_hbm, crm_ref, sems):
    slots = crm_hbm.shape[1] // CX
    order = rows_from_levels(True)
    copies = []
    for p in range(NI // 2):
        for t in range(ZP // TZ):
            rows = min(TZ, CZ - t * TZ)
            parts = [y_ref[(t * TZ + z) * CX + p * 2 * SUB : (t * TZ + z) * CX + (p + 1) * 2 * SUB, :] for z in range(rows)]
            if rows < TZ:
                parts.append(jnp.zeros(((TZ - rows) * 2 * SUB, slots), jnp.bfloat16))
            turned = lax.dot_general(
                order, jnp.concatenate(parts, axis=0), (((1,), (0,)), ((), ())), preferred_element_type=jnp.float32
            ).astype(jnp.bfloat16)
            for i in range(2):
                for s in range(SUB):
                    x = s * NI + 2 * p + i
                    k = (i * SUB + s) * TZ
                    crm_ref[t * TZ : t * TZ + rows, x * slots : (x + 1) * slots] = turned[k : k + rows]
        for s in range(SUB):
            here = pl.ds((s * NI + 2 * p) * slots, 2 * slots)
            copy = pltpu.make_async_copy(crm_ref.at[:, here], crm_hbm.at[:, here], sems.at[p * SUB + s])
            copy.start()
            copies.append(copy)
    for copy in copies:
        copy.wait()


def finish_kernel(staged, moved_ref, take_ref, *refs):
    back_refs = refs[:-3]
    out_hbm, part_ref, sems = refs[-3:]
    rest = pltpu.make_async_copy(moved_ref.at[:, 2 * L :], out_hbm.at[:, 2 * L :], sems.at[0])
    rest.start()
    if staged:
        parts = arrived(back_refs, take_ref.shape[1] // staged)
        back = jnp.concatenate([part for _, part in parts[0::2] + parts[1::2]], axis=0)
    else:
        back = back_refs[0][...]
    part_ref[...] = moved_ref[:, : 2 * L] + split_dot(take_ref[...], back)
    first = pltpu.make_async_copy(part_ref, out_hbm.at[:, : 2 * L], sems.at[1])
    first.start()
    rest.wait()
    first.wait()


def cost(us):
    return pl.CostEstimate(flops=0, bytes_accessed=int(us * 3.0e6), transcendentals=0)


def far(x):
    return pltpu.with_memory_space_constraint(x, pltpu.HBM)


def shards(state, owners, orient, crm_state, active_levels, vertical_map, diffusion):
    f32, bf16 = jnp.float32, jnp.bfloat16
    n_tiles = lax.axis_size("cols")
    per_tile = state.shape[1]
    width = state.shape[2]
    cap_slots = max(2, 2 * per_tile // n_tiles)
    slots = n_tiles * cap_slots
    rows_f = CZ * CX
    staged = n_tiles if n_tiles == STAGED else 0
    if staged:
        sent = (pltpu.VMEM((slots // 2, 2 * L), f32),) * 2
    else:
        sent = (jax.ShapeDtypeStruct((slots, 2 * L), f32),)
    hbm = pl.BlockSpec(memory_space=pltpu.HBM)
    dma = pltpu.SemaphoreType.DMA
    tile = state[0]
    outer, inner = call(
        rows_kernel,
        (pltpu.VMEM((TW, width), f32), pltpu.VMEM((TW, width), f32)),
        (far(tile),),
        in_specs=[hbm],
        scratch=(dma((2,)),),
        cost=cost(0.5),
    )
    outer = swap(outer, "edge", 1)
    inner = swap(inner, "edge", 0)
    near, put, take, flip = call(
        functools.partial(slots_kernel, cap_slots, staged),
        (
            pltpu.VMEM((per_tile, width), f32),
            pltpu.VMEM((slots, per_tile), bf16),
            pltpu.VMEM((per_tile, slots), bf16),
            pltpu.VMEM((2, TW, LANES), jnp.int32),
        ),
        (far(tile), far(owners.reshape(1, per_tile)), far(orient[0])),
        in_specs=[hbm] * 3,
        scratch=(pltpu.VMEM((1, per_tile), jnp.int32), pltpu.VMEM((1, 2), jnp.int32), dma((3,))),
        cost=cost(1),
    )
    moved, *outgoing = call(
        edge_kernel,
        (pltpu.VMEM((per_tile, width), f32), *sent),
        (near, outer, inner, flip, put),
        cost=cost(1),
    )
    received = exchange(outgoing)
    prepared = call(
        prepare_kernel,
        (
            pltpu.VMEM((rows_f, slots), bf16),
            pltpu.VMEM((ZP, slots), f32),
            pltpu.VMEM((ZP, slots), f32),
            pltpu.VMEM((6, ZP, slots), f32),
            pltpu.VMEM((2 * ZP, 6 * L), bf16),
            pltpu.VMEM((6 * ZP, 2 * L), bf16),
        ),
        (far(crm_state[0, 0]), far(active_levels[0]), far(diffusion), far(vertical_map)),
        in_specs=[hbm] * 4,
        scratch=(
            pltpu.VMEM((CZ, CX * slots), bf16),
            pltpu.VMEM((1, slots), jnp.int32),
            pltpu.SMEM((CZ - 1,), f32),
            pltpu.VMEM((CZ, L), f32),
            dma((4,)),
        ),
        cost=cost(4),
    )
    after, *tend = call(
        functools.partial(physics_kernel, staged),
        (pltpu.VMEM((rows_f, slots), bf16), *sent),
        (*received, *prepared),
        scratch=(
            pltpu.VMEM((rows_f, slots), f32),
            pltpu.VMEM((5, ZP, slots), f32),
            pltpu.VMEM((2, ZP, slots), f32),
            pltpu.VMEM((slots, 2 * L), f32),
            pltpu.VMEM((slots, 2 * L), f32),
        ),
        aliases={len(received): 0},
        cost=cost(5),
    )
    returned = exchange(tend)
    crm_new = call(
        store_kernel,
        jax.ShapeDtypeStruct((CZ, CX * slots), bf16),
        (after,),
        scratch=(pltpu.VMEM((CZ, CX * slots), bf16), dma((NI // 2 * SUB,))),
        out_specs=hbm,
        cost=cost(3),
    )
    new_state = call(
        functools.partial(finish_kernel, staged),
        jax.ShapeDtypeStruct((per_tile, width), f32),
        (moved, take, *returned),
        scratch=(pltpu.VMEM((per_tile, 2 * L), f32), dma((2,))),
        out_specs=hbm,
        cost=cost(0.7),
    )
    return (new_state[None], crm_new[None, None])


def solution(mesh):
    in_specs = (
        P("edge", "cols", None),
        P("edge", "cols", None),
        P("edge", "cols", None),
        P("edge", "cols", None, None),
        P("edge", "cols", None),
        P(),
        P(),
    )
    out_specs = (P("edge", "cols", None), P("edge", "cols", None, None))
    return jax.shard_map(shards, mesh=mesh, in_specs=in_specs, out_specs=out_specs, check_vma=False)
```

```python
import functools

import jax
import jax.numpy as jnp
from jax import lax
from jax.experimental import pallas as pl
from jax.experimental.pallas import tpu as pltpu
from jax.sharding import PartitionSpec as P

L = 64
CX = 64
CZ = 58
TW = 8
SUBSTEPS = 2
ZP = 64
LANES = 128
SUB = 8
NI = CX // SUB
STAGED = 8
TZ = 16

kappa_edge = 0.25
max_courant = 0.9
relax_rate = 0.5


def call(body, outs, args, scratch=(), in_specs=None, out_specs=None, cost=None, limit=32 << 20, aliases=None):
    kw = {}
    if out_specs is not None:
        kw["out_specs"] = out_specs
    if in_specs is not None:
        kw["in_specs"] = in_specs
    return pl.pallas_call(
        body,
        out_shape=outs,
        scratch_shapes=list(scratch),
        compiler_params=pltpu.CompilerParams(vmem_limit_bytes=limit),
        cost_estimate=cost,
        input_output_aliases=aliases or {},
        **kw,
    )(*args)


def swap(value, axis, first):
    count = lax.axis_size(axis)
    pairs = []
    for one in range(first, count, 2):
        other = (one + 1) % count
        pairs += [(one, other), (other, one)]
    return lax.ppermute(value, axis, pairs)


def pair_kernel(ahead, own_ref, got_ref, *refs):
    pair_refs = refs[ahead:]
    rows = pair_refs[0].shape[0] // 2
    for k, ref in enumerate(pair_refs):
        far = len(pair_refs) - k
        here = slice(far * rows, (far + 1) * rows)
        ref[:rows, :] = own_ref[here, :]
        ref[rows:, :] = got_ref[here, :]


def exchange(sent, ahead=()):
    count = lax.axis_size("cols")
    if len(sent) == 1:
        whole = sent[0].reshape(count, -1, sent[0].shape[1])
        return [lax.all_to_all(whole, "cols", split_axis=0, concat_axis=0, tiled=True).reshape(sent[0].shape)]

    def trade(value, k):
        return lax.ppermute(value, "cols", [(c, c ^ k) for c in range(count)])

    own, other = sent
    got = trade(other, 1)
    far_ones = count // 2 - 1
    pairs = call(
        functools.partial(pair_kernel, len(ahead)),
        tuple(pltpu.VMEM((2 * own.shape[0] // (count // 2), own.shape[1]), jnp.float32) for _ in range(far_ones)),
        (own, got, *ahead),
        in_specs=[pl.BlockSpec(memory_space=pltpu.VMEM)] * 2 + [pl.BlockSpec(memory_space=pl.ANY)] * len(ahead),
        cost=cost(0.2),
    )
    return [own, got, *[trade(pair, 2 * (far_ones - k)) for k, pair in enumerate(pairs)]]


def arrived(refs, rows):
    out = [(0, refs[0][:rows, :]), (1, refs[1][:rows, :])]
    for k, ref in enumerate(refs[:1:-1]):
        out += [(2 * (k + 1), ref[:rows, :]), (2 * (k + 1) + 1, ref[rows:, :])]
    return out


def tile_rows(distance, rows):
    return pl.ds(pl.multiple_of((lax.axis_index("cols") ^ distance) * rows, SUB), rows)


def odd_strip():
    return lax.rem(lax.axis_index("edge"), 2)


def split_dot(chosen, value):
    high, low = parts_of(value)
    pick = lambda part: lax.dot_general(chosen, part, (((1,), (0,)), ((), ())), preferred_element_type=jnp.float32)
    return pick(high) + pick(low)


def parts_of(value):
    high = value.astype(jnp.bfloat16)
    return high, (value - high.astype(jnp.float32)).astype(jnp.bfloat16)


def rows_kernel(state_hbm, outer_ref, inner_ref, sems):
    last = state_hbm.shape[0] - TW
    outer = pl.multiple_of(odd_strip() * last, TW)
    inner = pl.multiple_of((1 - odd_strip()) * last, TW)
    copies = [
        pltpu.make_async_copy(state_hbm.at[pl.ds(outer, TW)], outer_ref, sems.at[0]),
        pltpu.make_async_copy(state_hbm.at[pl.ds(inner, TW)], inner_ref, sems.at[1]),
    ]
    for copy in copies:
        copy.start()
    for copy in copies:
        copy.wait()


def slots_kernel(cap, staged, state_hbm, owners_hbm, orient_hbm, tile_ref, put_ref, take_ref, flip_ref, own_ref, turn_ref, sems):
    per_tile = owners_hbm.shape[1]
    n_slots = put_ref.shape[0]
    copies = [
        pltpu.make_async_copy(owners_hbm, own_ref, sems.at[0]),
        pltpu.make_async_copy(orient_hbm, turn_ref, sems.at[1]),
        pltpu.make_async_copy(state_hbm, tile_ref, sems.at[2]),
    ]
    for copy in copies:
        copy.start()
    row = lax.broadcasted_iota(jnp.int32, (per_tile, per_tile), 0)
    col = lax.broadcasted_iota(jnp.int32, (per_tile, per_tile), 1)
    q_down = lax.broadcasted_iota(jnp.int32, (n_slots, per_tile), 0)
    q_across = lax.broadcasted_iota(jnp.int32, (per_tile, n_slots), 1)
    copies[0].wait()
    named = own_ref[...]
    if staged:
        named = named ^ lax.axis_index("cols")
        named = (named & 1) * (staged // 2) + (named >> 1)
    across = jnp.broadcast_to(named, (per_tile, per_tile))
    down = across.T
    same = down == across
    before_col = jnp.where(same & (row < col), 1.0, 0.0)
    before_row = jnp.where(same & (col < row), 1.0, 0.0)
    rank_across = jnp.sum(before_col, axis=0, keepdims=True).astype(jnp.int32)
    rank_down = jnp.sum(before_row, axis=1, keepdims=True).astype(jnp.int32)
    slot_across = across[0:1, :] * cap + rank_across
    slot_down = down[:, 0:1] * cap + rank_down
    put_ref[...] = jnp.where(q_down == slot_across, 1.0, 0.0).astype(jnp.bfloat16)
    take_ref[...] = jnp.where(q_across == slot_down, 1.0, 0.0).astype(jnp.bfloat16)
    copies[1].wait()
    for k in range(2):
        flip_ref[k] = jnp.broadcast_to(turn_ref[0:1, k : k + 1], (TW, LANES))
    copies[2].wait()


def edge_kernel(tile_ref, outer_ref, inner_ref, flip_ref, put_ref, moved_ref, *out_refs):
    per_tile, width = tile_ref.shape

    odd = odd_strip() == 1

    def turned(value, k):
        back = jnp.concatenate([value[TW - 1 - w : TW - w] for w in range(TW)], axis=0)
        flip = jnp.concatenate([flip_ref[k]] * (width // LANES), axis=1)
        return jnp.where(flip == 1, back, value)

    outer, inner = outer_ref[...], inner_ref[...]
    low = turned(jnp.where(odd, inner, outer), 0)
    high = turned(jnp.where(odd, outer, inner), 1)
    tiles = tile_ref[...]
    below = jnp.concatenate([low, tiles[: per_tile - TW]], axis=0)
    above = jnp.concatenate([tiles[TW:], high], axis=0)
    moved = tiles + kappa_edge * ((above + below) - 2.0 * tiles)
    picked = split_dot(put_ref[...], moved[:, : 2 * L])
    for k, ref in enumerate(out_refs):
        rows = ref.shape[0]
        ref[...] = picked[k * rows : (k + 1) * rows]
    moved_ref[...] = moved


def rows_from_levels(flipped):
    n = 2 * SUB * TZ
    a = lax.broadcasted_iota(jnp.int32, (n, n), 1 if flipped else 0)
    b = lax.broadcasted_iota(jnp.int32, (n, n), 0 if flipped else 1)
    z, p, s = a >> 4, (a >> 3) & 1, a & 7
    return jnp.where(b == p * (SUB * TZ) + s * TZ + z, 1.0, 0.0).astype(jnp.bfloat16)


def prepare_kernel(
    crm_hbm, active_hbm, diff_hbm, vm_hbm, f_ref, mean_ref, sq_ref, coef_ref, wa_ref, wb_ref, crm_ref, act_ref, diff_ref, vm_ref, sems
):
    slots = active_hbm.shape[1]
    copies = [
        pltpu.make_async_copy(active_hbm, act_ref, sems.at[0]),
        pltpu.make_async_copy(diff_hbm, diff_ref, sems.at[1]),
        pltpu.make_async_copy(vm_hbm, vm_ref, sems.at[2]),
        pltpu.make_async_copy(crm_hbm, crm_ref, sems.at[3]),
    ]
    for copy in copies:
        copy.start()
    order = rows_from_levels(False)
    coef_ref[...] = jnp.zeros_like(coef_ref)
    copies[0].wait()
    copies[1].wait()
    active = act_ref[...]
    nothing = jnp.zeros((1, slots), jnp.float32)

    def link(i):
        if i < 0 or i >= CZ - 1:
            return nothing
        return jnp.where(i + 1 < active, diff_ref[i], 0.0)

    up, down = nothing, nothing
    for z in range(CZ):
        lower, upper = link(z - 1), link(z)
        up = 1.0 / (1.0 + lower + upper - lower * (lower * up))
        coef_ref[0, z : z + 1, :] = up
        coef_ref[1, z : z + 1, :] = lower * up
        coef_ref[2, z : z + 1, :] = upper * up
        y = CZ - 1 - z
        lower, upper = link(y - 1), link(y)
        down = 1.0 / (1.0 + lower + upper - upper * (upper * down))
        coef_ref[3, y : y + 1, :] = down
        coef_ref[4, y : y + 1, :] = upper * down
        coef_ref[5, y : y + 1, :] = lower * down
    copies[2].wait()
    pad = jnp.zeros((CZ, L), jnp.float32)
    rest = jnp.zeros((ZP - CZ, 2 * L), jnp.float32)
    both = [jnp.concatenate([vm_ref[...], pad], axis=1), rest, jnp.concatenate([pad, vm_ref[...]], axis=1), rest]
    high, low = parts_of(jnp.concatenate(both, axis=0))
    wa_ref[...] = jnp.concatenate([high, low, high], axis=1)
    wb_ref[...] = jnp.concatenate([high, high, low], axis=0)

    copies[3].wait()
    for t in range(ZP // TZ):
        rows = min(TZ, CZ - t * TZ)
        total = jnp.zeros((TZ, slots), jnp.float32)
        square = jnp.zeros((TZ, slots), jnp.float32)
        for p in range(NI // 2):
            parts = []
            for i in (2 * p, 2 * p + 1):
                for s in range(SUB):
                    x = s * NI + i
                    v = crm_ref[t * TZ : t * TZ + rows, x * slots : (x + 1) * slots]
                    wide = v.astype(jnp.float32)
                    if rows < TZ:
                        wide = jnp.concatenate([wide, jnp.zeros((TZ - rows, slots), jnp.float32)], axis=0)
                        v = wide.astype(jnp.bfloat16)
                    total = total + wide
                    square = square + wide * wide
                    parts.append(v)
            turned = lax.dot_general(
                order, jnp.concatenate(parts, axis=0), (((1,), (0,)), ((), ())), preferred_element_type=jnp.float32
            ).astype(jnp.bfloat16)
            for z in range(rows):
                base = (t * TZ + z) * CX + p * 2 * SUB
                f_ref[base : base + 2 * SUB, :] = turned[z * 2 * SUB : (z + 1) * 2 * SUB]
        mean_ref[t * TZ : (t + 1) * TZ, :] = total * (1.0 / CX)
        sq_ref[t * TZ : (t + 1) * TZ, :] = square * (1.0 / CX)


def physics_kernel(staged, *refs):
    n_in = staged // 2 + 1 if staged else 1
    sent_refs, refs = refs[:n_in], refs[n_in:]
    f_ref, mean_ref, sq_ref, coef_ref, wa_ref, wb_ref, y_ref = refs[:7]
    back_refs = refs[7:-5]
    g_ref, adv_ref, sum_ref, cols_ref, tend_ref = refs[-5:]
    slots = cols_ref.shape[0]
    if staged:
        rows = slots // staged
        for distance, value in arrived(sent_refs, rows):
            cols_ref[tile_rows(distance, rows), :] = value
    else:
        cols_ref[...] = sent_refs[0][...]
    halves = slots // LANES
    for h in range(halves):
        lane = slice(h * LANES, (h + 1) * LANES)
        high, low = parts_of(cols_ref[lane, :])
        mapped = lax.dot_general(
            wa_ref[...],
            jnp.concatenate([high, high, low], axis=1),
            (((1,), (1,)), ((), ())),
            preferred_element_type=jnp.float32,
        )
        forcing = mapped[0:ZP]
        courant = max_courant * jax.nn.sigmoid(mapped[ZP:])
        inv1 = coef_ref[0, :, lane]
        inv2 = coef_ref[3, :, lane]
        adv_ref[0, :, lane] = inv1 * (1.0 - courant)
        adv_ref[1, :, lane] = inv1 * courant
        adv_ref[2, :, lane] = inv2 * (1.0 - courant)
        adv_ref[3, :, lane] = inv2 * courant
        adv_ref[4, :, lane] = inv1 * (relax_rate * (forcing - mean_ref[:, lane]))
    sum_ref[:, CZ:, :] = jnp.zeros((2, ZP - CZ, slots), jnp.float32)

    def spread(ref, k, z, lane):
        return jnp.broadcast_to(ref[k, z : z + 1, lane], (SUB, LANES))

    for h in range(halves):
        lane = slice(h * LANES, (h + 1) * LANES)

        def at(z, i, n=1):
            base = z * CX + i * SUB
            return slice(base, base + n * SUB)

        zero = jnp.zeros((SUB, LANES), jnp.float32)
        prev = [zero] * NI
        for z in range(CZ):
            a, b = spread(adv_ref, 0, z, lane), spread(adv_ref, 1, z, lane)
            d, e = spread(adv_ref, 4, z, lane), spread(coef_ref, 1, z, lane)
            f = []
            for i in range(0, NI, 2):
                pair = f_ref[at(z, i, 2), lane].astype(jnp.float32)
                f += [pair[:SUB], pair[SUB:]]
            behind = [pltpu.roll(f[NI - 1], 1, axis=0)] + f[: NI - 1]
            prev = [((a * f[i] + d) + b * behind[i]) + e * prev[i] for i in range(NI)]
            for i in range(NI):
                g_ref[at(z, i), lane] = prev[i]
        after = [zero] * NI
        prev = [zero] * NI
        for z in range(CZ - 1, -1, -1):
            g = spread(coef_ref, 2, z, lane)
            a, b = spread(adv_ref, 2, z, lane), spread(adv_ref, 3, z, lane)
            e = spread(coef_ref, 4, z, lane)
            after = [g_ref[at(z, i), lane] + g * after[i] for i in range(NI)]
            behind = [pltpu.roll(after[NI - 1], 1, axis=0)] + after[: NI - 1]
            prev = [(a * after[i] + b * behind[i]) + e * prev[i] for i in range(NI)]
            for i in range(NI):
                g_ref[at(z, i), lane] = prev[i]
        after = [zero] * NI
        for z in range(CZ):
            g = spread(coef_ref, 5, z, lane)
            after = [g_ref[at(z, i), lane] + g * after[i] for i in range(NI)]
            total = [after[i] + after[i + 1] for i in range(0, NI, 2)]
            square = [after[i] * after[i] + after[i + 1] * after[i + 1] for i in range(0, NI, 2)]
            for i in range(0, NI, 2):
                y_ref[at(z, i, 2), lane] = jnp.concatenate(after[i : i + 2], axis=0).astype(jnp.bfloat16)
            sum_ref[0, z : z + 1, lane] = jnp.sum((total[0] + total[1]) + (total[2] + total[3]), axis=0, keepdims=True)
            sum_ref[1, z : z + 1, lane] = jnp.sum((square[0] + square[1]) + (square[2] + square[3]), axis=0, keepdims=True)
        mean0, sq0 = mean_ref[:, lane], sq_ref[:, lane]
        mean1, sq1 = sum_ref[0, :, lane] * (1.0 / CX), sum_ref[1, :, lane] * (1.0 / CX)
        change = jnp.concatenate([mean1 - mean0, (sq1 - mean1 * mean1) - (sq0 - mean0 * mean0)], axis=0)
        high, low = parts_of(change)
        tend_ref[lane, :] = lax.dot_general(
            jnp.concatenate([high, low, high], axis=0),
            wb_ref[...],
            (((0,), (0,)), ((), ())),
            preferred_element_type=jnp.float32,
        )
    if staged:
        for distance in range(staged):
            place = distance // 2 * rows
            back_refs[distance % 2][place : place + rows, :] = tend_ref[tile_rows(distance, rows), :]
    else:
        back_refs[0][...] = tend_ref[...]


def store_kernel(y_ref, crm_hbm, crm_ref, sems):
    slots = crm_hbm.shape[1] // CX
    order = rows_from_levels(True)
    copies = []
    for p in range(NI // 2):
        for t in range(ZP // TZ):
            rows = min(TZ, CZ - t * TZ)
            parts = [y_ref[(t * TZ + z) * CX + p * 2 * SUB : (t * TZ + z) * CX + (p + 1) * 2 * SUB, :] for z in range(rows)]
            if rows < TZ:
                parts.append(jnp.zeros(((TZ - rows) * 2 * SUB, slots), jnp.bfloat16))
            turned = lax.dot_general(
                order, jnp.concatenate(parts, axis=0), (((1,), (0,)), ((), ())), preferred_element_type=jnp.float32
            ).astype(jnp.bfloat16)
            for i in range(2):
                for s in range(SUB):
                    x = s * NI + 2 * p + i
                    k = (i * SUB + s) * TZ
                    crm_ref[t * TZ : t * TZ + rows, x * slots : (x + 1) * slots] = turned[k : k + rows]
        for s in range(SUB):
            here = pl.ds((s * NI + 2 * p) * slots, 2 * slots)
            copy = pltpu.make_async_copy(crm_ref.at[:, here], crm_hbm.at[:, here], sems.at[p * SUB + s])
            copy.start()
            copies.append(copy)
    for copy in copies:
        copy.wait()


def finish_kernel(staged, moved_ref, take_ref, *refs):
    back_refs = refs[:-3]
    out_hbm, part_ref, sems = refs[-3:]
    rest = pltpu.make_async_copy(moved_ref.at[:, 2 * L :], out_hbm.at[:, 2 * L :], sems.at[0])
    rest.start()
    if staged:
        parts = arrived(back_refs, take_ref.shape[1] // staged)
        back = jnp.concatenate([part for _, part in parts[0::2] + parts[1::2]], axis=0)
    else:
        back = back_refs[0][...]
    part_ref[...] = moved_ref[:, : 2 * L] + split_dot(take_ref[...], back)
    first = pltpu.make_async_copy(part_ref, out_hbm.at[:, : 2 * L], sems.at[1])
    first.start()
    rest.wait()
    first.wait()


def cost(us):
    return pl.CostEstimate(flops=0, bytes_accessed=int(us * 3.0e6), transcendentals=0)


def far(x):
    return pltpu.with_memory_space_constraint(x, pltpu.HBM)


def shards(state, owners, orient, crm_state, active_levels, vertical_map, diffusion):
    f32, bf16 = jnp.float32, jnp.bfloat16
    n_tiles = lax.axis_size("cols")
    per_tile = state.shape[1]
    width = state.shape[2]
    cap_slots = max(2, 2 * per_tile // n_tiles)
    slots = n_tiles * cap_slots
    rows_f = CZ * CX
    staged = n_tiles if n_tiles == STAGED else 0
    if staged:
        sent = (pltpu.VMEM((slots // 2, 2 * L), f32),) * 2
    else:
        sent = (jax.ShapeDtypeStruct((slots, 2 * L), f32),)
    hbm = pl.BlockSpec(memory_space=pltpu.HBM)
    dma = pltpu.SemaphoreType.DMA
    tile = state[0]
    outer, inner = call(
        rows_kernel,
        (pltpu.VMEM((TW, width), f32), pltpu.VMEM((TW, width), f32)),
        (far(tile),),
        in_specs=[hbm],
        scratch=(dma((2,)),),
        cost=cost(0.5),
    )
    outer = swap(outer, "edge", 1)
    inner = swap(inner, "edge", 0)
    near, put, take, flip = call(
        functools.partial(slots_kernel, cap_slots, staged),
        (
            pltpu.VMEM((per_tile, width), f32),
            pltpu.VMEM((slots, per_tile), bf16),
            pltpu.VMEM((per_tile, slots), bf16),
            pltpu.VMEM((2, TW, LANES), jnp.int32),
        ),
        (far(tile), far(owners.reshape(1, per_tile)), far(orient[0])),
        in_specs=[hbm] * 3,
        scratch=(pltpu.VMEM((1, per_tile), jnp.int32), pltpu.VMEM((1, 2), jnp.int32), dma((3,))),
        cost=cost(1),
    )
    moved, *outgoing = call(
        edge_kernel,
        (pltpu.VMEM((per_tile, width), f32), *sent),
        (near, outer, inner, flip, put),
        cost=cost(1),
    )
    prepared = call(
        prepare_kernel,
        (
            pltpu.VMEM((rows_f, slots), bf16),
            pltpu.VMEM((ZP, slots), f32),
            pltpu.VMEM((ZP, slots), f32),
            pltpu.VMEM((6, ZP, slots), f32),
            pltpu.VMEM((2 * ZP, 6 * L), bf16),
            pltpu.VMEM((6 * ZP, 2 * L), bf16),
        ),
        (far(crm_state[0, 0]), far(active_levels[0]), far(diffusion), far(vertical_map)),
        in_specs=[hbm] * 4,
        scratch=(
            pltpu.VMEM((CZ, CX * slots), bf16),
            pltpu.VMEM((1, slots), jnp.int32),
            pltpu.SMEM((CZ - 1,), f32),
            pltpu.VMEM((CZ, L), f32),
            dma((4,)),
        ),
        cost=cost(4),
    )
    received = exchange(outgoing, prepared[1:2])
    after, *tend = call(
        functools.partial(physics_kernel, staged),
        (pltpu.VMEM((rows_f, slots), bf16), *sent),
        (*received, *prepared),
        scratch=(
            pltpu.VMEM((rows_f, slots), f32),
            pltpu.VMEM((5, ZP, slots), f32),
            pltpu.VMEM((2, ZP, slots), f32),
            pltpu.VMEM((slots, 2 * L), f32),
            pltpu.VMEM((slots, 2 * L), f32),
        ),
        aliases={len(received): 0},
        cost=cost(5),
    )
    returned = exchange(tend)
    crm_new = call(
        store_kernel,
        jax.ShapeDtypeStruct((CZ, CX * slots), bf16),
        (after,),
        scratch=(pltpu.VMEM((CZ, CX * slots), bf16), dma((NI // 2 * SUB,))),
        out_specs=hbm,
        cost=cost(3),
    )
    new_state = call(
        functools.partial(finish_kernel, staged),
        jax.ShapeDtypeStruct((per_tile, width), f32),
        (moved, take, *returned),
        scratch=(pltpu.VMEM((per_tile, 2 * L), f32), dma((2,))),
        out_specs=hbm,
        cost=cost(0.7),
    )
    return (new_state[None], crm_new[None, None])


def solution(mesh):
    in_specs = (
        P("edge", "cols", None),
        P("edge", "cols", None),
        P("edge", "cols", None),
        P("edge", "cols", None, None),
        P("edge", "cols", None),
        P(),
        P(),
    )
    out_specs = (P("edge", "cols", None), P("edge", "cols", None, None))
    return jax.shard_map(shards, mesh=mesh, in_specs=in_specs, out_specs=out_specs, check_vma=False)
```

```python
import functools

import jax
import jax.numpy as jnp
from jax import lax
from jax.experimental import pallas as pl
from jax.experimental.pallas import tpu as pltpu
from jax.sharding import PartitionSpec as P

L = 64
CX = 64
CZ = 58
TW = 8
SUBSTEPS = 2
ZP = 64
LANES = 128
SUB = 8
NI = CX // SUB
STAGED = 8
ORDER_OUT = (2, 3, 1)
ORDER_BACK = (3, 2, 1)
TZ = 16

kappa_edge = 0.25
max_courant = 0.9
relax_rate = 0.5


def call(body, outs, args, scratch=(), in_specs=None, out_specs=None, cost=None, limit=32 << 20, aliases=None):
    kw = {}
    if out_specs is not None:
        kw["out_specs"] = out_specs
    if in_specs is not None:
        kw["in_specs"] = in_specs
    return pl.pallas_call(
        body,
        out_shape=outs,
        scratch_shapes=list(scratch),
        compiler_params=pltpu.CompilerParams(vmem_limit_bytes=limit),
        cost_estimate=cost,
        input_output_aliases=aliases or {},
        **kw,
    )(*args)


def swap(value, axis, first):
    count = lax.axis_size(axis)
    pairs = []
    for one in range(first, count, 2):
        other = (one + 1) % count
        pairs += [(one, other), (other, one)]
    return lax.ppermute(value, axis, pairs)


def pair_kernel(order, ahead, own_ref, got_ref, *refs):
    pair_refs = refs[ahead:]
    rows = pair_refs[0].shape[0] // 2
    for far, ref in zip(order, pair_refs):
        here = slice(far * rows, (far + 1) * rows)
        ref[:rows, :] = own_ref[here, :]
        ref[rows:, :] = got_ref[here, :]


def exchange(sent, order, ahead=()):
    count = lax.axis_size("cols")
    if len(sent) == 1:
        whole = sent[0].reshape(count, -1, sent[0].shape[1])
        return [lax.all_to_all(whole, "cols", split_axis=0, concat_axis=0, tiled=True).reshape(sent[0].shape)]

    def trade(value, k):
        return lax.ppermute(value, "cols", [(c, c ^ k) for c in range(count)])

    own, other = sent
    got = trade(other, 1)
    pairs = call(
        functools.partial(pair_kernel, order, len(ahead)),
        tuple(pltpu.VMEM((2 * own.shape[0] // (count // 2), own.shape[1]), jnp.float32) for _ in order),
        (own, got, *ahead),
        in_specs=[pl.BlockSpec(memory_space=pltpu.VMEM)] * 2 + [pl.BlockSpec(memory_space=pl.ANY)] * len(ahead),
        cost=cost(0.2),
    )
    return [own, got, *[trade(pair, 2 * far) for far, pair in zip(order, pairs)]]


def arrived(refs, rows, order):
    out = [(0, refs[0][:rows, :]), (1, refs[1][:rows, :])]
    for far, ref in sorted(zip(order, refs[2:]), key=lambda pair: pair[0]):
        out += [(2 * far, ref[:rows, :]), (2 * far + 1, ref[rows:, :])]
    return out


def tile_rows(distance, rows):
    return pl.ds(pl.multiple_of((lax.axis_index("cols") ^ distance) * rows, SUB), rows)


def odd_strip():
    return lax.rem(lax.axis_index("edge"), 2)


def split_dot(chosen, value):
    high, low = parts_of(value)
    pick = lambda part: lax.dot_general(chosen, part, (((1,), (0,)), ((), ())), preferred_element_type=jnp.float32)
    return pick(high) + pick(low)


def parts_of(value):
    high = value.astype(jnp.bfloat16)
    return high, (value - high.astype(jnp.float32)).astype(jnp.bfloat16)


def rows_kernel(state_hbm, outer_ref, inner_ref, sems):
    last = state_hbm.shape[0] - TW
    outer = pl.multiple_of(odd_strip() * last, TW)
    inner = pl.multiple_of((1 - odd_strip()) * last, TW)
    copies = [
        pltpu.make_async_copy(state_hbm.at[pl.ds(outer, TW)], outer_ref, sems.at[0]),
        pltpu.make_async_copy(state_hbm.at[pl.ds(inner, TW)], inner_ref, sems.at[1]),
    ]
    for copy in copies:
        copy.start()
    for copy in copies:
        copy.wait()


def slots_kernel(cap, staged, state_hbm, owners_hbm, orient_hbm, tile_ref, put_ref, take_ref, flip_ref, own_ref, turn_ref, sems):
    per_tile = owners_hbm.shape[1]
    n_slots = put_ref.shape[0]
    copies = [
        pltpu.make_async_copy(owners_hbm, own_ref, sems.at[0]),
        pltpu.make_async_copy(orient_hbm, turn_ref, sems.at[1]),
        pltpu.make_async_copy(state_hbm, tile_ref, sems.at[2]),
    ]
    for copy in copies:
        copy.start()
    row = lax.broadcasted_iota(jnp.int32, (per_tile, per_tile), 0)
    col = lax.broadcasted_iota(jnp.int32, (per_tile, per_tile), 1)
    q_down = lax.broadcasted_iota(jnp.int32, (n_slots, per_tile), 0)
    q_across = lax.broadcasted_iota(jnp.int32, (per_tile, n_slots), 1)
    copies[0].wait()
    named = own_ref[...]
    if staged:
        named = named ^ lax.axis_index("cols")
        named = (named & 1) * (staged // 2) + (named >> 1)
    across = jnp.broadcast_to(named, (per_tile, per_tile))
    down = across.T
    same = down == across
    before_col = jnp.where(same & (row < col), 1.0, 0.0)
    before_row = jnp.where(same & (col < row), 1.0, 0.0)
    rank_across = jnp.sum(before_col, axis=0, keepdims=True).astype(jnp.int32)
    rank_down = jnp.sum(before_row, axis=1, keepdims=True).astype(jnp.int32)
    slot_across = across[0:1, :] * cap + rank_across
    slot_down = down[:, 0:1] * cap + rank_down
    put_ref[...] = jnp.where(q_down == slot_across, 1.0, 0.0).astype(jnp.bfloat16)
    take_ref[...] = jnp.where(q_across == slot_down, 1.0, 0.0).astype(jnp.bfloat16)
    copies[1].wait()
    for k in range(2):
        flip_ref[k] = jnp.broadcast_to(turn_ref[0:1, k : k + 1], (TW, LANES))
    copies[2].wait()


def edge_kernel(tile_ref, outer_ref, inner_ref, flip_ref, put_ref, moved_ref, *out_refs):
    per_tile, width = tile_ref.shape

    odd = odd_strip() == 1

    def turned(value, k):
        back = jnp.concatenate([value[TW - 1 - w : TW - w] for w in range(TW)], axis=0)
        flip = jnp.concatenate([flip_ref[k]] * (width // LANES), axis=1)
        return jnp.where(flip == 1, back, value)

    outer, inner = outer_ref[...], inner_ref[...]
    low = turned(jnp.where(odd, inner, outer), 0)
    high = turned(jnp.where(odd, outer, inner), 1)
    tiles = tile_ref[...]
    below = jnp.concatenate([low, tiles[: per_tile - TW]], axis=0)
    above = jnp.concatenate([tiles[TW:], high], axis=0)
    moved = tiles + kappa_edge * ((above + below) - 2.0 * tiles)
    picked = split_dot(put_ref[...], moved[:, : 2 * L])
    for k, ref in enumerate(out_refs):
        rows = ref.shape[0]
        ref[...] = picked[k * rows : (k + 1) * rows]
    moved_ref[...] = moved


def rows_from_levels(flipped):
    n = 2 * SUB * TZ
    a = lax.broadcasted_iota(jnp.int32, (n, n), 1 if flipped else 0)
    b = lax.broadcasted_iota(jnp.int32, (n, n), 0 if flipped else 1)
    z, p, s = a >> 4, (a >> 3) & 1, a & 7
    return jnp.where(b == p * (SUB * TZ) + s * TZ + z, 1.0, 0.0).astype(jnp.bfloat16)


def prepare_kernel(
    crm_hbm, active_hbm, diff_hbm, vm_hbm, f_ref, mean_ref, sq_ref, coef_ref, wa_ref, wb_ref, crm_ref, act_ref, diff_ref, vm_ref, sems
):
    slots = active_hbm.shape[1]
    copies = [
        pltpu.make_async_copy(active_hbm, act_ref, sems.at[0]),
        pltpu.make_async_copy(diff_hbm, diff_ref, sems.at[1]),
        pltpu.make_async_copy(vm_hbm, vm_ref, sems.at[2]),
        pltpu.make_async_copy(crm_hbm, crm_ref, sems.at[3]),
    ]
    for copy in copies:
        copy.start()
    order = rows_from_levels(False)
    coef_ref[...] = jnp.zeros_like(coef_ref)
    copies[0].wait()
    copies[1].wait()
    active = act_ref[...]
    nothing = jnp.zeros((1, slots), jnp.float32)

    def link(i):
        if i < 0 or i >= CZ - 1:
            return nothing
        return jnp.where(i + 1 < active, diff_ref[i], 0.0)

    up, down = nothing, nothing
    for z in range(CZ):
        lower, upper = link(z - 1), link(z)
        up = 1.0 / (1.0 + lower + upper - lower * (lower * up))
        coef_ref[0, z : z + 1, :] = up
        coef_ref[1, z : z + 1, :] = lower * up
        coef_ref[2, z : z + 1, :] = upper * up
        y = CZ - 1 - z
        lower, upper = link(y - 1), link(y)
        down = 1.0 / (1.0 + lower + upper - upper * (upper * down))
        coef_ref[3, y : y + 1, :] = down
        coef_ref[4, y : y + 1, :] = upper * down
        coef_ref[5, y : y + 1, :] = lower * down
    copies[2].wait()
    pad = jnp.zeros((CZ, L), jnp.float32)
    rest = jnp.zeros((ZP - CZ, 2 * L), jnp.float32)
    both = [jnp.concatenate([vm_ref[...], pad], axis=1), rest, jnp.concatenate([pad, vm_ref[...]], axis=1), rest]
    high, low = parts_of(jnp.concatenate(both, axis=0))
    wa_ref[...] = jnp.concatenate([high, low, high], axis=1)
    wb_ref[...] = jnp.concatenate([high, high, low], axis=0)

    copies[3].wait()
    for t in range(ZP // TZ):
        rows = min(TZ, CZ - t * TZ)
        total = jnp.zeros((TZ, slots), jnp.float32)
        square = jnp.zeros((TZ, slots), jnp.float32)
        for p in range(NI // 2):
            parts = []
            for i in (2 * p, 2 * p + 1):
                for s in range(SUB):
                    x = s * NI + i
                    v = crm_ref[t * TZ : t * TZ + rows, x * slots : (x + 1) * slots]
                    wide = v.astype(jnp.float32)
                    if rows < TZ:
                        wide = jnp.concatenate([wide, jnp.zeros((TZ - rows, slots), jnp.float32)], axis=0)
                        v = wide.astype(jnp.bfloat16)
                    total = total + wide
                    square = square + wide * wide
                    parts.append(v)
            turned = lax.dot_general(
                order, jnp.concatenate(parts, axis=0), (((1,), (0,)), ((), ())), preferred_element_type=jnp.float32
            ).astype(jnp.bfloat16)
            for z in range(rows):
                base = (t * TZ + z) * CX + p * 2 * SUB
                f_ref[base : base + 2 * SUB, :] = turned[z * 2 * SUB : (z + 1) * 2 * SUB]
        mean_ref[t * TZ : (t + 1) * TZ, :] = total * (1.0 / CX)
        sq_ref[t * TZ : (t + 1) * TZ, :] = square * (1.0 / CX)


def physics_kernel(staged, *refs):
    n_in = staged // 2 + 1 if staged else 1
    sent_refs, refs = refs[:n_in], refs[n_in:]
    f_ref, mean_ref, sq_ref, coef_ref, wa_ref, wb_ref, y_ref = refs[:7]
    back_refs = refs[7:-5]
    g_ref, adv_ref, sum_ref, cols_ref, tend_ref = refs[-5:]
    slots = cols_ref.shape[0]
    if staged:
        rows = slots // staged
        for distance, value in arrived(sent_refs, rows, ORDER_OUT):
            cols_ref[tile_rows(distance, rows), :] = value
    else:
        cols_ref[...] = sent_refs[0][...]
    halves = slots // LANES
    for h in range(halves):
        lane = slice(h * LANES, (h + 1) * LANES)
        high, low = parts_of(cols_ref[lane, :])
        mapped = lax.dot_general(
            wa_ref[...],
            jnp.concatenate([high, high, low], axis=1),
            (((1,), (1,)), ((), ())),
            preferred_element_type=jnp.float32,
        )
        forcing = mapped[0:ZP]
        courant = max_courant * jax.nn.sigmoid(mapped[ZP:])
        inv1 = coef_ref[0, :, lane]
        inv2 = coef_ref[3, :, lane]
        adv_ref[0, :, lane] = inv1 * (1.0 - courant)
        adv_ref[1, :, lane] = inv1 * courant
        adv_ref[2, :, lane] = inv2 * (1.0 - courant)
        adv_ref[3, :, lane] = inv2 * courant
        adv_ref[4, :, lane] = inv1 * (relax_rate * (forcing - mean_ref[:, lane]))
    sum_ref[:, CZ:, :] = jnp.zeros((2, ZP - CZ, slots), jnp.float32)

    def spread(ref, k, z, lane):
        return jnp.broadcast_to(ref[k, z : z + 1, lane], (SUB, LANES))

    for h in range(halves):
        lane = slice(h * LANES, (h + 1) * LANES)

        def at(z, i, n=1):
            base = z * CX + i * SUB
            return slice(base, base + n * SUB)

        zero = jnp.zeros((SUB, LANES), jnp.float32)
        prev = [zero] * NI
        for z in range(CZ):
            a, b = spread(adv_ref, 0, z, lane), spread(adv_ref, 1, z, lane)
            d, e = spread(adv_ref, 4, z, lane), spread(coef_ref, 1, z, lane)
            f = []
            for i in range(0, NI, 2):
                pair = f_ref[at(z, i, 2), lane].astype(jnp.float32)
                f += [pair[:SUB], pair[SUB:]]
            behind = [pltpu.roll(f[NI - 1], 1, axis=0)] + f[: NI - 1]
            prev = [((a * f[i] + d) + b * behind[i]) + e * prev[i] for i in range(NI)]
            for i in range(NI):
                g_ref[at(z, i), lane] = prev[i]
        after = [zero] * NI
        prev = [zero] * NI
        for z in range(CZ - 1, -1, -1):
            g = spread(coef_ref, 2, z, lane)
            a, b = spread(adv_ref, 2, z, lane), spread(adv_ref, 3, z, lane)
            e = spread(coef_ref, 4, z, lane)
            after = [g_ref[at(z, i), lane] + g * after[i] for i in range(NI)]
            behind = [pltpu.roll(after[NI - 1], 1, axis=0)] + after[: NI - 1]
            prev = [(a * after[i] + b * behind[i]) + e * prev[i] for i in range(NI)]
            for i in range(NI):
                g_ref[at(z, i), lane] = prev[i]
        after = [zero] * NI
        for z in range(CZ):
            g = spread(coef_ref, 5, z, lane)
            after = [g_ref[at(z, i), lane] + g * after[i] for i in range(NI)]
            total = [after[i] + after[i + 1] for i in range(0, NI, 2)]
            square = [after[i] * after[i] + after[i + 1] * after[i + 1] for i in range(0, NI, 2)]
            for i in range(0, NI, 2):
                y_ref[at(z, i, 2), lane] = jnp.concatenate(after[i : i + 2], axis=0).astype(jnp.bfloat16)
            sum_ref[0, z : z + 1, lane] = jnp.sum((total[0] + total[1]) + (total[2] + total[3]), axis=0, keepdims=True)
            sum_ref[1, z : z + 1, lane] = jnp.sum((square[0] + square[1]) + (square[2] + square[3]), axis=0, keepdims=True)
        mean0, sq0 = mean_ref[:, lane], sq_ref[:, lane]
        mean1, sq1 = sum_ref[0, :, lane] * (1.0 / CX), sum_ref[1, :, lane] * (1.0 / CX)
        change = jnp.concatenate([mean1 - mean0, (sq1 - mean1 * mean1) - (sq0 - mean0 * mean0)], axis=0)
        high, low = parts_of(change)
        tend_ref[lane, :] = lax.dot_general(
            jnp.concatenate([high, low, high], axis=0),
            wb_ref[...],
            (((0,), (0,)), ((), ())),
            preferred_element_type=jnp.float32,
        )
    if staged:
        for distance in range(staged):
            place = distance // 2 * rows
            back_refs[distance % 2][place : place + rows, :] = tend_ref[tile_rows(distance, rows), :]
    else:
        back_refs[0][...] = tend_ref[...]


def store_kernel(y_ref, crm_hbm, crm_ref, sems):
    slots = crm_hbm.shape[1] // CX
    order = rows_from_levels(True)
    copies = []
    for p in range(NI // 2):
        for t in range(ZP // TZ):
            rows = min(TZ, CZ - t * TZ)
            parts = [y_ref[(t * TZ + z) * CX + p * 2 * SUB : (t * TZ + z) * CX + (p + 1) * 2 * SUB, :] for z in range(rows)]
            if rows < TZ:
                parts.append(jnp.zeros(((TZ - rows) * 2 * SUB, slots), jnp.bfloat16))
            turned = lax.dot_general(
                order, jnp.concatenate(parts, axis=0), (((1,), (0,)), ((), ())), preferred_element_type=jnp.float32
            ).astype(jnp.bfloat16)
            for i in range(2):
                for s in range(SUB):
                    x = s * NI + 2 * p + i
                    k = (i * SUB + s) * TZ
                    crm_ref[t * TZ : t * TZ + rows, x * slots : (x + 1) * slots] = turned[k : k + rows]
        for s in range(SUB):
            here = pl.ds((s * NI + 2 * p) * slots, 2 * slots)
            copy = pltpu.make_async_copy(crm_ref.at[:, here], crm_hbm.at[:, here], sems.at[p * SUB + s])
            copy.start()
            copies.append(copy)
    for copy in copies:
        copy.wait()


def finish_kernel(staged, moved_ref, take_ref, *refs):
    back_refs = refs[:-3]
    out_hbm, part_ref, sems = refs[-3:]
    rest = pltpu.make_async_copy(moved_ref.at[:, 2 * L :], out_hbm.at[:, 2 * L :], sems.at[0])
    rest.start()
    if staged:
        parts = arrived(back_refs, take_ref.shape[1] // staged, ORDER_BACK)
        back = jnp.concatenate([part for _, part in parts[0::2] + parts[1::2]], axis=0)
    else:
        back = back_refs[0][...]
    part_ref[...] = moved_ref[:, : 2 * L] + split_dot(take_ref[...], back)
    first = pltpu.make_async_copy(part_ref, out_hbm.at[:, : 2 * L], sems.at[1])
    first.start()
    rest.wait()
    first.wait()


def cost(us):
    return pl.CostEstimate(flops=0, bytes_accessed=int(us * 3.0e6), transcendentals=0)


def far(x):
    return pltpu.with_memory_space_constraint(x, pltpu.HBM)


def shards(state, owners, orient, crm_state, active_levels, vertical_map, diffusion):
    f32, bf16 = jnp.float32, jnp.bfloat16
    n_tiles = lax.axis_size("cols")
    per_tile = state.shape[1]
    width = state.shape[2]
    cap_slots = max(2, 2 * per_tile // n_tiles)
    slots = n_tiles * cap_slots
    rows_f = CZ * CX
    staged = n_tiles if n_tiles == STAGED else 0
    if staged:
        sent = (pltpu.VMEM((slots // 2, 2 * L), f32),) * 2
    else:
        sent = (jax.ShapeDtypeStruct((slots, 2 * L), f32),)
    hbm = pl.BlockSpec(memory_space=pltpu.HBM)
    dma = pltpu.SemaphoreType.DMA
    tile = state[0]
    outer, inner = call(
        rows_kernel,
        (pltpu.VMEM((TW, width), f32), pltpu.VMEM((TW, width), f32)),
        (far(tile),),
        in_specs=[hbm],
        scratch=(dma((2,)),),
        cost=cost(0.5),
    )
    outer = swap(outer, "edge", 1)
    inner = swap(inner, "edge", 0)
    near, put, take, flip = call(
        functools.partial(slots_kernel, cap_slots, staged),
        (
            pltpu.VMEM((per_tile, width), f32),
            pltpu.VMEM((slots, per_tile), bf16),
            pltpu.VMEM((per_tile, slots), bf16),
            pltpu.VMEM((2, TW, LANES), jnp.int32),
        ),
        (far(tile), far(owners.reshape(1, per_tile)), far(orient[0])),
        in_specs=[hbm] * 3,
        scratch=(pltpu.VMEM((1, per_tile), jnp.int32), pltpu.VMEM((1, 2), jnp.int32), dma((3,))),
        cost=cost(1),
    )
    moved, *outgoing = call(
        edge_kernel,
        (pltpu.VMEM((per_tile, width), f32), *sent),
        (near, outer, inner, flip, put),
        cost=cost(1),
    )
    prepared = call(
        prepare_kernel,
        (
            pltpu.VMEM((rows_f, slots), bf16),
            pltpu.VMEM((ZP, slots), f32),
            pltpu.VMEM((ZP, slots), f32),
            pltpu.VMEM((6, ZP, slots), f32),
            pltpu.VMEM((2 * ZP, 6 * L), bf16),
            pltpu.VMEM((6 * ZP, 2 * L), bf16),
        ),
        (far(crm_state[0, 0]), far(active_levels[0]), far(diffusion), far(vertical_map)),
        in_specs=[hbm] * 4,
        scratch=(
            pltpu.VMEM((CZ, CX * slots), bf16),
            pltpu.VMEM((1, slots), jnp.int32),
            pltpu.SMEM((CZ - 1,), f32),
            pltpu.VMEM((CZ, L), f32),
            dma((4,)),
        ),
        cost=cost(4),
    )
    received = exchange(outgoing, ORDER_OUT, prepared[1:2])
    after, *tend = call(
        functools.partial(physics_kernel, staged),
        (pltpu.VMEM((rows_f, slots), bf16), *sent),
        (*received, *prepared),
        scratch=(
            pltpu.VMEM((rows_f, slots), f32),
            pltpu.VMEM((5, ZP, slots), f32),
            pltpu.VMEM((2, ZP, slots), f32),
            pltpu.VMEM((slots, 2 * L), f32),
            pltpu.VMEM((slots, 2 * L), f32),
        ),
        aliases={len(received): 0},
        cost=cost(5),
    )
    returned = exchange(tend, ORDER_BACK)
    crm_new = call(
        store_kernel,
        jax.ShapeDtypeStruct((CZ, CX * slots), bf16),
        (after,),
        scratch=(pltpu.VMEM((CZ, CX * slots), bf16), dma((NI // 2 * SUB,))),
        out_specs=hbm,
        cost=cost(3),
    )
    new_state = call(
        functools.partial(finish_kernel, staged),
        jax.ShapeDtypeStruct((per_tile, width), f32),
        (moved, take, *returned),
        scratch=(pltpu.VMEM((per_tile, 2 * L), f32), dma((2,))),
        out_specs=hbm,
        cost=cost(0.7),
    )
    return (new_state[None], crm_new[None, None])


def solution(mesh):
    in_specs = (
        P("edge", "cols", None),
        P("edge", "cols", None),
        P("edge", "cols", None),
        P("edge", "cols", None, None),
        P("edge", "cols", None),
        P(),
        P(),
    )
    out_specs = (P("edge", "cols", None), P("edge", "cols", None, None))
    return jax.shard_map(shards, mesh=mesh, in_specs=in_specs, out_specs=out_specs, check_vma=False)
```

```python
import functools

import jax
import jax.numpy as jnp
from jax import lax
from jax.experimental import pallas as pl
from jax.experimental.pallas import tpu as pltpu
from jax.sharding import PartitionSpec as P

L = 64
CX = 64
CZ = 58
TW = 8
SUBSTEPS = 2
ZP = 64
LANES = 128
SUB = 8
NI = CX // SUB
STAGED = 8
ORDER_OUT = (3, 2, 1)
ORDER_BACK = (2, 3, 1)
TZ = 16

kappa_edge = 0.25
max_courant = 0.9
relax_rate = 0.5


def call(body, outs, args, scratch=(), in_specs=None, out_specs=None, cost=None, limit=32 << 20, aliases=None):
    kw = {}
    if out_specs is not None:
        kw["out_specs"] = out_specs
    if in_specs is not None:
        kw["in_specs"] = in_specs
    return pl.pallas_call(
        body,
        out_shape=outs,
        scratch_shapes=list(scratch),
        compiler_params=pltpu.CompilerParams(vmem_limit_bytes=limit),
        cost_estimate=cost,
        input_output_aliases=aliases or {},
        **kw,
    )(*args)


def swap(value, axis, first):
    count = lax.axis_size(axis)
    pairs = []
    for one in range(first, count, 2):
        other = (one + 1) % count
        pairs += [(one, other), (other, one)]
    return lax.ppermute(value, axis, pairs)


def pair_kernel(order, ahead, own_ref, got_ref, *refs):
    pair_refs = refs[ahead:]
    rows = pair_refs[0].shape[0] // 2
    for far, ref in zip(order, pair_refs):
        here = slice(far * rows, (far + 1) * rows)
        ref[:rows, :] = own_ref[here, :]
        ref[rows:, :] = got_ref[here, :]


def exchange(sent, order, ahead=()):
    count = lax.axis_size("cols")
    if len(sent) == 1:
        whole = sent[0].reshape(count, -1, sent[0].shape[1])
        return [lax.all_to_all(whole, "cols", split_axis=0, concat_axis=0, tiled=True).reshape(sent[0].shape)]

    def trade(value, k):
        return lax.ppermute(value, "cols", [(c, c ^ k) for c in range(count)])

    own, other = sent
    got = trade(other, 1)
    pairs = call(
        functools.partial(pair_kernel, order, len(ahead)),
        tuple(pltpu.VMEM((2 * own.shape[0] // (count // 2), own.shape[1]), jnp.float32) for _ in order),
        (own, got, *ahead),
        in_specs=[pl.BlockSpec(memory_space=pltpu.VMEM)] * 2 + [pl.BlockSpec(memory_space=pl.ANY)] * len(ahead),
        cost=cost(0.2),
    )
    return [own, got, *[trade(pair, 2 * far) for far, pair in zip(order, pairs)]]


def arrived(refs, rows, order):
    out = [(0, refs[0][:rows, :]), (1, refs[1][:rows, :])]
    for far, ref in sorted(zip(order, refs[2:]), key=lambda pair: pair[0]):
        out += [(2 * far, ref[:rows, :]), (2 * far + 1, ref[rows:, :])]
    return out


def tile_rows(distance, rows):
    return pl.ds(pl.multiple_of((lax.axis_index("cols") ^ distance) * rows, SUB), rows)


def odd_strip():
    return lax.rem(lax.axis_index("edge"), 2)


def split_dot(chosen, value):
    high, low = parts_of(value)
    pick = lambda part: lax.dot_general(chosen, part, (((1,), (0,)), ((), ())), preferred_element_type=jnp.float32)
    return pick(high) + pick(low)


def parts_of(value):
    high = value.astype(jnp.bfloat16)
    return high, (value - high.astype(jnp.float32)).astype(jnp.bfloat16)


def rows_kernel(state_hbm, outer_ref, inner_ref, sems):
    last = state_hbm.shape[0] - TW
    outer = pl.multiple_of(odd_strip() * last, TW)
    inner = pl.multiple_of((1 - odd_strip()) * last, TW)
    copies = [
        pltpu.make_async_copy(state_hbm.at[pl.ds(outer, TW)], outer_ref, sems.at[0]),
        pltpu.make_async_copy(state_hbm.at[pl.ds(inner, TW)], inner_ref, sems.at[1]),
    ]
    for copy in copies:
        copy.start()
    for copy in copies:
        copy.wait()


def slots_kernel(cap, staged, state_hbm, owners_hbm, orient_hbm, tile_ref, put_ref, take_ref, flip_ref, own_ref, turn_ref, sems):
    per_tile = owners_hbm.shape[1]
    n_slots = put_ref.shape[0]
    copies = [
        pltpu.make_async_copy(owners_hbm, own_ref, sems.at[0]),
        pltpu.make_async_copy(orient_hbm, turn_ref, sems.at[1]),
        pltpu.make_async_copy(state_hbm, tile_ref, sems.at[2]),
    ]
    for copy in copies:
        copy.start()
    row = lax.broadcasted_iota(jnp.int32, (per_tile, per_tile), 0)
    col = lax.broadcasted_iota(jnp.int32, (per_tile, per_tile), 1)
    q_down = lax.broadcasted_iota(jnp.int32, (n_slots, per_tile), 0)
    q_across = lax.broadcasted_iota(jnp.int32, (per_tile, n_slots), 1)
    copies[0].wait()
    named = own_ref[...]
    if staged:
        named = named ^ lax.axis_index("cols")
        named = (named & 1) * (staged // 2) + (named >> 1)
    across = jnp.broadcast_to(named, (per_tile, per_tile))
    down = across.T
    same = down == across
    before_col = jnp.where(same & (row < col), 1.0, 0.0)
    before_row = jnp.where(same & (col < row), 1.0, 0.0)
    rank_across = jnp.sum(before_col, axis=0, keepdims=True).astype(jnp.int32)
    rank_down = jnp.sum(before_row, axis=1, keepdims=True).astype(jnp.int32)
    slot_across = across[0:1, :] * cap + rank_across
    slot_down = down[:, 0:1] * cap + rank_down
    put_ref[...] = jnp.where(q_down == slot_across, 1.0, 0.0).astype(jnp.bfloat16)
    take_ref[...] = jnp.where(q_across == slot_down, 1.0, 0.0).astype(jnp.bfloat16)
    copies[1].wait()
    for k in range(2):
        flip_ref[k] = jnp.broadcast_to(turn_ref[0:1, k : k + 1], (TW, LANES))
    copies[2].wait()


def edge_kernel(tile_ref, outer_ref, inner_ref, flip_ref, put_ref, moved_ref, *out_refs):
    per_tile, width = tile_ref.shape

    odd = odd_strip() == 1

    def turned(value, k):
        back = jnp.concatenate([value[TW - 1 - w : TW - w] for w in range(TW)], axis=0)
        flip = jnp.concatenate([flip_ref[k]] * (width // LANES), axis=1)
        return jnp.where(flip == 1, back, value)

    outer, inner = outer_ref[...], inner_ref[...]
    low = turned(jnp.where(odd, inner, outer), 0)
    high = turned(jnp.where(odd, outer, inner), 1)
    tiles = tile_ref[...]
    below = jnp.concatenate([low, tiles[: per_tile - TW]], axis=0)
    above = jnp.concatenate([tiles[TW:], high], axis=0)
    moved = tiles + kappa_edge * ((above + below) - 2.0 * tiles)
    picked = split_dot(put_ref[...], moved[:, : 2 * L])
    for k, ref in enumerate(out_refs):
        rows = ref.shape[0]
        ref[...] = picked[k * rows : (k + 1) * rows]
    moved_ref[...] = moved


def rows_from_levels(flipped):
    n = 2 * SUB * TZ
    a = lax.broadcasted_iota(jnp.int32, (n, n), 1 if flipped else 0)
    b = lax.broadcasted_iota(jnp.int32, (n, n), 0 if flipped else 1)
    z, p, s = a >> 4, (a >> 3) & 1, a & 7
    return jnp.where(b == p * (SUB * TZ) + s * TZ + z, 1.0, 0.0).astype(jnp.bfloat16)


def prepare_kernel(
    crm_hbm, active_hbm, diff_hbm, vm_hbm, f_ref, mean_ref, sq_ref, coef_ref, wa_ref, wb_ref, crm_ref, act_ref, diff_ref, vm_ref, sems
):
    slots = active_hbm.shape[1]
    copies = [
        pltpu.make_async_copy(active_hbm, act_ref, sems.at[0]),
        pltpu.make_async_copy(diff_hbm, diff_ref, sems.at[1]),
        pltpu.make_async_copy(vm_hbm, vm_ref, sems.at[2]),
        pltpu.make_async_copy(crm_hbm, crm_ref, sems.at[3]),
    ]
    for copy in copies:
        copy.start()
    order = rows_from_levels(False)
    coef_ref[...] = jnp.zeros_like(coef_ref)
    copies[0].wait()
    copies[1].wait()
    active = act_ref[...]
    nothing = jnp.zeros((1, slots), jnp.float32)

    def link(i):
        if i < 0 or i >= CZ - 1:
            return nothing
        return jnp.where(i + 1 < active, diff_ref[i], 0.0)

    up, down = nothing, nothing
    for z in range(CZ):
        lower, upper = link(z - 1), link(z)
        up = 1.0 / (1.0 + lower + upper - lower * (lower * up))
        coef_ref[0, z : z + 1, :] = up
        coef_ref[1, z : z + 1, :] = lower * up
        coef_ref[2, z : z + 1, :] = upper * up
        y = CZ - 1 - z
        lower, upper = link(y - 1), link(y)
        down = 1.0 / (1.0 + lower + upper - upper * (upper * down))
        coef_ref[3, y : y + 1, :] = down
        coef_ref[4, y : y + 1, :] = upper * down
        coef_ref[5, y : y + 1, :] = lower * down
    copies[2].wait()
    pad = jnp.zeros((CZ, L), jnp.float32)
    rest = jnp.zeros((ZP - CZ, 2 * L), jnp.float32)
    both = [jnp.concatenate([vm_ref[...], pad], axis=1), rest, jnp.concatenate([pad, vm_ref[...]], axis=1), rest]
    high, low = parts_of(jnp.concatenate(both, axis=0))
    wa_ref[...] = jnp.concatenate([high, low, high], axis=1)
    wb_ref[...] = jnp.concatenate([high, high, low], axis=0)

    copies[3].wait()
    for t in range(ZP // TZ):
        rows = min(TZ, CZ - t * TZ)
        total = jnp.zeros((TZ, slots), jnp.float32)
        square = jnp.zeros((TZ, slots), jnp.float32)
        for p in range(NI // 2):
            parts = []
            for i in (2 * p, 2 * p + 1):
                for s in range(SUB):
                    x = s * NI + i
                    v = crm_ref[t * TZ : t * TZ + rows, x * slots : (x + 1) * slots]
                    wide = v.astype(jnp.float32)
                    if rows < TZ:
                        wide = jnp.concatenate([wide, jnp.zeros((TZ - rows, slots), jnp.float32)], axis=0)
                        v = wide.astype(jnp.bfloat16)
                    total = total + wide
                    square = square + wide * wide
                    parts.append(v)
            turned = lax.dot_general(
                order, jnp.concatenate(parts, axis=0), (((1,), (0,)), ((), ())), preferred_element_type=jnp.float32
            ).astype(jnp.bfloat16)
            for z in range(rows):
                base = (t * TZ + z) * CX + p * 2 * SUB
                f_ref[base : base + 2 * SUB, :] = turned[z * 2 * SUB : (z + 1) * 2 * SUB]
        mean_ref[t * TZ : (t + 1) * TZ, :] = total * (1.0 / CX)
        sq_ref[t * TZ : (t + 1) * TZ, :] = square * (1.0 / CX)


def physics_kernel(staged, *refs):
    n_in = staged // 2 + 1 if staged else 1
    sent_refs, refs = refs[:n_in], refs[n_in:]
    f_ref, mean_ref, sq_ref, coef_ref, wa_ref, wb_ref, y_ref = refs[:7]
    back_refs = refs[7:-5]
    g_ref, adv_ref, sum_ref, cols_ref, tend_ref = refs[-5:]
    slots = cols_ref.shape[0]
    if staged:
        rows = slots // staged
        for distance, value in arrived(sent_refs, rows, ORDER_OUT):
            cols_ref[tile_rows(distance, rows), :] = value
    else:
        cols_ref[...] = sent_refs[0][...]
    halves = slots // LANES
    for h in range(halves):
        lane = slice(h * LANES, (h + 1) * LANES)
        high, low = parts_of(cols_ref[lane, :])
        mapped = lax.dot_general(
            wa_ref[...],
            jnp.concatenate([high, high, low], axis=1),
            (((1,), (1,)), ((), ())),
            preferred_element_type=jnp.float32,
        )
        forcing = mapped[0:ZP]
        courant = max_courant * jax.nn.sigmoid(mapped[ZP:])
        inv1 = coef_ref[0, :, lane]
        inv2 = coef_ref[3, :, lane]
        adv_ref[0, :, lane] = inv1 * (1.0 - courant)
        adv_ref[1, :, lane] = inv1 * courant
        adv_ref[2, :, lane] = inv2 * (1.0 - courant)
        adv_ref[3, :, lane] = inv2 * courant
        adv_ref[4, :, lane] = inv1 * (relax_rate * (forcing - mean_ref[:, lane]))
    sum_ref[:, CZ:, :] = jnp.zeros((2, ZP - CZ, slots), jnp.float32)

    def spread(ref, k, z, lane):
        return jnp.broadcast_to(ref[k, z : z + 1, lane], (SUB, LANES))

    for h in range(halves):
        lane = slice(h * LANES, (h + 1) * LANES)

        def at(z, i, n=1):
            base = z * CX + i * SUB
            return slice(base, base + n * SUB)

        zero = jnp.zeros((SUB, LANES), jnp.float32)
        prev = [zero] * NI
        for z in range(CZ):
            a, b = spread(adv_ref, 0, z, lane), spread(adv_ref, 1, z, lane)
            d, e = spread(adv_ref, 4, z, lane), spread(coef_ref, 1, z, lane)
            f = []
            for i in range(0, NI, 2):
                pair = f_ref[at(z, i, 2), lane].astype(jnp.float32)
                f += [pair[:SUB], pair[SUB:]]
            behind = [pltpu.roll(f[NI - 1], 1, axis=0)] + f[: NI - 1]
            prev = [((a * f[i] + d) + b * behind[i]) + e * prev[i] for i in range(NI)]
            for i in range(NI):
                g_ref[at(z, i), lane] = prev[i]
        after = [zero] * NI
        prev = [zero] * NI
        for z in range(CZ - 1, -1, -1):
            g = spread(coef_ref, 2, z, lane)
            a, b = spread(adv_ref, 2, z, lane), spread(adv_ref, 3, z, lane)
            e = spread(coef_ref, 4, z, lane)
            after = [g_ref[at(z, i), lane] + g * after[i] for i in range(NI)]
            behind = [pltpu.roll(after[NI - 1], 1, axis=0)] + after[: NI - 1]
            prev = [(a * after[i] + b * behind[i]) + e * prev[i] for i in range(NI)]
            for i in range(NI):
                g_ref[at(z, i), lane] = prev[i]
        after = [zero] * NI
        for z in range(CZ):
            g = spread(coef_ref, 5, z, lane)
            after = [g_ref[at(z, i), lane] + g * after[i] for i in range(NI)]
            total = [after[i] + after[i + 1] for i in range(0, NI, 2)]
            square = [after[i] * after[i] + after[i + 1] * after[i + 1] for i in range(0, NI, 2)]
            for i in range(0, NI, 2):
                y_ref[at(z, i, 2), lane] = jnp.concatenate(after[i : i + 2], axis=0).astype(jnp.bfloat16)
            sum_ref[0, z : z + 1, lane] = jnp.sum((total[0] + total[1]) + (total[2] + total[3]), axis=0, keepdims=True)
            sum_ref[1, z : z + 1, lane] = jnp.sum((square[0] + square[1]) + (square[2] + square[3]), axis=0, keepdims=True)
        mean0, sq0 = mean_ref[:, lane], sq_ref[:, lane]
        mean1, sq1 = sum_ref[0, :, lane] * (1.0 / CX), sum_ref[1, :, lane] * (1.0 / CX)
        change = jnp.concatenate([mean1 - mean0, (sq1 - mean1 * mean1) - (sq0 - mean0 * mean0)], axis=0)
        high, low = parts_of(change)
        tend_ref[lane, :] = lax.dot_general(
            jnp.concatenate([high, low, high], axis=0),
            wb_ref[...],
            (((0,), (0,)), ((), ())),
            preferred_element_type=jnp.float32,
        )
    if staged:
        for distance in range(staged):
            place = distance // 2 * rows
            back_refs[distance % 2][place : place + rows, :] = tend_ref[tile_rows(distance, rows), :]
    else:
        back_refs[0][...] = tend_ref[...]


def store_kernel(y_ref, crm_hbm, crm_ref, sems):
    slots = crm_hbm.shape[1] // CX
    order = rows_from_levels(True)
    copies = []
    for p in range(NI // 2):
        for t in range(ZP // TZ):
            rows = min(TZ, CZ - t * TZ)
            parts = [y_ref[(t * TZ + z) * CX + p * 2 * SUB : (t * TZ + z) * CX + (p + 1) * 2 * SUB, :] for z in range(rows)]
            if rows < TZ:
                parts.append(jnp.zeros(((TZ - rows) * 2 * SUB, slots), jnp.bfloat16))
            turned = lax.dot_general(
                order, jnp.concatenate(parts, axis=0), (((1,), (0,)), ((), ())), preferred_element_type=jnp.float32
            ).astype(jnp.bfloat16)
            for i in range(2):
                for s in range(SUB):
                    x = s * NI + 2 * p + i
                    k = (i * SUB + s) * TZ
                    crm_ref[t * TZ : t * TZ + rows, x * slots : (x + 1) * slots] = turned[k : k + rows]
        for s in range(SUB):
            here = pl.ds((s * NI + 2 * p) * slots, 2 * slots)
            copy = pltpu.make_async_copy(crm_ref.at[:, here], crm_hbm.at[:, here], sems.at[p * SUB + s])
            copy.start()
            copies.append(copy)
    for copy in copies:
        copy.wait()


def finish_kernel(staged, moved_ref, take_ref, *refs):
    back_refs = refs[:-3]
    out_hbm, part_ref, sems = refs[-3:]
    rest = pltpu.make_async_copy(moved_ref.at[:, 2 * L :], out_hbm.at[:, 2 * L :], sems.at[0])
    rest.start()
    if staged:
        parts = arrived(back_refs, take_ref.shape[1] // staged, ORDER_BACK)
        back = jnp.concatenate([part for _, part in parts[0::2] + parts[1::2]], axis=0)
    else:
        back = back_refs[0][...]
    part_ref[...] = moved_ref[:, : 2 * L] + split_dot(take_ref[...], back)
    first = pltpu.make_async_copy(part_ref, out_hbm.at[:, : 2 * L], sems.at[1])
    first.start()
    rest.wait()
    first.wait()


def cost(us):
    return pl.CostEstimate(flops=0, bytes_accessed=int(us * 3.0e6), transcendentals=0)


def far(x):
    return pltpu.with_memory_space_constraint(x, pltpu.HBM)


def shards(state, owners, orient, crm_state, active_levels, vertical_map, diffusion):
    f32, bf16 = jnp.float32, jnp.bfloat16
    n_tiles = lax.axis_size("cols")
    per_tile = state.shape[1]
    width = state.shape[2]
    cap_slots = max(2, 2 * per_tile // n_tiles)
    slots = n_tiles * cap_slots
    rows_f = CZ * CX
    staged = n_tiles if n_tiles == STAGED else 0
    if staged:
        sent = (pltpu.VMEM((slots // 2, 2 * L), f32),) * 2
    else:
        sent = (jax.ShapeDtypeStruct((slots, 2 * L), f32),)
    hbm = pl.BlockSpec(memory_space=pltpu.HBM)
    dma = pltpu.SemaphoreType.DMA
    tile = state[0]
    outer, inner = call(
        rows_kernel,
        (pltpu.VMEM((TW, width), f32), pltpu.VMEM((TW, width), f32)),
        (far(tile),),
        in_specs=[hbm],
        scratch=(dma((2,)),),
        cost=cost(0.5),
    )
    outer = swap(outer, "edge", 1)
    inner = swap(inner, "edge", 0)
    near, put, take, flip = call(
        functools.partial(slots_kernel, cap_slots, staged),
        (
            pltpu.VMEM((per_tile, width), f32),
            pltpu.VMEM((slots, per_tile), bf16),
            pltpu.VMEM((per_tile, slots), bf16),
            pltpu.VMEM((2, TW, LANES), jnp.int32),
        ),
        (far(tile), far(owners.reshape(1, per_tile)), far(orient[0])),
        in_specs=[hbm] * 3,
        scratch=(pltpu.VMEM((1, per_tile), jnp.int32), pltpu.VMEM((1, 2), jnp.int32), dma((3,))),
        cost=cost(1),
    )
    moved, *outgoing = call(
        edge_kernel,
        (pltpu.VMEM((per_tile, width), f32), *sent),
        (near, outer, inner, flip, put),
        cost=cost(1),
    )
    prepared = call(
        prepare_kernel,
        (
            pltpu.VMEM((rows_f, slots), bf16),
            pltpu.VMEM((ZP, slots), f32),
            pltpu.VMEM((ZP, slots), f32),
            pltpu.VMEM((6, ZP, slots), f32),
            pltpu.VMEM((2 * ZP, 6 * L), bf16),
            pltpu.VMEM((6 * ZP, 2 * L), bf16),
        ),
        (far(crm_state[0, 0]), far(active_levels[0]), far(diffusion), far(vertical_map)),
        in_specs=[hbm] * 4,
        scratch=(
            pltpu.VMEM((CZ, CX * slots), bf16),
            pltpu.VMEM((1, slots), jnp.int32),
            pltpu.SMEM((CZ - 1,), f32),
            pltpu.VMEM((CZ, L), f32),
            dma((4,)),
        ),
        cost=cost(4),
    )
    received = exchange(outgoing, ORDER_OUT, prepared[1:2])
    after, *tend = call(
        functools.partial(physics_kernel, staged),
        (pltpu.VMEM((rows_f, slots), bf16), *sent),
        (*received, *prepared),
        scratch=(
            pltpu.VMEM((rows_f, slots), f32),
            pltpu.VMEM((5, ZP, slots), f32),
            pltpu.VMEM((2, ZP, slots), f32),
            pltpu.VMEM((slots, 2 * L), f32),
            pltpu.VMEM((slots, 2 * L), f32),
        ),
        aliases={len(received): 0},
        cost=cost(5),
    )
    returned = exchange(tend, ORDER_BACK)
    crm_new = call(
        store_kernel,
        jax.ShapeDtypeStruct((CZ, CX * slots), bf16),
        (after,),
        scratch=(pltpu.VMEM((CZ, CX * slots), bf16), dma((NI // 2 * SUB,))),
        out_specs=hbm,
        cost=cost(3),
    )
    new_state = call(
        functools.partial(finish_kernel, staged),
        jax.ShapeDtypeStruct((per_tile, width), f32),
        (moved, take, *returned),
        scratch=(pltpu.VMEM((per_tile, 2 * L), f32), dma((2,))),
        out_specs=hbm,
        cost=cost(0.7),
    )
    return (new_state[None], crm_new[None, None])


def solution(mesh):
    in_specs = (
        P("edge", "cols", None),
        P("edge", "cols", None),
        P("edge", "cols", None),
        P("edge", "cols", None, None),
        P("edge", "cols", None),
        P(),
        P(),
    )
    out_specs = (P("edge", "cols", None), P("edge", "cols", None, None))
    return jax.shard_map(shards, mesh=mesh, in_specs=in_specs, out_specs=out_specs, check_vma=False)
```

```python
import functools

import jax
import jax.numpy as jnp
from jax import lax
from jax.experimental import pallas as pl
from jax.experimental.pallas import tpu as pltpu
from jax.sharding import PartitionSpec as P

L = 64
CX = 64
CZ = 58
TW = 8
SUBSTEPS = 2
ZP = 64
LANES = 128
SUB = 8
NI = CX // SUB
STAGED = 8
TZ = 16

kappa_edge = 0.25
max_courant = 0.9
relax_rate = 0.5


def call(body, outs, args, scratch=(), in_specs=None, out_specs=None, cost=None, limit=32 << 20, aliases=None):
    kw = {}
    if out_specs is not None:
        kw["out_specs"] = out_specs
    if in_specs is not None:
        kw["in_specs"] = in_specs
    return pl.pallas_call(
        body,
        out_shape=outs,
        scratch_shapes=list(scratch),
        compiler_params=pltpu.CompilerParams(vmem_limit_bytes=limit),
        cost_estimate=cost,
        input_output_aliases=aliases or {},
        **kw,
    )(*args)


def swap(value, axis, first):
    count = lax.axis_size(axis)
    pairs = []
    for one in range(first, count, 2):
        other = (one + 1) % count
        pairs += [(one, other), (other, one)]
    return lax.ppermute(value, axis, pairs)


def pair_kernel(ahead, own_ref, got_ref, *refs):
    pair_refs = refs[ahead:]
    rows = pair_refs[0].shape[0] // 2
    for k, ref in enumerate(pair_refs):
        far = len(pair_refs) - k
        here = slice(far * rows, (far + 1) * rows)
        ref[:rows, :] = own_ref[here, :]
        ref[rows:, :] = got_ref[here, :]


def exchange(sent, ahead=()):
    count = lax.axis_size("cols")
    if len(sent) == 1:
        whole = sent[0].reshape(count, -1, sent[0].shape[1])
        return [lax.all_to_all(whole, "cols", split_axis=0, concat_axis=0, tiled=True).reshape(sent[0].shape)]

    def trade(value, k):
        return lax.ppermute(value, "cols", [(c, c ^ k) for c in range(count)])

    own, other = sent
    got = trade(other, 1)
    far_ones = count // 2 - 1
    pairs = call(
        functools.partial(pair_kernel, len(ahead)),
        tuple(pltpu.VMEM((2 * own.shape[0] // (count // 2), own.shape[1]), jnp.float32) for _ in range(far_ones)),
        (own, got, *ahead),
        in_specs=[pl.BlockSpec(memory_space=pltpu.VMEM)] * 2 + [pl.BlockSpec(memory_space=pl.ANY)] * len(ahead),
        cost=cost(0.2),
    )
    return [own, got, *[trade(pair, 2 * (far_ones - k)) for k, pair in enumerate(pairs)]]


def arrived(refs, rows):
    out = [(0, refs[0][:rows, :]), (1, refs[1][:rows, :])]
    for k, ref in enumerate(refs[:1:-1]):
        out += [(2 * (k + 1), ref[:rows, :]), (2 * (k + 1) + 1, ref[rows:, :])]
    return out


def tile_rows(distance, rows):
    return pl.ds(pl.multiple_of((lax.axis_index("cols") ^ distance) * rows, SUB), rows)


def odd_strip():
    return lax.rem(lax.axis_index("edge"), 2)


def split_dot(chosen, value):
    high, low = parts_of(value)
    pick = lambda part: lax.dot_general(chosen, part, (((1,), (0,)), ((), ())), preferred_element_type=jnp.float32)
    return pick(high) + pick(low)


def parts_of(value):
    high = value.astype(jnp.bfloat16)
    return high, (value - high.astype(jnp.float32)).astype(jnp.bfloat16)


def rows_kernel(state_hbm, outer_ref, inner_ref, sems):
    last = state_hbm.shape[0] - TW
    outer = pl.multiple_of(odd_strip() * last, TW)
    inner = pl.multiple_of((1 - odd_strip()) * last, TW)
    copies = [
        pltpu.make_async_copy(state_hbm.at[pl.ds(outer, TW)], outer_ref, sems.at[0]),
        pltpu.make_async_copy(state_hbm.at[pl.ds(inner, TW)], inner_ref, sems.at[1]),
    ]
    for copy in copies:
        copy.start()
    for copy in copies:
        copy.wait()


def slots_kernel(cap, staged, state_hbm, owners_hbm, orient_hbm, tile_ref, put_ref, take_ref, flip_ref, own_ref, turn_ref, sems):
    per_tile = owners_hbm.shape[1]
    n_slots = put_ref.shape[0]
    copies = [
        pltpu.make_async_copy(owners_hbm, own_ref, sems.at[0]),
        pltpu.make_async_copy(orient_hbm, turn_ref, sems.at[1]),
        pltpu.make_async_copy(state_hbm, tile_ref, sems.at[2]),
    ]
    for copy in copies:
        copy.start()
    row = lax.broadcasted_iota(jnp.int32, (per_tile, per_tile), 0)
    col = lax.broadcasted_iota(jnp.int32, (per_tile, per_tile), 1)
    q_down = lax.broadcasted_iota(jnp.int32, (n_slots, per_tile), 0)
    q_across = lax.broadcasted_iota(jnp.int32, (per_tile, n_slots), 1)
    copies[0].wait()
    named = own_ref[...]
    if staged:
        named = named ^ lax.axis_index("cols")
        named = (named & 1) * (staged // 2) + (named >> 1)
    across = jnp.broadcast_to(named, (per_tile, per_tile))
    down = across.T
    same = down == across
    before_col = jnp.where(same & (row < col), 1.0, 0.0)
    before_row = jnp.where(same & (col < row), 1.0, 0.0)
    rank_across = jnp.sum(before_col, axis=0, keepdims=True).astype(jnp.int32)
    rank_down = jnp.sum(before_row, axis=1, keepdims=True).astype(jnp.int32)
    slot_across = across[0:1, :] * cap + rank_across
    slot_down = down[:, 0:1] * cap + rank_down
    put_ref[...] = jnp.where(q_down == slot_across, 1.0, 0.0).astype(jnp.bfloat16)
    take_ref[...] = jnp.where(q_across == slot_down, 1.0, 0.0).astype(jnp.bfloat16)
    copies[1].wait()
    for k in range(2):
        flip_ref[k] = jnp.broadcast_to(turn_ref[0:1, k : k + 1], (TW, LANES))
    copies[2].wait()


def edge_kernel(tile_ref, outer_ref, inner_ref, flip_ref, put_ref, moved_ref, *out_refs):
    per_tile, width = tile_ref.shape

    odd = odd_strip() == 1

    def turned(value, k):
        back = jnp.concatenate([value[TW - 1 - w : TW - w] for w in range(TW)], axis=0)
        flip = jnp.concatenate([flip_ref[k]] * (width // LANES), axis=1)
        return jnp.where(flip == 1, back, value)

    outer, inner = outer_ref[...], inner_ref[...]
    low = turned(jnp.where(odd, inner, outer), 0)
    high = turned(jnp.where(odd, outer, inner), 1)
    tiles = tile_ref[...]
    below = jnp.concatenate([low, tiles[: per_tile - TW]], axis=0)
    above = jnp.concatenate([tiles[TW:], high], axis=0)
    moved = tiles + kappa_edge * ((above + below) - 2.0 * tiles)
    picked = split_dot(put_ref[...], moved[:, : 2 * L])
    for k, ref in enumerate(out_refs):
        rows = ref.shape[0]
        ref[...] = picked[k * rows : (k + 1) * rows]
    moved_ref[...] = moved


def rows_from_levels(flipped):
    n = 2 * SUB * TZ
    a = lax.broadcasted_iota(jnp.int32, (n, n), 1 if flipped else 0)
    b = lax.broadcasted_iota(jnp.int32, (n, n), 0 if flipped else 1)
    z, p, s = a >> 4, (a >> 3) & 1, a & 7
    return jnp.where(b == p * (SUB * TZ) + s * TZ + z, 1.0, 0.0).astype(jnp.bfloat16)


def prepare_kernel(
    crm_hbm, active_hbm, diff_hbm, vm_hbm, f_ref, mean_ref, sq_ref, coef_ref, wa_ref, wb_ref, crm_ref, act_ref, diff_ref, vm_ref, sems
):
    slots = active_hbm.shape[1]
    copies = [
        pltpu.make_async_copy(active_hbm, act_ref, sems.at[0]),
        pltpu.make_async_copy(diff_hbm, diff_ref, sems.at[1]),
        pltpu.make_async_copy(vm_hbm, vm_ref, sems.at[2]),
        pltpu.make_async_copy(crm_hbm, crm_ref, sems.at[3]),
    ]
    for copy in copies:
        copy.start()
    order = rows_from_levels(False)
    coef_ref[...] = jnp.zeros_like(coef_ref)
    copies[0].wait()
    copies[1].wait()
    active = act_ref[...]
    nothing = jnp.zeros((1, slots), jnp.float32)

    def link(i):
        if i < 0 or i >= CZ - 1:
            return nothing
        return jnp.where(i + 1 < active, diff_ref[i], 0.0)

    up, down = nothing, nothing
    for z in range(CZ):
        lower, upper = link(z - 1), link(z)
        up = 1.0 / (1.0 + lower + upper - lower * (lower * up))
        coef_ref[0, z : z + 1, :] = up
        coef_ref[1, z : z + 1, :] = lower * up
        coef_ref[2, z : z + 1, :] = upper * up
        y = CZ - 1 - z
        lower, upper = link(y - 1), link(y)
        down = 1.0 / (1.0 + lower + upper - upper * (upper * down))
        coef_ref[3, y : y + 1, :] = down
        coef_ref[4, y : y + 1, :] = upper * down
        coef_ref[5, y : y + 1, :] = lower * down
    copies[2].wait()
    pad = jnp.zeros((CZ, L), jnp.float32)
    rest = jnp.zeros((ZP - CZ, 2 * L), jnp.float32)
    both = [jnp.concatenate([vm_ref[...], pad], axis=1), rest, jnp.concatenate([pad, vm_ref[...]], axis=1), rest]
    high, low = parts_of(jnp.concatenate(both, axis=0))
    wa_ref[...] = jnp.concatenate([high, low, high], axis=1)
    wb_ref[...] = jnp.concatenate([high, high, low], axis=0)

    copies[3].wait()
    for t in range(ZP // TZ):
        rows = min(TZ, CZ - t * TZ)
        total = jnp.zeros((TZ, slots), jnp.float32)
        square = jnp.zeros((TZ, slots), jnp.float32)
        for p in range(NI // 2):
            parts = []
            for i in (2 * p, 2 * p + 1):
                for s in range(SUB):
                    x = s * NI + i
                    v = crm_ref[t * TZ : t * TZ + rows, x * slots : (x + 1) * slots]
                    wide = v.astype(jnp.float32)
                    if rows < TZ:
                        wide = jnp.concatenate([wide, jnp.zeros((TZ - rows, slots), jnp.float32)], axis=0)
                        v = wide.astype(jnp.bfloat16)
                    total = total + wide
                    square = square + wide * wide
                    parts.append(v)
            turned = lax.dot_general(
                order, jnp.concatenate(parts, axis=0), (((1,), (0,)), ((), ())), preferred_element_type=jnp.float32
            ).astype(jnp.bfloat16)
            for z in range(rows):
                base = (t * TZ + z) * CX + p * 2 * SUB
                f_ref[base : base + 2 * SUB, :] = turned[z * 2 * SUB : (z + 1) * 2 * SUB]
        mean_ref[t * TZ : (t + 1) * TZ, :] = total * (1.0 / CX)
        sq_ref[t * TZ : (t + 1) * TZ, :] = square * (1.0 / CX)


def physics_kernel(staged, *refs):
    n_in = staged // 2 + 1 if staged else 1
    sent_refs, refs = refs[:n_in], refs[n_in:]
    f_ref, mean_ref, sq_ref, coef_ref, wa_ref, wb_ref, y_ref = refs[:7]
    back_refs = refs[7:-5]
    g_ref, adv_ref, sum_ref, cols_ref, tend_ref = refs[-5:]
    slots = cols_ref.shape[0]
    if staged:
        rows = slots // staged
        for distance, value in arrived(sent_refs, rows):
            cols_ref[tile_rows(distance, rows), :] = value
    else:
        cols_ref[...] = sent_refs[0][...]
    halves = slots // LANES
    for h in range(halves):
        lane = slice(h * LANES, (h + 1) * LANES)
        high, low = parts_of(cols_ref[lane, :])
        mapped = lax.dot_general(
            wa_ref[...],
            jnp.concatenate([high, high, low], axis=1),
            (((1,), (1,)), ((), ())),
            preferred_element_type=jnp.float32,
        )
        forcing = mapped[0:ZP]
        courant = max_courant * jax.nn.sigmoid(mapped[ZP:])
        inv1 = coef_ref[0, :, lane]
        inv2 = coef_ref[3, :, lane]
        adv_ref[0, :, lane] = inv1 * (1.0 - courant)
        adv_ref[1, :, lane] = inv1 * courant
        adv_ref[2, :, lane] = inv2 * (1.0 - courant)
        adv_ref[3, :, lane] = inv2 * courant
        adv_ref[4, :, lane] = inv1 * (relax_rate * (forcing - mean_ref[:, lane]))
    sum_ref[:, CZ:, :] = jnp.zeros((2, ZP - CZ, slots), jnp.float32)

    def spread(ref, k, z, lane):
        return jnp.broadcast_to(ref[k, z : z + 1, lane], (SUB, LANES))

    for h in range(halves):
        lane = slice(h * LANES, (h + 1) * LANES)

        def at(z, i, n=1):
            base = z * CX + i * SUB
            return slice(base, base + n * SUB)

        zero = jnp.zeros((SUB, LANES), jnp.float32)
        prev = [zero] * NI
        for z in range(CZ):
            a, b = spread(adv_ref, 0, z, lane), spread(adv_ref, 1, z, lane)
            d, e = spread(adv_ref, 4, z, lane), spread(coef_ref, 1, z, lane)
            f = []
            for i in range(0, NI, 2):
                pair = f_ref[at(z, i, 2), lane].astype(jnp.float32)
                f += [pair[:SUB], pair[SUB:]]
            behind = [pltpu.roll(f[NI - 1], 1, axis=0)] + f[: NI - 1]
            prev = [((a * f[i] + d) + b * behind[i]) + e * prev[i] for i in range(NI)]
            for i in range(NI):
                g_ref[at(z, i), lane] = prev[i]
        after = [zero] * NI
        prev = [zero] * NI
        for z in range(CZ - 1, -1, -1):
            g = spread(coef_ref, 2, z, lane)
            a, b = spread(adv_ref, 2, z, lane), spread(adv_ref, 3, z, lane)
            e = spread(coef_ref, 4, z, lane)
            after = [g_ref[at(z, i), lane] + g * after[i] for i in range(NI)]
            behind = [pltpu.roll(after[NI - 1], 1, axis=0)] + after[: NI - 1]
            prev = [(a * after[i] + b * behind[i]) + e * prev[i] for i in range(NI)]
            for i in range(NI):
                g_ref[at(z, i), lane] = prev[i]
        after = [zero] * NI
        for z in range(CZ):
            g = spread(coef_ref, 5, z, lane)
            after = [g_ref[at(z, i), lane] + g * after[i] for i in range(NI)]
            total = [after[i] + after[i + 1] for i in range(0, NI, 2)]
            square = [after[i] * after[i] + after[i + 1] * after[i + 1] for i in range(0, NI, 2)]
            for i in range(0, NI, 2):
                y_ref[at(z, i, 2), lane] = jnp.concatenate(after[i : i + 2], axis=0).astype(jnp.bfloat16)
            sum_ref[0, z : z + 1, lane] = jnp.sum((total[0] + total[1]) + (total[2] + total[3]), axis=0, keepdims=True)
            sum_ref[1, z : z + 1, lane] = jnp.sum((square[0] + square[1]) + (square[2] + square[3]), axis=0, keepdims=True)
        mean0, sq0 = mean_ref[:, lane], sq_ref[:, lane]
        mean1, sq1 = sum_ref[0, :, lane] * (1.0 / CX), sum_ref[1, :, lane] * (1.0 / CX)
        change = jnp.concatenate([mean1 - mean0, (sq1 - mean1 * mean1) - (sq0 - mean0 * mean0)], axis=0)
        high, low = parts_of(change)
        tend_ref[lane, :] = lax.dot_general(
            jnp.concatenate([high, low, high], axis=0),
            wb_ref[...],
            (((0,), (0,)), ((), ())),
            preferred_element_type=jnp.float32,
        )
    if staged:
        for distance in range(staged):
            place = distance // 2 * rows
            back_refs[distance % 2][place : place + rows, :] = tend_ref[tile_rows(distance, rows), :]
    else:
        back_refs[0][...] = tend_ref[...]


def store_kernel(y_ref, crm_hbm, crm_ref, sems):
    slots = crm_hbm.shape[1] // CX
    order = rows_from_levels(True)
    copies = []
    for p in range(NI // 2):
        for t in range(ZP // TZ):
            rows = min(TZ, CZ - t * TZ)
            parts = [y_ref[(t * TZ + z) * CX + p * 2 * SUB : (t * TZ + z) * CX + (p + 1) * 2 * SUB, :] for z in range(rows)]
            if rows < TZ:
                parts.append(jnp.zeros(((TZ - rows) * 2 * SUB, slots), jnp.bfloat16))
            turned = lax.dot_general(
                order, jnp.concatenate(parts, axis=0), (((1,), (0,)), ((), ())), preferred_element_type=jnp.float32
            ).astype(jnp.bfloat16)
            for i in range(2):
                for s in range(SUB):
                    x = s * NI + 2 * p + i
                    k = (i * SUB + s) * TZ
                    crm_ref[t * TZ : t * TZ + rows, x * slots : (x + 1) * slots] = turned[k : k + rows]
        for s in range(SUB):
            here = pl.ds((s * NI + 2 * p) * slots, 2 * slots)
            copy = pltpu.make_async_copy(crm_ref.at[:, here], crm_hbm.at[:, here], sems.at[p * SUB + s])
            copy.start()
            copies.append(copy)
    for copy in copies:
        copy.wait()


def finish_kernel(staged, moved_ref, take_ref, *refs):
    back_refs = refs[:-3]
    out_hbm, part_ref, sems = refs[-3:]
    rest = pltpu.make_async_copy(moved_ref.at[:, 2 * L :], out_hbm.at[:, 2 * L :], sems.at[0])
    rest.start()
    if staged:
        parts = arrived(back_refs, take_ref.shape[1] // staged)
        back = jnp.concatenate([part for _, part in parts[0::2] + parts[1::2]], axis=0)
    else:
        back = back_refs[0][...]
    part_ref[...] = moved_ref[:, : 2 * L] + split_dot(take_ref[...], back)
    first = pltpu.make_async_copy(part_ref, out_hbm.at[:, : 2 * L], sems.at[1])
    first.start()
    rest.wait()
    first.wait()


def cost(us):
    return pl.CostEstimate(flops=0, bytes_accessed=int(us * 3.0e6), transcendentals=0)


def far(x):
    return pltpu.with_memory_space_constraint(x, pltpu.HBM)


def shards(state, owners, orient, crm_state, active_levels, vertical_map, diffusion):
    f32, bf16 = jnp.float32, jnp.bfloat16
    n_tiles = lax.axis_size("cols")
    per_tile = state.shape[1]
    width = state.shape[2]
    cap_slots = max(2, 2 * per_tile // n_tiles)
    slots = n_tiles * cap_slots
    rows_f = CZ * CX
    staged = n_tiles if n_tiles == STAGED else 0
    if staged:
        sent = (pltpu.VMEM((slots // 2, 2 * L), f32),) * 2
    else:
        sent = (jax.ShapeDtypeStruct((slots, 2 * L), f32),)
    hbm = pl.BlockSpec(memory_space=pltpu.HBM)
    dma = pltpu.SemaphoreType.DMA
    tile = state[0]
    outer, inner = call(
        rows_kernel,
        (pltpu.VMEM((TW, width), f32), pltpu.VMEM((TW, width), f32)),
        (far(tile),),
        in_specs=[hbm],
        scratch=(dma((2,)),),
        cost=cost(0.5),
    )
    outer = swap(outer, "edge", 1)
    inner = swap(inner, "edge", 0)
    near, put, take, flip = call(
        functools.partial(slots_kernel, cap_slots, staged),
        (
            pltpu.VMEM((per_tile, width), f32),
            pltpu.VMEM((slots, per_tile), bf16),
            pltpu.VMEM((per_tile, slots), bf16),
            pltpu.VMEM((2, TW, LANES), jnp.int32),
        ),
        (far(tile), far(owners.reshape(1, per_tile)), far(orient[0])),
        in_specs=[hbm] * 3,
        scratch=(pltpu.VMEM((1, per_tile), jnp.int32), pltpu.VMEM((1, 2), jnp.int32), dma((3,))),
        cost=cost(1),
    )
    moved, *outgoing = call(
        edge_kernel,
        (pltpu.VMEM((per_tile, width), f32), *sent),
        (near, outer, inner, flip, put),
        cost=cost(1),
    )
    prepared = call(
        prepare_kernel,
        (
            pltpu.VMEM((rows_f, slots), bf16),
            pltpu.VMEM((ZP, slots), f32),
            pltpu.VMEM((ZP, slots), f32),
            pltpu.VMEM((6, ZP, slots), f32),
            pltpu.VMEM((2 * ZP, 6 * L), bf16),
            pltpu.VMEM((6 * ZP, 2 * L), bf16),
        ),
        (far(crm_state[0, 0]), far(active_levels[0]), far(diffusion), far(vertical_map)),
        in_specs=[hbm] * 4,
        scratch=(
            pltpu.VMEM((CZ, CX * slots), bf16),
            pltpu.VMEM((1, slots), jnp.int32),
            pltpu.SMEM((CZ - 1,), f32),
            pltpu.VMEM((CZ, L), f32),
            dma((4,)),
        ),
        cost=cost(4),
    )
    received = exchange(outgoing, prepared[1:2])
    after, *tend = call(
        functools.partial(physics_kernel, staged),
        (pltpu.VMEM((rows_f, slots), bf16), *sent),
        (*received, *prepared),
        scratch=(
            pltpu.VMEM((rows_f, slots), f32),
            pltpu.VMEM((5, ZP, slots), f32),
            pltpu.VMEM((2, ZP, slots), f32),
            pltpu.VMEM((slots, 2 * L), f32),
            pltpu.VMEM((slots, 2 * L), f32),
        ),
        aliases={len(received): 0},
        cost=cost(5),
    )
    crm_new = call(
        store_kernel,
        jax.ShapeDtypeStruct((CZ, CX * slots), bf16),
        (after,),
        scratch=(pltpu.VMEM((CZ, CX * slots), bf16), dma((NI // 2 * SUB,))),
        out_specs=hbm,
        cost=cost(3),
    )
    returned = exchange(tend, (crm_new,))
    new_state = call(
        functools.partial(finish_kernel, staged),
        jax.ShapeDtypeStruct((per_tile, width), f32),
        (moved, take, *returned),
        scratch=(pltpu.VMEM((per_tile, 2 * L), f32), dma((2,))),
        out_specs=hbm,
        cost=cost(0.7),
    )
    return (new_state[None], crm_new[None, None])


def solution(mesh):
    in_specs = (
        P("edge", "cols", None),
        P("edge", "cols", None),
        P("edge", "cols", None),
        P("edge", "cols", None, None),
        P("edge", "cols", None),
        P(),
        P(),
    )
    out_specs = (P("edge", "cols", None), P("edge", "cols", None, None))
    return jax.shard_map(shards, mesh=mesh, in_specs=in_specs, out_specs=out_specs, check_vma=False)
```
